32 devices in a mesh: batch: 8 (over z, y), blk: 4 (over x, core).
Axes of the slice: x: 2, y: 2, z: 4, core: 2. Of those that a mesh axis runs over, the one named last changes fastest.
Arguments:
- tokens: bfloat16 [8192, 768], P(('batch', 'blk')), may hold values from -6 to 6
- memory: bfloat16 [8, 512, 768], P('batch', 'blk'), may hold values from -6 to 6
- mem_pos: int32 [8, 512], P('batch', 'blk'), may hold values from 0 to 4095
- seg_count: int32 [8], P('batch'), may hold values from 1 to 4, as said below
- w_qkv: bfloat16 [2, 768, 2304], replicated, may hold values from -0.21875 to 0.21875
- w_out: bfloat16 [2, 768, 768], replicated, may hold values from -0.875 to 0.875
- w_up: bfloat16 [2, 768, 3072], replicated, may hold values from -0.21875 to 0.21875
- w_down: bfloat16 [2, 3072, 768], replicated, may hold values from -0.109375 to 0.109375
- gain_attn: float32 [2, 768], replicated, may hold values from 0.5 to 1.5
- gain_mlp: float32 [2, 768], replicated, may hold values from 0.5 to 1.5
- w_mu: float32 [2, 256], replicated, may hold values from -0.1875 to 0.1875
- w_sig: float32 [2, 256], replicated, may hold values from -0.1875 to 0.1875
- cotangent: bfloat16 [8192, 768], P(('batch', 'blk')), may hold values from -6 to 6
Outputs:
- mixed: bfloat16 [8192, 768], P(('batch', 'blk'))
- d_tokens: float32 [8192, 768], P(('batch', 'blk'))
- d_w_qkv: float32 [2, 768, 2304], P(None, 'blk')
- d_w_out: float32 [2, 768, 768], P(None, 'blk')
- d_w_up: float32 [2, 768, 3072], P(None, 'blk')
- d_w_down: float32 [2, 3072, 768], P(None, 'blk')
- d_gain_attn: float32 [2, 768], P(None, 'blk')
- d_gain_mlp: float32 [2, 768], P(None, 'blk')
- d_w_mu: float32 [2, 256], P(None, 'blk')
- d_w_sig: float32 [2, 256], P(None, 'blk')
The draws below stay inside these ranges and needn't reach their ends.
Inputs may be any that keep to these rules, and one draw needn't show every extreme that they name: `seg_count`: some document fills all 4 segments; most are short.
All inputs are finite; a program needn't handle non-finite values.
Results may differ from the reference program's by a relative error of at most 0.018.
Values may be sent and summed in bfloat16 or wider, within the bound.
No kernel may reach another device: no remote copies, remote signals or barrier semaphores. Data moves between devices by JAX's collectives and lax.ppermute only.
A program may use at most 448 MiB of HBM per device.

```python
import jax
import jax.numpy as jnp
from jax import lax

HEADS = 12
HEAD = 64
D = 768
FF = 3072
NBASIS = 256
LAYERS = 2
ROWS = 256
MEMPOS = 4096
DOCS = 8
SEQ = 1024
MEM = 512
TOKENS = 8192
N_BLK = 4


def draw_seg_count(key, part):
    key = jax.random.fold_in(key, 7)
    first_key, second_key, third_key = jax.random.split(key, 3)
    first = jax.random.randint(first_key, (DOCS,), 1, N_BLK + 1)
    second = jax.random.randint(second_key, (DOCS,), 1, N_BLK + 1)
    counts = jnp.minimum(first, second)
    chosen = jax.random.randint(third_key, (), 0, DOCS)
    counts = jnp.where(jnp.arange(DOCS) == chosen, N_BLK, counts)
    return counts.astype(jnp.int32)


def touch_ends(values, key, smallest, top_value):
    longest = values.shape.index(max(values.shape))
    spots = []
    for shift in (0, 1):
        where = [jax.random.randint(jax.random.fold_in(key, axis), (), 0, length) for axis, length in enumerate(values.shape)]
        where[longest] = (where[longest] + shift) % values.shape[longest]
        spots.append(tuple(where))
    return values.at[spots[0]].set(smallest).at[spots[1]].set(top_value)


def block_scale(rng, dims, cuts, low, high):
    def one(dim, shards_of):
        steps = jax.random.uniform(jax.random.fold_in(jax.random.fold_in(rng, 6), dim), (shards_of,), jnp.float32, low / len(cuts), high / len(cuts))
        return jnp.repeat(jnp.exp(steps), dims[dim] // shards_of).reshape((-1,) + (1,) * (len(dims) - dim - 1))

    loudness = one(*cuts[0])
    for cut in cuts[1:]:
        loudness = loudness * one(*cut)
    return loudness


def gaussian(rng, shape, scale, reach, shards=(), kind=jnp.bfloat16):
    result = jax.random.normal(rng, shape, jnp.float32) * scale
    if len(shards) > 0:
        result = block_scale(rng, shape, shards, -0.22, 0.18) * result
    return jnp.clip(result, min=-reach, max=reach).astype(kind)


def setup_inputs(seed: int = 0) -> dict:
    streams_of = jax.random.split(jax.random.key(seed), 14)
    tokens = gaussian(streams_of[0], (TOKENS, D), 1.0, 6.0, ((0, 32),))
    memory = gaussian(streams_of[1], (DOCS, MEM, D), 1.0, 6.0, ((0, 8), (1, 4)))
    mem_pos = touch_ends(jax.random.randint(streams_of[2], (DOCS, MEM), 0, MEMPOS), jax.random.fold_in(streams_of[2], 1), 0, MEMPOS - 1).astype(jnp.int32)
    seg_count = draw_seg_count(jax.random.fold_in(streams_of[13], 71), 0)
    w_qkv = gaussian(streams_of[4], (LAYERS, D, 3 * D), D ** -0.5, 0.21875)
    w_out = gaussian(streams_of[5], (LAYERS, D, D), (D // 16) ** -0.5, 0.875)
    w_up = gaussian(streams_of[6], (LAYERS, D, FF), D ** -0.5, 0.21875)
    w_down = gaussian(streams_of[7], (LAYERS, FF, D), FF ** -0.5, 0.109375)
    gain_attn = jnp.clip(1.0 + 0.1 * jax.random.normal(streams_of[8], (LAYERS, D), jnp.float32), 0.5, 1.5)
    gain_mlp = jnp.clip(1.0 + 0.1 * jax.random.normal(streams_of[9], (LAYERS, D), jnp.float32), 0.5, 1.5)
    w_mu = gaussian(streams_of[10], (LAYERS, NBASIS), (4 * NBASIS) ** -0.5, 0.1875, (), jnp.float32)
    w_sig = gaussian(streams_of[11], (LAYERS, NBASIS), (4 * NBASIS) ** -0.5, 0.1875, (), jnp.float32)
    cotangent = gaussian(streams_of[12], (TOKENS, D), 1.0, 6.0, ((0, 32),))
    return {"tokens": tokens, "memory": memory, "mem_pos": mem_pos, "seg_count": seg_count, "w_qkv": w_qkv, "w_out": w_out, "w_up": w_up, "w_down": w_down, "gain_attn": gain_attn, "gain_mlp": gain_mlp, "w_mu": w_mu, "w_sig": w_sig, "cotangent": cotangent}


highest = lax.Precision.HIGHEST
ridge_weight = 0.5

@jax.custom_vjp
def low(v):
    return lax.optimization_barrier(v.astype(jnp.bfloat16)).astype(jnp.float32)

@jax.custom_vjp
def low_back(v):
    return v

def low_keep(v):
    return (low(v), None)

def low_pass(kept, grad):
    return (grad,)

def back_keep(v):
    return (v, None)

def back_low(kept, grad):
    return (low(grad),)
low.defvjp(low_keep, low_pass)
low_back.defvjp(back_keep, back_low)

def rounded(value):
    return low(low_back(value))

def layer_norm(inputs, gain):
    average = lax.optimization_barrier(jnp.mean(inputs, axis=-1, keepdims=True))
    centred = inputs - average
    spread = lax.optimization_barrier(jnp.mean(centred * centred, axis=-1, keepdims=True))
    return centred * lax.rsqrt(spread + 1e-05) * gain

def centres_of(count):
    return (jnp.arange(count).astype(jnp.float32) + 0.5) / count

def density(scores, weight_mu, weight_sig):
    count = scores.shape[-1]
    breadth = 1.0 / count
    place = jax.nn.sigmoid(lax.optimization_barrier(jnp.sum(scores * weight_mu, axis=-1, keepdims=True)))
    variance = (0.5 + jax.nn.softplus(lax.optimization_barrier(jnp.sum(scores * weight_sig, axis=-1, keepdims=True)))) / 64.0
    offset = place - centres_of(count)
    return jnp.sqrt(breadth * breadth / variance) * jnp.exp(-offset * offset / (2.0 * variance))

def basis_table(positions):
    breadth = 1.0 / NBASIS
    times = (positions.astype(jnp.float32) + 0.5) / MEMPOS
    offset = times[:, None] - centres_of(NBASIS)[None, :]
    return jnp.exp(-offset * offset / (2.0 * breadth * breadth))

def coefficients(samples, positions):
    basis = basis_table(positions)
    gram = jnp.dot(basis.T, basis, precision=highest) + ridge_weight * jnp.eye(NBASIS, dtype=jnp.float32)
    right = jnp.dot(basis.T, samples, precision=highest)
    factor = jnp.linalg.cholesky(gram)
    return jax.scipy.linalg.cho_solve((factor, True), right)

def block(hidden, coeff_low, allowed, layer, params):
    w_qkv, w_out, w_up, w_down, gain_attn, gain_mlp, w_mu, w_sig = params
    length = hidden.shape[0]
    scale = HEAD ** (-0.5)
    normed = low(layer_norm(hidden, gain_attn[layer]))
    qkv = rounded(jnp.dot(normed, w_qkv[layer], precision=highest))
    query = qkv[:, :D].reshape(length, HEADS, HEAD)
    keys = qkv[:, D:2 * D].reshape(length, HEADS, HEAD)
    values = qkv[:, 2 * D:].reshape(length, HEADS, HEAD)
    scores = low_back(jnp.einsum('qhd,khd->hqk', query, keys, precision=highest) * scale)
    scores = jnp.where(allowed[None], scores, -1e+30)
    probs = low(jax.nn.softmax(scores, axis=-1))
    local = jnp.einsum('hqk,khd->qhd', probs, values, precision=highest)
    memory_kv = low(jnp.dot(coeff_low, w_qkv[layer][:, D:], precision=highest))
    mem_keys = memory_kv[:, :D].reshape(NBASIS, HEADS, HEAD)
    mem_values = memory_kv[:, D:].reshape(NBASIS, HEADS, HEAD)
    mem_scores = low_back(jnp.einsum('qhd,nhd->hqn', query, mem_keys, precision=highest) * scale)
    weights = low(density(mem_scores, w_mu[layer], w_sig[layer]))
    recalled = jnp.einsum('hqn,nhd->qhd', weights, mem_values, precision=highest)
    attended = rounded((local + recalled).reshape(length, D))
    middle = hidden + low_back(jnp.dot(attended, w_out[layer], precision=highest))
    normed2 = low(layer_norm(middle, gain_mlp[layer]))
    upward = low_back(jnp.dot(normed2, w_up[layer], precision=highest))
    active = low(jax.nn.gelu(upward, approximate=True))
    return middle + low_back(jnp.dot(active, w_down[layer], precision=highest))

def document(inputs, coeffs, length, params):
    places = jnp.arange(SEQ).astype(jnp.int32)
    allowed = (places[None, :] <= places[:, None]) & (places[None, :] < length)
    coeff_low = low(coeffs)
    hidden = inputs
    for layer in range(LAYERS):
        hidden = block(hidden, coeff_low, allowed, layer, params)
    return hidden

def reference(tokens, memory, mem_pos, seg_count, w_qkv, w_out, w_up, w_down, gain_attn, gain_mlp, w_mu, w_sig, cotangent):
    lengths = (seg_count * ROWS).astype(jnp.int32)
    params = tuple((item.astype(jnp.float32) for item in (w_qkv, w_out, w_up, w_down, gain_attn, gain_mlp, w_mu, w_sig)))
    inputs = tokens.astype(jnp.float32).reshape(DOCS, SEQ, D)
    samples_all = memory.astype(jnp.float32)

    def forward(inputs, params):

        def coeff_one(item):
            return coefficients(item[0], item[1])
        coeffs = lax.map(coeff_one, (samples_all, mem_pos))

        def one_doc(item):
            return document(item[0], item[1], item[2], params)
        return lax.map(jax.checkpoint(one_doc), (inputs, coeffs, lengths))
    outputs, pullback = jax.vjp(forward, inputs, params)
    places = jnp.arange(SEQ).astype(jnp.int32)
    live = (places[None, :] < lengths[:, None]).astype(jnp.float32)
    grad_out = cotangent.astype(jnp.float32).reshape(DOCS, SEQ, D) * live[:, :, None]
    d_inputs, d_params = pullback(grad_out)
    return (outputs.reshape(TOKENS, D).astype(jnp.bfloat16), d_inputs.reshape(TOKENS, D), d_params[0], d_params[1], d_params[2], d_params[3], d_params[4], d_params[5], d_params[6], d_params[7])
```

```python
import jax
import jax.numpy as jnp
from jax import lax
from jax.sharding import PartitionSpec as P

HEADS = 12
HEAD = 64
D = 768
NBASIS = 256
LAYERS = 2
MEMPOS = 4096

highest = lax.Precision.HIGHEST
ridge_weight = 0.5
bf16 = jnp.bfloat16
f32 = jnp.float32


def dot32(a, b):
    return jnp.dot(a, b, preferred_element_type=f32)


def layer_norm(inputs, gain):
    average = jnp.mean(inputs, axis=-1, keepdims=True)
    centred = inputs - average
    spread = jnp.mean(centred * centred, axis=-1, keepdims=True)
    return centred * lax.rsqrt(spread + 1e-05) * gain


def centres_of(count):
    return (jnp.arange(count).astype(f32) + 0.5) / count


def density(scores, weight_mu, weight_sig):
    count = scores.shape[-1]
    breadth = 1.0 / count
    place = jax.nn.sigmoid(jnp.sum(scores * weight_mu, axis=-1, keepdims=True))
    variance = (0.5 + jax.nn.softplus(jnp.sum(scores * weight_sig, axis=-1, keepdims=True))) / 64.0
    offset = place - centres_of(count)
    return jnp.sqrt(breadth * breadth / variance) * jnp.exp(-offset * offset / (2.0 * variance))


def basis_table(positions):
    breadth = 1.0 / NBASIS
    times = (positions.astype(f32) + 0.5) / MEMPOS
    offset = times[:, None] - centres_of(NBASIS)[None, :]
    return jnp.exp(-offset * offset / (2.0 * breadth * breadth))


def gelu_piece(upward):
    return jax.nn.gelu(upward, approximate=True)


def masked_scores(query, keys, allowed, scale):
    scores = jnp.einsum("qhd,khd->hqk", query, keys, preferred_element_type=f32) * scale
    return jnp.where(allowed[None], scores, -1e30)


def swap(value, axis, bit):
    count = lax.axis_size(axis)
    return lax.ppermute(value, axis, [(i, i ^ bit) for i in range(count)])


def bits_of(axis):
    return [1 << i for i in range(lax.axis_size(axis).bit_length() - 1)]


def relative_gather(value, axis):
    held = {0: value}
    for bit in reversed(bits_of(axis)):
        held.update({k | bit: swap(v, axis, bit) for k, v in list(held.items())})
    return [held[k] for k in range(lax.axis_size(axis))]


def relative_scatter(parts, axis):
    held = dict(enumerate(parts))
    for bit in bits_of(axis):
        sent = {k: swap(v, axis, bit) for k, v in held.items() if k & bit}
        held = {
            k: (v.astype(f32) + sent[k | bit].astype(f32)).astype(bf16)
            for k, v in held.items()
            if not k & bit
        }
    return held[0]


def split_order(count):
    width = count.bit_length() - 1
    return [int(format(k, "b").zfill(width)[::-1], 2) if width else 0 for k in range(count)]


def shard_columns(left, axis):
    count = lax.axis_size(axis)
    own = lax.axis_index(axis)
    size = left.shape[1] // count
    return [
        lax.dynamic_slice_in_dim(left, jnp.bitwise_xor(own, k) * size, size, axis=1)
        for k in split_order(count)
    ]


def reduce_weight(left, right):
    pieces = shard_columns(left, "blk")
    half = len(pieces) // 2
    keep = jnp.concatenate(pieces[:half], 1)
    send = jnp.concatenate(pieces[half:], 1)
    bits = bits_of("blk")
    got = swap(dot32(send.T, right).astype(bf16), "blk", bits[0])
    total = (dot32(keep.T, right) + got.astype(f32)).astype(bf16)
    for bit in bits[1:]:
        rows = total.shape[0] // 2
        got = swap(total[rows:], "blk", bit)
        total = (total[:rows].astype(f32) + got.astype(f32)).astype(bf16)
    own = lax.axis_index("batch")
    bits = bits_of("batch")
    for bit in bits:
        rows = total.shape[0] // 2
        side = jnp.where(jnp.bitwise_and(own, bit) > 0, rows, 0)
        got = swap(lax.dynamic_slice_in_dim(total, rows - side, rows, 0), "batch", bit)
        kept = lax.dynamic_slice_in_dim(total, side, rows, 0)
        total = (kept.astype(f32) + got.astype(f32)).astype(bf16)
    for bit in reversed(bits):
        got = swap(total, "batch", bit)
        upper = jnp.bitwise_and(own, bit) > 0
        total = jnp.concatenate([jnp.where(upper, got, total), jnp.where(upper, total, got)], 0)
    return total.astype(f32)


def on_device(
    tokens,
    memory,
    mem_pos,
    seg_count,
    w_qkv,
    w_out,
    w_up,
    w_down,
    gain_attn,
    gain_mlp,
    w_mu,
    w_sig,
    cotangent,
):
    rows = tokens.shape[0]
    width = D
    heads = HEADS
    head = HEAD
    count = lax.axis_size("blk")
    seq = rows * count
    scale = HEAD ** (-0.5)
    length = seg_count[0] * rows
    own = lax.axis_index("blk")
    own_places = own * rows + jnp.arange(rows, dtype=jnp.int32)
    all_places = jnp.concatenate(
        [jnp.bitwise_xor(own, k) * rows + jnp.arange(rows, dtype=jnp.int32) for k in range(count)]
    )
    allowed = (all_places[None, :] <= own_places[:, None]) & (all_places[None, :] < length)
    places = jnp.concatenate(relative_gather(mem_pos[0], "blk"), 0)
    samples = jnp.concatenate(relative_gather(memory[0], "blk"), 0).astype(f32)
    basis = basis_table(places)
    gram = jnp.dot(basis.T, basis, precision=highest)
    right = jnp.dot(basis.T, samples, precision=highest)
    gram = gram + ridge_weight * jnp.eye(NBASIS, dtype=f32)
    factor = jnp.linalg.cholesky(gram)
    coeff_low = jax.scipy.linalg.cho_solve((factor, True), right).astype(bf16)
    hidden = tokens.astype(f32)
    saved = []
    for layer in range(LAYERS):
        normed = layer_norm(hidden, gain_attn[layer]).astype(bf16)
        normed_all = jnp.concatenate(relative_gather(normed, "blk"), 0)
        query = dot32(normed, w_qkv[layer][:, :width]).astype(bf16).reshape(rows, heads, head)
        kv_whole = dot32(normed_all, w_qkv[layer][:, width:]).astype(bf16)
        keys = kv_whole[:, :width].reshape(seq, heads, head)
        values = kv_whole[:, width:].reshape(seq, heads, head)
        scores = masked_scores(query, keys, allowed, scale)
        peak = jnp.max(scores, axis=-1, keepdims=True)
        expo = jnp.exp(scores - peak)
        total = jnp.sum(expo, axis=-1, keepdims=True)
        probs = (expo / total).astype(bf16)
        log_total = peak + jnp.log(total)
        local = jnp.einsum("hqk,khd->qhd", probs, values, preferred_element_type=f32)
        memory_kv = dot32(coeff_low, w_qkv[layer][:, width:]).astype(bf16)
        mem_keys = memory_kv[:, :width].reshape(NBASIS, heads, head)
        mem_values = memory_kv[:, width:].reshape(NBASIS, heads, head)
        mem_scores = (
            jnp.einsum("qhd,nhd->hqn", query, mem_keys, preferred_element_type=f32) * scale
        )
        weights = density(mem_scores, w_mu[layer], w_sig[layer]).astype(bf16)
        recalled = jnp.einsum("hqn,nhd->qhd", weights, mem_values, preferred_element_type=f32)
        attended = (local + recalled).reshape(rows, width).astype(bf16)
        middle = hidden + dot32(attended, w_out[layer])
        normed2 = layer_norm(middle, gain_mlp[layer]).astype(bf16)
        upward = dot32(normed2, w_up[layer])
        active = gelu_piece(upward).astype(bf16)
        saved.append(
            (
                hidden,
                normed,
                normed_all,
                query,
                keys,
                values,
                log_total,
                mem_keys,
                mem_values,
                attended,
                middle,
                normed2,
                upward,
                active,
            )
        )
        hidden = middle + dot32(active, w_down[layer])
    live = (own_places < length).astype(f32)[:, None]
    grad = cotangent.astype(f32) * live
    results = [None] * LAYERS
    small = [None] * LAYERS
    for layer in reversed(range(LAYERS)):
        (
            layer_input,
            normed,
            normed_all,
            query,
            keys,
            values,
            log_total,
            mem_keys,
            mem_values,
            attended,
            middle,
            normed2,
            upward,
            active,
        ) = saved[layer]
        grad_low = grad.astype(bf16)
        d_down = reduce_weight(active, grad_low)
        d_active = dot32(grad_low, w_down[layer].T)
        unused, gelu_back = jax.vjp(gelu_piece, upward)
        d_upward = gelu_back(d_active)[0].astype(bf16)
        d_up = reduce_weight(normed2, d_upward)
        d_normed2 = dot32(d_upward, w_up[layer].T)
        unused, norm_back = jax.vjp(layer_norm, middle, gain_mlp[layer])
        d_middle, d_gain_mlp = norm_back(d_normed2)
        grad = grad + d_middle
        grad_low = grad.astype(bf16)
        d_out = reduce_weight(attended, grad_low)
        d_attended = dot32(grad_low, w_out[layer].T).astype(bf16)
        d_heads = d_attended.reshape(rows, heads, head)
        scores = masked_scores(query, keys, allowed, scale)
        probs = jnp.exp(scores - log_total)
        probs_low = probs.astype(bf16)
        d_probs = jnp.einsum("qhd,khd->hqk", d_heads, values, preferred_element_type=f32)
        correction = jnp.sum(probs * d_probs, axis=-1, keepdims=True)
        d_scores = (probs * (d_probs - correction)).astype(bf16)
        d_query = jnp.einsum("hqk,khd->qhd", d_scores, keys, preferred_element_type=f32)
        d_keys = jnp.einsum("hqk,qhd->khd", d_scores, query, preferred_element_type=f32)
        d_values = jnp.einsum("hqk,qhd->khd", probs_low, d_heads, preferred_element_type=f32)
        mem_scores = (
            jnp.einsum("qhd,nhd->hqn", query, mem_keys, preferred_element_type=f32) * scale
        )
        weights, density_back = jax.vjp(density, mem_scores, w_mu[layer], w_sig[layer])
        weights_low = weights.astype(bf16)
        d_weights = jnp.einsum("qhd,nhd->hqn", d_heads, mem_values, preferred_element_type=f32)
        d_mem_values = jnp.einsum("hqn,qhd->nhd", weights_low, d_heads, preferred_element_type=f32)
        d_mem_scores, d_mu, d_sig = density_back(d_weights)
        d_mem_low = d_mem_scores.astype(bf16)
        d_query = d_query + jnp.einsum(
            "hqn,nhd->qhd", d_mem_low, mem_keys, preferred_element_type=f32
        )
        d_mem_keys = jnp.einsum("hqn,qhd->nhd", d_mem_low, query, preferred_element_type=f32)
        d_query = (d_query * scale).reshape(rows, width).astype(bf16)
        d_kv = jnp.concatenate(
            [(d_keys * scale).reshape(seq, width), d_values.reshape(seq, width)], 1
        ).astype(bf16)
        d_memory_kv = jnp.concatenate(
            [(d_mem_keys * scale).reshape(NBASIS, width), d_mem_values.reshape(NBASIS, width)], 1
        ).astype(bf16)
        d_normed_terms = dot32(d_kv, w_qkv[layer][:, width:].T)
        d_normed_terms = d_normed_terms + jnp.pad(
            dot32(d_query, w_qkv[layer][:, :width].T), ((0, seq - rows), (0, 0))
        )
        d_normed_terms = d_normed_terms.astype(bf16).reshape(count, rows, width)
        d_normed = relative_scatter([d_normed_terms[k] for k in range(count)], "blk").astype(f32)
        d_kv_weight = reduce_weight(
            jnp.concatenate([normed_all, coeff_low], 0), jnp.concatenate([d_kv, d_memory_kv], 0)
        )
        d_q_weight = reduce_weight(normed, d_query)
        unused, norm_back = jax.vjp(layer_norm, layer_input, gain_attn[layer])
        d_input, d_gain_attn = norm_back(d_normed)
        grad = grad + d_input
        results[layer] = (jnp.concatenate([d_q_weight, d_kv_weight], 1), d_out, d_up, d_down)
        small[layer] = (d_gain_attn, d_gain_mlp, d_mu, d_sig)
    sizes = [item.shape[0] for item in small[0]]
    packed = jnp.concatenate([item for layer in small for item in layer])
    packed = lax.psum(packed, ("batch", "blk")).reshape(LAYERS, sum(sizes))
    shares = []
    first = 0
    for size in sizes:
        share = size // count
        shares.append(lax.dynamic_slice_in_dim(packed, first + own * share, share, 1))
        first += size
    return (
        hidden.astype(bf16),
        grad,
        *[jnp.stack([results[layer][i] for layer in range(LAYERS)]) for i in range(4)],
        *shares,
    )


def solution(mesh):
    placed = (
        P(("batch", "blk"), None),
        P("batch", "blk", None),
        P("batch", "blk"),
        P("batch"),
        P(),
        P(),
        P(),
        P(),
        P(),
        P(),
        P(),
        P(),
        P(("batch", "blk"), None),
    )
    return jax.shard_map(
        on_device,
        mesh=mesh,
        in_specs=placed,
        out_specs=(
            P(("batch", "blk"), None),
            P(("batch", "blk"), None),
            P(None, "blk", None),
            P(None, "blk", None),
            P(None, "blk", None),
            P(None, "blk", None),
            P(None, "blk"),
            P(None, "blk"),
            P(None, "blk"),
            P(None, "blk"),
        ),
        check_vma=False,
    )
```

```python
import functools

import jax
import jax.numpy as jnp
from jax import lax
from jax.experimental import pallas as pl
from jax.experimental.pallas import tpu as pltpu
from jax.sharding import PartitionSpec as P

HEADS = 12
HEAD = 64
D = 768
NBASIS = 256
LAYERS = 2
MEMPOS = 4096
PAIRS = HEADS // 2
PAIR = 2 * HEAD

COST_SCALE = 5e8
highest = lax.Precision.HIGHEST
ridge_weight = 0.5
bf16 = jnp.bfloat16
f32 = jnp.float32

NT = (((1,), (1,)), ((), ()))
TN = (((0,), (0,)), ((), ()))
VMEM = pl.BlockSpec(memory_space=pltpu.VMEM)


ANY = pl.BlockSpec(memory_space=pl.ANY)
LIMIT = 58 * 1024 * 1024
CHUNKS = 4


def cost(microseconds):
    return pl.CostEstimate(
        flops=int(microseconds * COST_SCALE), bytes_accessed=0, transcendentals=0
    )


def gauss_jordan(panel, first):
    count, width = panel.shape
    lane = lax.broadcasted_iota(jnp.int32, (1, width), 1)
    line = lax.broadcasted_iota(jnp.int32, (count, 1), 0)

    def spread(value, column):
        return jnp.broadcast_to(value[:, column : column + 1], value.shape)

    for p in range(0, count, 2):
        c = first + p
        row0, row1 = panel[p : p + 1, :], panel[p + 1 : p + 2, :]
        a, b = spread(row0, c), spread(row0, c + 1)
        e, d = spread(row1, c), spread(row1, c + 1)
        over = 1.0 / (a * d - b * e)
        clear0 = jnp.where(lane == c, 1.0, jnp.where(lane == c + 1, 0.0, row0))
        clear1 = jnp.where(lane == c, 0.0, jnp.where(lane == c + 1, 1.0, row1))
        new0 = (d * clear0 - b * clear1) * over
        new1 = (a * clear1 - e * clear0) * over
        factor0, factor1 = spread(panel, c), spread(panel, c + 1)
        rest = jnp.where((lane == c) | (lane == c + 1), 0.0, panel)
        rest = rest - factor0 * new0 - factor1 * new1
        panel = jnp.where(line == p, new0, jnp.where(line == p + 1, new1, rest))
    return panel


def basis_of(places):
    times = (places.astype(f32) + 0.5) / MEMPOS
    centres = (lax.broadcasted_iota(jnp.int32, (NBASIS, 1), 0).astype(f32) + 0.5) / NBASIS
    breadth = 1.0 / NBASIS
    offset = times - centres
    return jnp.exp(-offset * offset / (2.0 * breadth * breadth))


def gram_of(basis):
    line = lax.broadcasted_iota(jnp.int32, (NBASIS, NBASIS), 0)
    lane = lax.broadcasted_iota(jnp.int32, (NBASIS, NBASIS), 1)
    gram = lax.dot_general(basis, basis, NT, precision=highest, preferred_element_type=f32)
    return gram + jnp.where(line == lane, ridge_weight, 0.0)


def inverse_kernel(places_ref, inverse_ref):
    lane = lax.broadcasted_iota(jnp.int32, (NBASIS, NBASIS), 1)
    inverse_ref[...] = gram_of(basis_of(places_ref[...]))
    step = 32
    for first in range(0, NBASIS, step):
        panel = gauss_jordan(inverse_ref[first : first + step, :], first)
        columns = inverse_ref[...][:, first : first + step]
        inside = (lane >= first) & (lane < first + step)
        product = jnp.dot(columns, panel, precision=highest, preferred_element_type=f32)
        inverse_ref[...] = jnp.where(inside, 0.0, inverse_ref[...]) - product
        inverse_ref[first : first + step, :] = panel


def coeff_kernel(places_ref, samples_ref, inverse_ref, coeff_ref):
    def product(a, b):
        return jnp.dot(a, b, precision=highest, preferred_element_type=f32)

    basis = basis_of(places_ref[...])
    right = product(basis, samples_ref[...].astype(f32))
    coeffs = product(inverse_ref[...], right)
    coeffs += product(inverse_ref[...], right - product(gram_of(basis), coeffs))
    coeff_ref[...] = coeffs.astype(bf16)


def ridge_inverse(places):
    return pl.pallas_call(
        inverse_kernel,
        out_shape=jax.ShapeDtypeStruct((NBASIS, NBASIS), f32),
        in_specs=[VMEM],
        out_specs=VMEM,
        compiler_params=pltpu.CompilerParams(vmem_limit_bytes=40 * 1024 * 1024),
        cost_estimate=cost(16.6),
        name="ridge_inverse",
    )(places)


def ridge_coeffs(places, samples, inverse):
    return pl.pallas_call(
        coeff_kernel,
        out_shape=jax.ShapeDtypeStruct((NBASIS, D), bf16),
        in_specs=[VMEM] * 3,
        out_specs=VMEM,
        compiler_params=pltpu.CompilerParams(vmem_limit_bytes=40 * 1024 * 1024),
        cost_estimate=cost(4.4),
        name="ridge_coeffs",
    )(places, samples, inverse)


def expand_maps(maps, mem_keys):
    vectors = jnp.dot(maps, mem_keys.astype(f32), precision=highest, preferred_element_type=f32)
    row = lax.broadcasted_iota(jnp.int32, (8 * PAIRS, D), 0)
    which = row % 8
    lane_head = lax.broadcasted_iota(jnp.int32, (8 * PAIRS, D), 1) // HEAD
    owned = (which < 4) & (lane_head == 2 * (row // 8) + which // 2)
    both = jnp.where(which % 2 == 0, vectors[0:1, :], vectors[1:2, :])
    return jnp.where(owned, both, 0.0)


def memory_weights(logits):
    breadth = 1.0 / NBASIS
    place = 1.0 / (1.0 + jnp.exp(-logits[0:1, :]))
    sigma = logits[1:2, :]
    soft = jnp.maximum(sigma, 0.0) + jnp.log(1.0 + jnp.exp(-jnp.abs(sigma)))
    variance = (0.5 + soft) / 64.0
    centres = (lax.broadcasted_iota(jnp.int32, (NBASIS, 1), 0).astype(f32) + 0.5) / NBASIS
    offset = place - centres
    weights = (breadth * lax.rsqrt(variance)) * jnp.exp(offset * offset * (-0.5 / variance))
    return weights, place, variance, offset


def head_lanes(value, which):
    lane = lax.broadcasted_iota(jnp.int32, value.shape, 1)
    return jnp.where((lane < HEAD) == (which == 0), value, jnp.zeros_like(value))


def pair_block(rows, shift=0):
    return pl.BlockSpec((rows, PAIR), lambda p: (0, p + shift))


def whole_block(shape):
    return pl.BlockSpec(shape, lambda p: (0,) * len(shape))


def attend_back_kernel(
    bias, query_all, mem_keys_all, maps, lse, q, k, v, mv, da,
    dq, dk, dv, dmk, dmv, dmaps, logits, lines, dq_t,
):
    pair = pl.program_id(0)
    scale = HEAD**-0.5

    @pl.when(pair == 0)
    def _():
        table = expand_maps(maps[...], mem_keys_all[...])
        wide = query_all[...].astype(f32) * scale
        logits[...] = lax.dot_general(
            table, wide, NT, precision=highest, preferred_element_type=f32
        )

    rows8 = logits[pl.ds(pl.multiple_of(pair * 8, 8), 8), :]
    k_t = k[...].T
    halves = []
    derived = []
    d_keys = d_values = d_mem_values = None
    for s in range(2):
        qh = head_lanes(q[...], s) * jnp.asarray(scale, bf16)
        dh = head_lanes(da[...], s)
        scores = lax.dot_general(k[...], qh, NT, preferred_element_type=f32) + bias[...]
        probs = jnp.exp(scores - lse[0, s : s + 1, :])
        d_probs = lax.dot_general(v[...], dh, NT, preferred_element_type=f32)
        correction = jnp.sum(probs * d_probs, axis=0, keepdims=True)
        d_scores = (probs * (d_probs - correction)).astype(bf16)
        key_term = jnp.dot(d_scores, qh, preferred_element_type=f32)
        value_term = jnp.dot(probs.astype(bf16), dh, preferred_element_type=f32)
        query_term = jnp.dot(k_t, d_scores, preferred_element_type=f32) * scale
        weights, place, variance, offset = memory_weights(rows8[2 * s : 2 * s + 2, :])
        d_weights = lax.dot_general(mv[...], dh, NT, preferred_element_type=f32)
        mem_term = jnp.dot(weights.astype(bf16), dh, preferred_element_type=f32)
        moved = d_weights * weights
        sum0 = jnp.sum(moved, axis=0, keepdims=True)
        moved = moved * offset
        sum1 = jnp.sum(moved, axis=0, keepdims=True)
        sum2 = jnp.sum(moved * offset, axis=0, keepdims=True)
        d_place = -sum1 / variance
        d_variance = (sum2 / variance - sum0) * (0.5 / variance)
        derived.append(d_place * place * (1.0 - place))
        sigma = rows8[2 * s + 1 : 2 * s + 2, :]
        derived.append(d_variance * (1.0 / 64.0) / (1.0 + jnp.exp(-sigma)))
        halves.append(query_term[s * HEAD : (s + 1) * HEAD, :])
        d_keys = key_term if s == 0 else d_keys + key_term
        d_values = value_term if s == 0 else d_values + value_term
        d_mem_values = mem_term if s == 0 else d_mem_values + mem_term
    dk[...] = d_keys.astype(bf16)
    dv[...] = d_values.astype(bf16)
    dmv[...] = d_mem_values.astype(bf16)
    dq_t[pair] = jnp.concatenate(halves, 0).T
    lines[pl.ds(pl.multiple_of(pair * 8, 8), 8), :] = jnp.concatenate(
        derived + [jnp.zeros((4, derived[0].shape[1]), f32)], 0
    )

    @pl.when(pair == PAIRS - 1)
    def _():
        table = expand_maps(maps[...], mem_keys_all[...])
        low = lines[...].astype(bf16)
        back = lax.dot_general(low, table.astype(bf16), TN, preferred_element_type=f32) * scale
        for p in range(PAIRS):
            at = slice(p * PAIR, (p + 1) * PAIR)
            dq[:, at] = (dq_t[p] + back[:, at]).astype(bf16)
        sums = jnp.dot(low, query_all[...], preferred_element_type=f32) * scale
        row = lax.broadcasted_iota(jnp.int32, sums.shape, 0)
        which = row % 8
        lane_head = lax.broadcasted_iota(jnp.int32, sums.shape, 1) // HEAD
        owned = (which < 4) & (lane_head == 2 * (row // 8) + which // 2)
        sums = jnp.where(owned, sums, 0.0)
        even = jnp.sum(jnp.where(which % 2 == 0, sums, 0.0), axis=0, keepdims=True)
        odd = jnp.sum(jnp.where(which % 2 == 1, sums, 0.0), axis=0, keepdims=True)
        both = jnp.concatenate([even, odd, jnp.zeros((6, D), f32)], 0).astype(bf16)
        dmk[...] = lax.dot_general(
            maps[...].astype(bf16), both, TN, preferred_element_type=f32
        ).astype(bf16)
        dmaps[...] = lax.dot_general(both, mem_keys_all[...], NT, preferred_element_type=f32)


def attend_back(bias, query, kv, memory_kv, maps, lse, d_attended, extra=()):
    rows = query.shape[0]
    seq = kv.shape[0]
    return pl.pallas_call(
        after(attend_back_kernel, 10, extra),
        grid=(PAIRS,),
        in_specs=[
            whole_block((seq, rows)),
            whole_block((rows, D)),
            whole_block((NBASIS, D)),
            whole_block((8, NBASIS)),
            pl.BlockSpec((1, 8, rows), lambda p: (p, 0, 0)),
            pair_block(rows),
            pair_block(seq),
            pair_block(seq, PAIRS),
            pair_block(NBASIS, PAIRS),
            pair_block(rows),
        ]
        + [ANY] * len(extra),
        out_specs=[
            whole_block((rows, D)),
            pair_block(seq),
            pair_block(seq),
            whole_block((NBASIS, D)),
            pair_block(NBASIS),
            whole_block((8, NBASIS)),
        ],
        out_shape=[
            jax.ShapeDtypeStruct((rows, D), bf16),
            jax.ShapeDtypeStruct((seq, D), bf16),
            jax.ShapeDtypeStruct((seq, D), bf16),
            jax.ShapeDtypeStruct((NBASIS, D), bf16),
            jax.ShapeDtypeStruct((NBASIS, D), bf16),
            jax.ShapeDtypeStruct((8, NBASIS), f32),
        ],
        scratch_shapes=[
            pltpu.VMEM((8 * PAIRS, rows), f32),
            pltpu.VMEM((8 * PAIRS, rows), f32),
            pltpu.VMEM((PAIRS, rows, PAIR), f32),
        ],
        compiler_params=pltpu.CompilerParams(vmem_limit_bytes=56 * 1024 * 1024),
        cost_estimate=cost(18.3),
        name="attend_back",
    )(bias, query, memory_kv, maps, lse, query, kv, kv, memory_kv, d_attended, *extra)


def call_options(name, microseconds):
    return dict(
        compiler_params=pltpu.CompilerParams(vmem_limit_bytes=LIMIT),
        cost_estimate=cost(microseconds),
        name=name,
    )


def after(kernel, inputs, extra):
    def body(*refs):
        kernel(*refs[:inputs], *refs[inputs + len(extra) :])

    return body


def gate(values, extra):
    def kernel(*refs):
        del refs

    count = len(values)
    return pl.pallas_call(
        kernel,
        in_specs=[ANY] * (count + len(extra)),
        out_specs=[ANY] * count,
        out_shape=[jax.ShapeDtypeStruct(value.shape, value.dtype) for value in values],
        input_output_aliases={i: i for i in range(count)},
        **call_options("gate", 1.0),
    )(*values, *extra)


def dot_nt(a, b):
    return lax.dot_general(a, b, NT, preferred_element_type=f32)


def dot_tn(a, b):
    return lax.dot_general(a, b, TN, preferred_element_type=f32)


def normalise(value):
    centred = value - jnp.mean(value, axis=1, keepdims=True)
    spread = jnp.mean(centred * centred, axis=1, keepdims=True)
    factor = lax.rsqrt(spread + 1e-05)
    return centred * factor, factor


def norm_backward(value, gain, d_out):
    unit, factor = normalise(value)
    d_unit = d_out * gain
    mean0 = jnp.mean(d_unit, axis=1, keepdims=True)
    mean1 = jnp.mean(d_unit * unit, axis=1, keepdims=True)
    return factor * (d_unit - mean0 - unit * mean1), jnp.sum(d_out * unit, axis=0, keepdims=True)


def gelu_parts(upward):
    outer = 0.7978845608028654
    square = upward * upward
    inner = jnp.tanh(upward * (outer + outer * 0.044715 * square))
    half = 0.5 * (1.0 + inner)
    slope = half + 0.5 * upward * (1.0 - inner * inner) * (outer + 3.0 * outer * 0.044715 * square)
    return upward * half, slope


def store_shard(count, own, shard, rows, send, keep):
    size = rows.shape[0]
    width = count.bit_length() - 1
    relative = jnp.bitwise_xor(own, shard)
    place = 0
    for bit in range(width):
        place += jnp.bitwise_and(lax.shift_right_logical(relative, bit), 1) << (width - 1 - bit)

    @pl.when(place >= count // 2)
    def _():
        send[pl.ds(pl.multiple_of((place - count // 2) * size, 16), size), :] = rows

    @pl.when(place < count // 2)
    def _():
        keep[pl.ds(pl.multiple_of(place * size, 16), size), :] = rows


def store_shards(count, own, value, send, keep):
    size = value.shape[0] // count
    for shard in range(count):
        rows = value[shard * size : (shard + 1) * size, :].astype(bf16)
        store_shard(count, own, shard, rows, send, keep)


def attend_kernel(layer, count, *refs):
    parts = refs[:count]
    bias, coeff, maps, w_hbm = refs[count : count + 4]
    out, lse, query, kv, memory_kv = refs[count + 4 : count + 9]
    w, logits, sem = refs[count + 9 :]
    copy = pltpu.make_async_copy(w_hbm.at[layer], w, sem)
    copy.start()
    copy.wait()
    rows = query.shape[0]
    query[...] = jnp.dot(parts[0][...], w[:, :D], preferred_element_type=f32).astype(bf16)
    memory_kv[...] = jnp.dot(coeff[...], w[:, D:], preferred_element_type=f32).astype(bf16)
    for k in range(count):
        kv[k * rows : (k + 1) * rows, :] = jnp.dot(
            parts[k][...], w[:, D:], preferred_element_type=f32
        ).astype(bf16)
    table = expand_maps(maps[...], memory_kv[:, :D])
    wide = query[...].astype(f32) * HEAD**-0.5
    logits[...] = lax.dot_general(table, wide, NT, precision=highest, preferred_element_type=f32)

    def body(pair, carry):
        at = pl.ds(pl.multiple_of(pair * PAIR, PAIR), PAIR)
        value_at = pl.ds(pl.multiple_of(D + pair * PAIR, PAIR), PAIR)
        lines = logits[pl.ds(pl.multiple_of(pair * 8, 8), 8), :]
        q, k = query[:, at], kv[:, at]
        v_t = kv[:, value_at].T
        mv_t = memory_kv[:, value_at].T
        halves = []
        totals = []
        for s in range(2):
            qh = head_lanes(q, s) * jnp.asarray(HEAD**-0.5, bf16)
            scores = dot_nt(k, qh) + bias[...]
            peak = jnp.max(scores, axis=0, keepdims=True)
            expo = jnp.exp(scores - peak)
            total = jnp.sum(expo, axis=0, keepdims=True)
            local = jnp.dot(v_t, expo.astype(bf16), preferred_element_type=f32) * (1.0 / total)
            weights = memory_weights(lines[2 * s : 2 * s + 2, :])[0]
            recalled = jnp.dot(mv_t, weights.astype(bf16), preferred_element_type=f32)
            halves.append((local + recalled)[s * HEAD : (s + 1) * HEAD, :])
            totals.append(peak + jnp.log(total))
        out[:, at] = jnp.concatenate(halves, 0).T.astype(bf16)
        lse[pair, 0:1, :] = totals[0]
        lse[pair, 1:2, :] = totals[1]
        return carry

    lax.fori_loop(0, PAIRS, body, 0)


def attend(layer, parts, bias, coeff, maps, w_qkv):
    rows = parts[0].shape[0]
    seq = rows * len(parts)
    return pl.pallas_call(
        functools.partial(attend_kernel, layer, len(parts)),
        in_specs=[VMEM] * (len(parts) + 3) + [ANY],
        out_specs=[VMEM] * 5,
        out_shape=[
            jax.ShapeDtypeStruct((rows, D), bf16),
            jax.ShapeDtypeStruct((PAIRS, 8, rows), f32),
            jax.ShapeDtypeStruct((rows, D), bf16),
            jax.ShapeDtypeStruct((seq, 2 * D), bf16),
            jax.ShapeDtypeStruct((NBASIS, 2 * D), bf16),
        ],
        scratch_shapes=[
            pltpu.VMEM((D, 3 * D), bf16),
            pltpu.VMEM((8 * PAIRS, rows), f32),
            pltpu.SemaphoreType.DMA,
        ],
        **call_options("attend", 20.8),
    )(*parts, bias, coeff, maps, w_qkv)


def mlp_kernel(last, count, own, *refs):
    attended, hidden, gain, next_gain, w_out, w_up, w_down = refs[:7]
    middle, normed2, upward, hidden_out, low_out = refs[7:12]
    shards = refs[12:]
    step = pl.program_id(0)

    @pl.when(step == 0)
    def _():
        middle[...] = hidden[...] + jnp.dot(
            attended[...], w_out[0], preferred_element_type=f32
        )
        normed2[...] = (normalise(middle[...])[0] * gain[...]).astype(bf16)
        hidden_out[...] = middle[...]

    up = jnp.dot(normed2[...], w_up[0], preferred_element_type=f32)
    upward[...] = up
    active = gelu_parts(up)[0].astype(bf16)
    hidden_out[...] += jnp.dot(active, w_down[0], preferred_element_type=f32)
    pieces = max(1, count // CHUNKS)
    share = active.shape[1] // pieces
    for i in range(pieces):
        relative = jnp.bitwise_xor(own[0], step * pieces + i)
        for k in range(count):

            @pl.when(relative == k)
            def _(i=i, k=k):
                shards[k][...] = active[:, i * share : (i + 1) * share]

    @pl.when(step == CHUNKS - 1)
    def _():
        value = hidden_out[...]
        low_out[...] = (value if last else normalise(value)[0] * next_gain[...]).astype(bf16)


def mlp(layer, last, count, own, attended, hidden, gain, next_gain, w_out, w_up, w_down):
    rows = hidden.shape[0]
    hidden_units = w_up.shape[2]
    chunk = hidden_units // CHUNKS
    share = hidden_units // count
    assert count >= CHUNKS
    whole = pl.BlockSpec((rows, D), lambda j, own: (0, 0))
    line = pl.BlockSpec((1, D), lambda j, own: (0, 0))
    shard = pl.BlockSpec((rows, share), lambda j, own: (0, 0))
    return pl.pallas_call(
        functools.partial(mlp_kernel, last, count),
        grid_spec=pltpu.PrefetchScalarGridSpec(
            num_scalar_prefetch=1,
            grid=(CHUNKS,),
            in_specs=[
                whole,
                whole,
                line,
                line,
                pl.BlockSpec((1, D, D), lambda j, own: (layer, 0, 0)),
                pl.BlockSpec((1, D, chunk), lambda j, own: (layer, 0, j)),
                pl.BlockSpec((1, chunk, D), lambda j, own: (layer, j, 0)),
            ],
            out_specs=[
                whole,
                whole,
                pl.BlockSpec((rows, chunk), lambda j, own: (0, j)),
                whole,
                whole,
            ]
            + [shard] * count,
        ),
        out_shape=[
            jax.ShapeDtypeStruct((rows, D), f32),
            jax.ShapeDtypeStruct((rows, D), bf16),
            jax.ShapeDtypeStruct((rows, hidden_units), f32),
            jax.ShapeDtypeStruct((rows, D), f32),
            jax.ShapeDtypeStruct((rows, D), bf16),
        ]
        + [jax.ShapeDtypeStruct((rows, share), bf16)] * count,
        **call_options("mlp", 10.4),
    )(own, attended, hidden, gain, next_gain, w_out, w_up, w_down)


def mlp_back_kernel(
    shards, own, grad, grad_low, upward, normed2, middle, gain, attended, w_out, w_up, w_down,
    send, keep, grad_out, low_out, d_attended, d_gain, left, d_normed,
):
    step = pl.program_id(0)

    @pl.when(step == 0)
    def _():
        left[...] = normed2[...].T

    @pl.when(step < CHUNKS)
    def _():
        d_active = dot_nt(grad_low[...], w_down[0])
        d_up = (d_active * gelu_parts(upward[...])[1]).astype(bf16)
        term = dot_nt(d_up, w_up[0])

        @pl.when(step == 0)
        def _():
            d_normed[...] = term

        @pl.when(step > 0)
        def _():
            d_normed[...] += term

        value = jnp.dot(left[...], d_up, preferred_element_type=f32)
        store_shards(shards, own[0], value, send.at[0], keep.at[0])

    @pl.when(step == CHUNKS)
    def _():
        d_middle, d_line = norm_backward(middle[...], gain[...], d_normed[...])
        total = grad[...] + d_middle
        grad_out[...] = total
        low = total.astype(bf16)
        low_out[...] = low
        d_attended[...] = dot_nt(low, w_out[0]).astype(bf16)
        d_gain[...] = d_line
        store_shards(shards, own[0], dot_tn(attended[...], low), send.at[0], keep.at[0])


def mlp_back(
    layer,
    shards,
    own,
    grad,
    grad_low,
    upward,
    normed2,
    middle,
    gain,
    attended,
    w_out,
    w_up,
    w_down,
    extra=(),
):
    rows = grad.shape[0]
    chunk = w_up.shape[2] // CHUNKS
    last = CHUNKS - 1
    whole = pl.BlockSpec((rows, D), lambda j, own: (0, 0))
    line = pl.BlockSpec((1, D), lambda j, own: (0, 0))
    half = pl.BlockSpec((1, D // 2, chunk), lambda j, own: (j, 0, 0))
    shape = jax.ShapeDtypeStruct((CHUNKS + 1, D // 2, chunk), bf16)
    return pl.pallas_call(
        after(functools.partial(mlp_back_kernel, shards), 11, extra),
        grid_spec=pltpu.PrefetchScalarGridSpec(
            num_scalar_prefetch=1,
            grid=(CHUNKS + 1,),
            in_specs=[
                whole,
                whole,
                pl.BlockSpec((rows, chunk), lambda j, own: (0, jnp.minimum(j, last))),
                whole,
                whole,
                line,
                whole,
                pl.BlockSpec((1, D, D), lambda j, own: (layer, 0, 0)),
                pl.BlockSpec((1, D, chunk), lambda j, own: (layer, 0, jnp.minimum(j, last))),
                pl.BlockSpec((1, chunk, D), lambda j, own: (layer, jnp.minimum(j, last), 0)),
            ]
            + [ANY] * len(extra),
            out_specs=[half, half, whole, whole, whole, line],
            scratch_shapes=[pltpu.VMEM((D, rows), bf16), pltpu.VMEM((rows, D), f32)],
        ),
        out_shape=[
            shape,
            shape,
            jax.ShapeDtypeStruct((rows, D), f32),
            jax.ShapeDtypeStruct((rows, D), bf16),
            jax.ShapeDtypeStruct((rows, D), bf16),
            jax.ShapeDtypeStruct((1, D), f32),
        ],
        **call_options("mlp_back", 14.6),
    )(own, grad, grad_low, upward, normed2, middle, gain, attended, w_out, w_up, w_down, *extra)


def down_kernel(count, *refs):
    out = refs[-1]
    total = dot_tn(refs[0][...], refs[count][...])
    for k in range(1, count):
        total += dot_tn(refs[k][...], refs[count + k][...])
    out[...] = total.astype(bf16)


def down_grad(actives, grads, extra=()):
    count = len(actives)
    return pl.pallas_call(
        after(functools.partial(down_kernel, count), 2 * count, extra),
        in_specs=[VMEM] * (2 * count) + [ANY] * len(extra),
        out_specs=VMEM,
        out_shape=jax.ShapeDtypeStruct((actives[0].shape[1], D), bf16),
        **call_options("down_grad", 4.3),
    )(*actives, *grads, *extra)


def input_kernel(layer, d_query, d_keys, d_values, w_hbm, *refs):
    outs, (w, sem) = refs[:-2], refs[-2:]
    copy = pltpu.make_async_copy(w_hbm.at[layer], w, sem)
    copy.start()
    copy.wait()
    rows = d_query.shape[0]
    total = dot_nt(d_keys[...], w[:, D : 2 * D]) + dot_nt(d_values[...], w[:, 2 * D :])
    outs[0][...] = (total[:rows, :] + dot_nt(d_query[...], w[:, :D])).astype(bf16)
    for k in range(1, len(outs)):
        outs[k][...] = total[k * rows : (k + 1) * rows, :].astype(bf16)


def input_terms(layer, count, d_query, d_keys, d_values, w_qkv, extra=()):
    return pl.pallas_call(
        after(functools.partial(input_kernel, layer), 4, extra),
        in_specs=[VMEM] * 3 + [ANY] + [ANY] * len(extra),
        out_specs=[VMEM] * count,
        out_shape=[jax.ShapeDtypeStruct(d_query.shape, bf16)] * count,
        scratch_shapes=[pltpu.VMEM((D, 3 * D), bf16), pltpu.SemaphoreType.DMA],
        **call_options("input_terms", 7.6),
    )(d_query, d_keys, d_values, w_qkv, *extra)


def attention_grad_kernel(count, own, *refs):
    parts = refs[:count]
    coeff, d_query, d_keys, d_values, d_mem_keys, d_mem_values, send, keep, left = refs[count:]
    rows = d_query.shape[0]
    seq = rows * count
    size = D // count
    for k in range(count):
        left[:, k * rows : (k + 1) * rows] = parts[k][...].T
    left[:, seq:] = coeff[...].T

    def product(a, b):
        return jnp.dot(a, b[...], preferred_element_type=f32)

    for shard in range(count):
        line = left[shard * size : (shard + 1) * size, :]
        own_line, all_line, mem_line = line[:, :rows], line[:, :seq], line[:, seq:]
        values = (
            product(own_line, d_query),
            product(all_line, d_keys) + product(mem_line, d_mem_keys),
            product(all_line, d_values) + product(mem_line, d_mem_values),
        )
        for i, value in enumerate(values):
            store_shard(count, own[0], shard, value.astype(bf16), send.at[i], keep.at[i])


def attention_grads(own, parts, coeff, derivatives, extra=()):
    smem = pl.BlockSpec(memory_space=pltpu.SMEM)
    shape = jax.ShapeDtypeStruct((3, D // 2, D), bf16)
    inputs = (*parts, coeff, *derivatives)
    return pl.pallas_call(
        after(functools.partial(attention_grad_kernel, len(parts)), 1 + len(inputs), extra),
        in_specs=[smem] + [VMEM] * len(inputs) + [ANY] * len(extra),
        out_specs=[VMEM, VMEM],
        out_shape=[shape, shape],
        scratch_shapes=[pltpu.VMEM((D, parts[0].shape[0] * len(parts) + NBASIS), bf16)],
        **call_options("attention_grads", 9.6),
    )(own, *inputs, *extra)


def norm_back_kernel(value, gain, d_out, grad, grad_out, low_out, d_gain):
    d_value, d_line = norm_backward(value[...], gain[...], d_out[...].astype(f32))
    total = grad[...] + d_value
    grad_out[...] = total
    low_out[...] = total.astype(bf16)
    d_gain[...] = d_line


def norm_back(value, gain, d_out, grad, extra=()):
    return pl.pallas_call(
        after(norm_back_kernel, 4, extra),
        in_specs=[VMEM] * 4 + [ANY] * len(extra),
        out_specs=[VMEM] * 3,
        out_shape=[
            jax.ShapeDtypeStruct(grad.shape, f32),
            jax.ShapeDtypeStruct(grad.shape, bf16),
            jax.ShapeDtypeStruct((1, D), f32),
        ],
        **call_options("norm_back", 3.1),
    )(value, gain, d_out, grad, *extra)


def start_kernel(live, tokens, gain, cotangent, hidden, normed, grad, grad_low):
    wide = tokens[...].astype(f32)
    hidden[...] = wide
    normed[...] = (normalise(wide)[0] * gain[...]).astype(bf16)
    masked = cotangent[...].astype(f32) * live[0].astype(f32)
    grad[...] = masked
    grad_low[...] = masked.astype(bf16)


def start(live, tokens, gain, cotangent):
    return pl.pallas_call(
        start_kernel,
        in_specs=[pl.BlockSpec(memory_space=pltpu.SMEM)] + [VMEM] * 3,
        out_specs=[VMEM] * 4,
        out_shape=[jax.ShapeDtypeStruct(tokens.shape, kind) for kind in (f32, bf16, f32, bf16)],
        **call_options("start", 2.5),
    )(live, tokens, gain, cotangent)


def swap(value, axis, bit):
    count = lax.axis_size(axis)
    return lax.ppermute(value, axis, [(i, i ^ bit) for i in range(count)])


def bits_of(axis):
    return [1 << i for i in range(lax.axis_size(axis).bit_length() - 1)]


def gather_steps(held, axis, bits):
    held = dict(held)
    for bit in reversed(bits):
        held.update({k | bit: swap(v, axis, bit) for k, v in list(held.items())})
    return held


def relative_gather(value, axis):
    held = gather_steps({0: value}, axis, bits_of(axis))
    return [held[k] for k in range(lax.axis_size(axis))]


def scatter_step(held, axis, bit):
    sent = {k: swap(v, axis, bit) for k, v in held.items() if k & bit}
    return {
        k: (v.astype(f32) + sent[k | bit].astype(f32)).astype(bf16)
        for k, v in held.items()
        if not k & bit
    }


class Sum:
    def __init__(self, *terms):
        self.terms = [(term, 0) for term in terms]
        self.rows = terms[0].shape[1]

    def added(self, terms):
        parts = [
            value
            if value.shape[1] == self.rows
            else lax.dynamic_slice_in_dim(value, at, self.rows, 1)
            for value, at in terms
        ]
        if len(parts) == 1:
            return parts[0]
        return sum(part.astype(f32) for part in parts).astype(bf16)

    def whole(self):
        return self.added(self.terms)

    def blocks(self):
        return self.terms[0][0].shape[0]

    def newest(self):
        return [self.terms[-1][0]]

    def split(self, side):
        self.rows = self.rows // 2
        sent = [(value, at + (1 - side) * self.rows) for value, at in self.terms]
        sent = self.added(sent)
        self.terms = [(value, at + side * self.rows) for value, at in self.terms]
        return sent

    def take(self, got):
        self.terms.append((got, 0))

    def over_blk(self, bit):
        return self.split(0), "blk", bit

    def over_batch(self, bit):
        side = jnp.where(jnp.bitwise_and(lax.axis_index("batch"), bit) > 0, 1, 0)
        return self.split(side), "batch", bit


def side_by_side(items):
    items = [item.whole() for item in items]
    return Sum(jnp.concatenate(items, 0))


def doubled(total, got, bit):
    upper = jnp.bitwise_and(lax.axis_index("batch"), bit) > 0
    return jnp.concatenate([jnp.where(upper, got, total), jnp.where(upper, total, got)], 1)


def gathered(total):
    blocks, rows, columns = total.shape
    whole = lax.all_gather(total.reshape(blocks * rows, columns), "batch", axis=0)
    return whole.reshape(-1, blocks, rows, columns)


def in_place(whole):
    count, blocks, rows, columns = whole.shape
    width = count.bit_length() - 1
    whole = whole.reshape((2,) * width + (blocks, rows, columns))
    order = (width,) + tuple(reversed(range(width))) + (width + 1, width + 2)
    return whole.transpose(order).reshape(blocks, -1, columns)


def on_device(
    tokens,
    memory,
    mem_pos,
    seg_count,
    w_qkv,
    w_out,
    w_up,
    w_down,
    gain_attn,
    gain_mlp,
    w_mu,
    w_sig,
    cotangent,
):
    rows = tokens.shape[0]
    hidden_units = w_up.shape[2]
    count = lax.axis_size("blk")
    length = seg_count[0] * rows
    own = lax.axis_index("blk")
    own_list = own.astype(jnp.int32).reshape(1)
    own_places = own * rows + jnp.arange(rows, dtype=jnp.int32)
    all_places = jnp.concatenate(
        [jnp.bitwise_xor(own, k) * rows + jnp.arange(rows, dtype=jnp.int32) for k in range(count)]
    )
    allowed = (all_places[:, None] <= own_places[None, :]) & (all_places[:, None] < length)
    bias = jnp.where(allowed, 0.0, -1e30).astype(f32)
    lives = (own < seg_count[0]).astype(jnp.int32).reshape(1)
    hidden, normed, grad, grad_low = start(lives, tokens, gain_attn[0:1], cotangent)
    places = jnp.concatenate(relative_gather(mem_pos, "blk"), 1)
    places, sample, normed = lax.optimization_barrier((places, memory[0], normed))
    bits = bits_of("blk")
    far = [gather_steps({0: value}, "blk", bits[1:]) for value in (sample, normed)]
    inverse = ridge_inverse(places)
    inverse, far, grad_low, bias = lax.optimization_barrier((inverse, far, grad_low, bias))
    samples, parts = [gather_steps(held, "blk", bits[:1]) for held in far]
    samples = jnp.concatenate([samples[k] for k in range(count)], 0)
    parts = [parts[k] for k in range(count)]
    coeff_low = ridge_coeffs(places, samples, inverse)
    coeff_low, grad_low = lax.optimization_barrier((coeff_low, grad_low))
    grad_parts = relative_gather(grad_low, "blk")
    saved = []
    for layer in range(LAYERS):
        final = layer == LAYERS - 1
        maps = jnp.concatenate(
            [w_mu[layer][None], w_sig[layer][None], jnp.zeros((6, NBASIS), f32)], 0
        )
        attended, lse, query, kv, memory_kv = attend(layer, parts, bias, coeff_low, maps, w_qkv)
        if layer == 0:
            grad_parts, attended = lax.optimization_barrier((grad_parts, attended))
        else:
            before, attended = lax.optimization_barrier((saved[layer - 1][-1], attended))
            saved[layer - 1] = saved[layer - 1][:-1] + (before,)
        after = min(layer + 1, LAYERS - 1)
        middle, normed2, upward, after_block, low, *shards = mlp(
            layer,
            final,
            count,
            own_list,
            attended,
            hidden,
            gain_mlp[layer : layer + 1],
            gain_attn[after : after + 1],
            w_out,
            w_up,
            w_down,
        )
        saved.append((hidden, parts, query, kv, memory_kv, maps, lse))
        saved[layer] += (attended, middle, normed2, upward)
        hidden = after_block
        if not final:
            parts = relative_gather(low, "blk")
            parts, shards = lax.optimization_barrier((parts, shards))
        shards = [shards[0]] + [swap(shards[k], "blk", k) for k in range(1, count)]
        saved[layer] += (shards,)
    mixed = low
    small = [None] * LAYERS
    near, far = bits[0], bits[1:]
    first, *others = bits_of("batch")

    def chain(item, moves):
        for axis, bit in moves:
            move = item.over_blk(bit) if axis == "blk" else item.over_batch(bit)
            item.take(swap(*move))

    def back(layer, grad, grad_low, extra=()):
        layer_input, parts, query, kv, memory_kv, maps, lse = saved[layer][:7]
        attended, middle, normed2, upward, shards = saved[layer][7:]
        inputs = (layer, count, own_list, grad, grad_low, upward, normed2, middle)
        inputs += (gain_mlp[layer : layer + 1], attended, w_out, w_up, w_down)
        return mlp_back(*inputs, extra)

    def attention(layer, d_attended, extra):
        layer_input, parts, query, kv, memory_kv, maps, lse = saved[layer][:7]
        outs = attend_back(bias, query, kv, memory_kv, maps, lse, d_attended, extra)
        return outs[:5], outs[5]

    layer = LAYERS - 1
    parts, shards = saved[layer][1], saved[layer][-1]
    sent, kept, grad, grad_low, d_attended, d_gain_mlp = back(layer, grad, grad_low)
    up1 = Sum(kept)
    (sent,) = gate([sent], shards[1:])
    up1.take(swap(sent, "blk", near))
    down = down_grad(shards, grad_parts)
    down1 = Sum(down.reshape(-1, D // count, D))
    moves = [("blk", bit) for bit in far]
    operand = up1.over_blk(far[0])
    derivatives, d_maps1 = attention(layer, d_attended, [operand[0], down])
    up1.take(swap(*operand))
    chain(up1, moves[1:])
    terms = input_terms(layer, count, *derivatives[:3], w_qkv)
    terms = scatter_step(dict(enumerate(terms)), "blk", near)
    numbers = [k for k in terms if k]
    terms.update(zip(numbers, gate([terms[k] for k in numbers], up1.newest())))
    extra = [terms[k] for k in terms if k] + up1.newest()
    for bit in far:
        terms = scatter_step(terms, "blk", bit)
    mlp1 = side_by_side([up1, down1])
    operand_y1 = mlp1.over_batch(first)
    sent, kept = attention_grads(own_list, parts, coeff_low, derivatives, extra)
    last1 = Sum(kept)
    last1.take(swap(sent, "blk", near))
    grad, grad_low, d_gain_attn = norm_back(
        saved[layer][0], gain_attn[layer : layer + 1], terms[0], grad
    )
    gains = jnp.concatenate([d_gain_attn, d_gain_mlp], 0)
    small[layer] = jnp.concatenate([gains, d_maps1[:2]], 1)

    layer = 0
    parts, shards = saved[layer][1], saved[layer][-1]
    operand = last1.over_blk(far[0])
    grad_first = grad_low
    sent, kept, grad, grad_low, d_attended, d_gain_mlp = back(
        layer, grad, grad_low, [operand[0], operand_y1[0]]
    )
    mlp1.take(swap(*operand_y1))
    last1.take(swap(*operand))
    chain(last1, moves[1:])
    grad_parts = gather_steps({0: grad_first}, "blk", far)
    (sent,) = gate(
        [sent], last1.newest() + mlp1.newest() + [grad_parts[k] for k in grad_parts if k]
    )
    up0 = Sum(kept)
    up0.take(swap(sent, "blk", near))
    operand = up0.over_blk(far[0])
    operand_y = last1.over_batch(first)
    operand_z1 = mlp1.over_batch(others[0])
    values = gate([operand_y[0], operand_z1[0]], up0.newest())
    operand_y = (values[0],) + operand_y[1:]
    operand_z1 = (values[1],) + operand_z1[1:]
    derivatives, d_maps0 = attention(
        layer, d_attended, [operand[0], operand_y[0], operand_z1[0]]
    )
    mlp1.take(swap(*operand_z1))
    up0.take(swap(*operand))
    chain(up0, moves[1:])
    last1.take(swap(*operand_y))
    grad_parts = gather_steps(grad_parts, "blk", [near])
    grad_parts = [grad_parts[k] for k in range(count)]
    operand_z1 = mlp1.over_batch(others[1])
    down = down_grad(shards, grad_parts, [operand_z1[0], d_maps0] + last1.newest())
    mlp1.take(swap(*operand_z1))
    down0 = Sum(down.reshape(-1, D // count, D))
    sent, kept = attention_grads(own_list, parts, coeff_low, derivatives, [down])
    (sent,) = gate([sent], mlp1.newest())
    last0 = Sum(kept)
    last0.take(swap(sent, "blk", near))
    mlp0 = side_by_side([up0, down0])
    chain(mlp1, [("batch", bit) for bit in others[2:]])
    early = mlp1.whole()
    *more, second, third, fourth = reversed(bits_of("batch"))
    for bit in more:
        early = doubled(early, swap(early, "batch", bit), bit)
    operand = last0.over_blk(far[0])
    operand_y = mlp0.over_batch(first)
    operand_z = last1.over_batch(others[0])
    values = gate([operand_y[0], operand_z[0], early], last0.newest())
    operand_y = (values[0],) + operand_y[1:]
    operand_z = (values[1],) + operand_z[1:]
    early = values[2]
    last1.take(swap(*operand_z))
    terms = input_terms(layer, count, *derivatives[:3], w_qkv, [operand[0], operand_y[0], early])
    last0.take(swap(*operand))
    chain(last0, moves[1:])
    mlp0.take(swap(*operand_y))
    got = swap(early, "batch", second)
    chain(last1, [("batch", bit) for bit in others[1:]])
    terms = scatter_step(dict(enumerate(terms)), "blk", near)
    numbers = [k for k in terms if k]
    terms.update(zip(numbers, gate([terms[k] for k in numbers], last0.newest() + mlp0.newest())))
    operand = last0.over_batch(first)
    early = doubled(early, got, second)
    got = swap(early, "batch", third)
    for bit in far:
        terms = scatter_step(terms, "blk", bit)
    last0.take(swap(*operand))
    operand_z = mlp0.over_batch(others[0])
    grad, grad_low, d_gain_attn = norm_back(
        saved[layer][0],
        gain_attn[layer : layer + 1],
        terms[0],
        grad,
        [operand[0], operand_z[0], got],
    )
    early = doubled(early, got, third)
    mlp0.take(swap(*operand_z))
    operand = last0.over_batch(others[0])
    operand = tuple(gate([operand[0]], [d_gain_attn])) + operand[1:]
    last0.take(swap(*operand))
    gains = jnp.concatenate([d_gain_attn, d_gain_mlp], 0)
    small[layer] = jnp.concatenate([gains, d_maps0[:2]], 1)
    packed = jnp.concatenate(small, 0)
    for bit in bits:
        packed = packed + swap(packed, "blk", bit)
    for item in (mlp0, last0):
        chain(item, [("batch", bit) for bit in others[1:]])
    got = swap(early, "batch", fourth)
    rest = [last1.whole(), mlp0.whole(), last0.whole()]
    rows_each = rest[0].shape[1]
    values = packed.astype(bf16).reshape(-1)
    pieces = -(-values.shape[0] // (rows_each * D))
    values = jnp.pad(values, (0, pieces * rows_each * D - values.shape[0]))
    rest.append(values.reshape(pieces, rows_each, D))
    (rest,) = gate([jnp.concatenate(rest, 0)], [got])
    mlp1 = doubled(early, got, fourth)
    rest = gathered(rest)
    packed = jnp.sum(rest[:, -pieces:].astype(f32), 0).reshape(-1)[: packed.size]
    rest = in_place(rest)[:-pieces]
    last1, mlp0, last0 = rest[:3], rest[3:-3], rest[-3:]
    packed = packed.reshape(LAYERS, 2, D + NBASIS)

    def share_of(value):
        share = value.shape[1] // count
        return lax.dynamic_slice_in_dim(value, own * share, share, 1)

    shares = [share_of(packed[:, i, at]) for at in (slice(0, D), slice(D, None)) for i in (0, 1)]


    def columns(blocks):
        return jnp.concatenate([blocks[i] for i in range(blocks.shape[0])], 1)

    def both(low, high):
        return jnp.stack([low, high]).astype(f32)

    return (
        mixed,
        grad,
        both(columns(last0), columns(last1)),
        both(mlp0[CHUNKS], mlp1[CHUNKS]),
        both(columns(mlp0[:CHUNKS]), columns(mlp1[:CHUNKS])),
        both(mlp0[CHUNKS + 1 :].reshape(-1, D), mlp1[CHUNKS + 1 :].reshape(-1, D)),
        *shares,
    )


def solution(mesh):
    placed = (
        P(("batch", "blk"), None),
        P("batch", "blk", None),
        P("batch", "blk"),
        P("batch"),
        P(),
        P(),
        P(),
        P(),
        P(),
        P(),
        P(),
        P(),
        P(("batch", "blk"), None),
    )
    return jax.shard_map(
        on_device,
        mesh=mesh,
        in_specs=placed,
        out_specs=(
            P(("batch", "blk"), None),
            P(("batch", "blk"), None),
            P(None, "blk", None),
            P(None, "blk", None),
            P(None, "blk", None),
            P(None, "blk", None),
            P(None, "blk"),
            P(None, "blk"),
            P(None, "blk"),
            P(None, "blk"),
        ),
        check_vma=False,
    )
```

```python
import functools

import jax
import jax.numpy as jnp
from jax import lax
from jax.experimental import pallas as pl
from jax.experimental.pallas import tpu as pltpu
from jax.sharding import PartitionSpec as P

HEADS = 12
HEAD = 64
D = 768
NBASIS = 256
LAYERS = 2
MEMPOS = 4096
PAIRS = HEADS // 2
PAIR = 2 * HEAD

COST_SCALE = 5e8
highest = lax.Precision.HIGHEST
ridge_weight = 0.5
bf16 = jnp.bfloat16
f32 = jnp.float32

NT = (((1,), (1,)), ((), ()))
TN = (((0,), (0,)), ((), ()))
VMEM = pl.BlockSpec(memory_space=pltpu.VMEM)


ANY = pl.BlockSpec(memory_space=pl.ANY)
LIMIT = 58 * 1024 * 1024
CHUNKS = 4


def cost(microseconds):
    return pl.CostEstimate(
        flops=int(microseconds * COST_SCALE), bytes_accessed=0, transcendentals=0
    )


def gauss_jordan(panel, first):
    count, width = panel.shape
    lane = lax.broadcasted_iota(jnp.int32, (1, width), 1)
    line = lax.broadcasted_iota(jnp.int32, (count, 1), 0)

    def spread(value, column):
        return jnp.broadcast_to(value[:, column : column + 1], value.shape)

    for p in range(0, count, 2):
        c = first + p
        row0, row1 = panel[p : p + 1, :], panel[p + 1 : p + 2, :]
        a, b = spread(row0, c), spread(row0, c + 1)
        e, d = spread(row1, c), spread(row1, c + 1)
        over = 1.0 / (a * d - b * e)
        clear0 = jnp.where(lane == c, 1.0, jnp.where(lane == c + 1, 0.0, row0))
        clear1 = jnp.where(lane == c, 0.0, jnp.where(lane == c + 1, 1.0, row1))
        new0 = (d * clear0 - b * clear1) * over
        new1 = (a * clear1 - e * clear0) * over
        factor0, factor1 = spread(panel, c), spread(panel, c + 1)
        rest = jnp.where((lane == c) | (lane == c + 1), 0.0, panel)
        rest = rest - factor0 * new0 - factor1 * new1
        panel = jnp.where(line == p, new0, jnp.where(line == p + 1, new1, rest))
    return panel


def basis_of(places):
    times = (places.astype(f32) + 0.5) / MEMPOS
    centres = (lax.broadcasted_iota(jnp.int32, (NBASIS, 1), 0).astype(f32) + 0.5) / NBASIS
    breadth = 1.0 / NBASIS
    offset = times - centres
    return jnp.exp(-offset * offset / (2.0 * breadth * breadth))


def gram_of(basis):
    line = lax.broadcasted_iota(jnp.int32, (NBASIS, NBASIS), 0)
    lane = lax.broadcasted_iota(jnp.int32, (NBASIS, NBASIS), 1)
    gram = lax.dot_general(basis, basis, NT, precision=highest, preferred_element_type=f32)
    return gram + jnp.where(line == lane, ridge_weight, 0.0)


def inverse_kernel(places_ref, inverse_ref):
    lane = lax.broadcasted_iota(jnp.int32, (NBASIS, NBASIS), 1)
    inverse_ref[...] = gram_of(basis_of(places_ref[...]))
    step = 32
    for first in range(0, NBASIS, step):
        panel = gauss_jordan(inverse_ref[first : first + step, :], first)
        columns = inverse_ref[...][:, first : first + step]
        inside = (lane >= first) & (lane < first + step)
        product = jnp.dot(columns, panel, precision=highest, preferred_element_type=f32)
        inverse_ref[...] = jnp.where(inside, 0.0, inverse_ref[...]) - product
        inverse_ref[first : first + step, :] = panel


def coeff_kernel(places_ref, samples_ref, inverse_ref, coeff_ref):
    def product(a, b):
        return jnp.dot(a, b, precision=highest, preferred_element_type=f32)

    basis = basis_of(places_ref[...])
    right = product(basis, samples_ref[...].astype(f32))
    coeffs = product(inverse_ref[...], right)
    coeffs += product(inverse_ref[...], right - product(gram_of(basis), coeffs))
    coeff_ref[...] = coeffs.astype(bf16)


def ridge_inverse(places):
    return pl.pallas_call(
        inverse_kernel,
        out_shape=jax.ShapeDtypeStruct((NBASIS, NBASIS), f32),
        in_specs=[VMEM],
        out_specs=VMEM,
        compiler_params=pltpu.CompilerParams(vmem_limit_bytes=40 * 1024 * 1024),
        cost_estimate=cost(16.6),
        name="ridge_inverse",
    )(places)


def ridge_coeffs(places, samples, inverse):
    return pl.pallas_call(
        coeff_kernel,
        out_shape=jax.ShapeDtypeStruct((NBASIS, D), bf16),
        in_specs=[VMEM] * 3,
        out_specs=VMEM,
        compiler_params=pltpu.CompilerParams(vmem_limit_bytes=40 * 1024 * 1024),
        cost_estimate=cost(4.4),
        name="ridge_coeffs",
    )(places, samples, inverse)


def expand_maps(maps, mem_keys):
    vectors = jnp.dot(maps, mem_keys.astype(f32), precision=highest, preferred_element_type=f32)
    row = lax.broadcasted_iota(jnp.int32, (8 * PAIRS, D), 0)
    which = row % 8
    lane_head = lax.broadcasted_iota(jnp.int32, (8 * PAIRS, D), 1) // HEAD
    owned = (which < 4) & (lane_head == 2 * (row // 8) + which // 2)
    both = jnp.where(which % 2 == 0, vectors[0:1, :], vectors[1:2, :])
    return jnp.where(owned, both, 0.0)


def memory_weights(logits):
    breadth = 1.0 / NBASIS
    place = 1.0 / (1.0 + jnp.exp(-logits[0:1, :]))
    sigma = logits[1:2, :]
    soft = jnp.maximum(sigma, 0.0) + jnp.log(1.0 + jnp.exp(-jnp.abs(sigma)))
    variance = (0.5 + soft) / 64.0
    centres = (lax.broadcasted_iota(jnp.int32, (NBASIS, 1), 0).astype(f32) + 0.5) / NBASIS
    offset = place - centres
    weights = (breadth * lax.rsqrt(variance)) * jnp.exp(offset * offset * (-0.5 / variance))
    return weights, place, variance, offset


def head_lanes(value, which):
    lane = lax.broadcasted_iota(jnp.int32, value.shape, 1)
    return jnp.where((lane < HEAD) == (which == 0), value, jnp.zeros_like(value))


def pair_block(rows, shift=0):
    return pl.BlockSpec((rows, PAIR), lambda p: (0, p + shift))


def whole_block(shape):
    return pl.BlockSpec(shape, lambda p: (0,) * len(shape))


def attend_back_kernel(
    bias, query_all, mem_keys_all, maps, lse, q, k, v, mv, da,
    dq, dk, dv, dmk, dmv, dmaps, logits, lines, dq_t,
):
    pair = pl.program_id(0)
    scale = HEAD**-0.5

    @pl.when(pair == 0)
    def _():
        table = expand_maps(maps[...], mem_keys_all[...])
        wide = query_all[...].astype(f32) * scale
        logits[...] = lax.dot_general(
            table, wide, NT, precision=highest, preferred_element_type=f32
        )

    rows8 = logits[pl.ds(pl.multiple_of(pair * 8, 8), 8), :]
    k_t = k[...].T
    halves = []
    derived = []
    d_keys = d_values = d_mem_values = None
    for s in range(2):
        qh = head_lanes(q[...], s) * jnp.asarray(scale, bf16)
        dh = head_lanes(da[...], s)
        scores = lax.dot_general(k[...], qh, NT, preferred_element_type=f32) + bias[...]
        probs = jnp.exp(scores - lse[0, s : s + 1, :])
        d_probs = lax.dot_general(v[...], dh, NT, preferred_element_type=f32)
        correction = jnp.sum(probs * d_probs, axis=0, keepdims=True)
        d_scores = (probs * (d_probs - correction)).astype(bf16)
        key_term = jnp.dot(d_scores, qh, preferred_element_type=f32)
        value_term = jnp.dot(probs.astype(bf16), dh, preferred_element_type=f32)
        query_term = jnp.dot(k_t, d_scores, preferred_element_type=f32) * scale
        weights, place, variance, offset = memory_weights(rows8[2 * s : 2 * s + 2, :])
        d_weights = lax.dot_general(mv[...], dh, NT, preferred_element_type=f32)
        mem_term = jnp.dot(weights.astype(bf16), dh, preferred_element_type=f32)
        moved = d_weights * weights
        sum0 = jnp.sum(moved, axis=0, keepdims=True)
        moved = moved * offset
        sum1 = jnp.sum(moved, axis=0, keepdims=True)
        sum2 = jnp.sum(moved * offset, axis=0, keepdims=True)
        d_place = -sum1 / variance
        d_variance = (sum2 / variance - sum0) * (0.5 / variance)
        derived.append(d_place * place * (1.0 - place))
        sigma = rows8[2 * s + 1 : 2 * s + 2, :]
        derived.append(d_variance * (1.0 / 64.0) / (1.0 + jnp.exp(-sigma)))
        halves.append(query_term[s * HEAD : (s + 1) * HEAD, :])
        d_keys = key_term if s == 0 else d_keys + key_term
        d_values = value_term if s == 0 else d_values + value_term
        d_mem_values = mem_term if s == 0 else d_mem_values + mem_term
    dk[...] = d_keys.astype(bf16)
    dv[...] = d_values.astype(bf16)
    dmv[...] = d_mem_values.astype(bf16)
    dq_t[pair] = jnp.concatenate(halves, 0).T
    lines[pl.ds(pl.multiple_of(pair * 8, 8), 8), :] = jnp.concatenate(
        derived + [jnp.zeros((4, derived[0].shape[1]), f32)], 0
    )

    @pl.when(pair == PAIRS - 1)
    def _():
        table = expand_maps(maps[...], mem_keys_all[...])
        low = lines[...].astype(bf16)
        back = lax.dot_general(low, table.astype(bf16), TN, preferred_element_type=f32) * scale
        for p in range(PAIRS):
            at = slice(p * PAIR, (p + 1) * PAIR)
            dq[:, at] = (dq_t[p] + back[:, at]).astype(bf16)
        sums = jnp.dot(low, query_all[...], preferred_element_type=f32) * scale
        row = lax.broadcasted_iota(jnp.int32, sums.shape, 0)
        which = row % 8
        lane_head = lax.broadcasted_iota(jnp.int32, sums.shape, 1) // HEAD
        owned = (which < 4) & (lane_head == 2 * (row // 8) + which // 2)
        sums = jnp.where(owned, sums, 0.0)
        even = jnp.sum(jnp.where(which % 2 == 0, sums, 0.0), axis=0, keepdims=True)
        odd = jnp.sum(jnp.where(which % 2 == 1, sums, 0.0), axis=0, keepdims=True)
        both = jnp.concatenate([even, odd, jnp.zeros((6, D), f32)], 0).astype(bf16)
        dmk[...] = lax.dot_general(
            maps[...].astype(bf16), both, TN, preferred_element_type=f32
        ).astype(bf16)
        dmaps[...] = lax.dot_general(both, mem_keys_all[...], NT, preferred_element_type=f32)


def attend_back(bias, query, kv, memory_kv, maps, lse, d_attended, extra=()):
    rows = query.shape[0]
    seq = kv.shape[0]
    return pl.pallas_call(
        after(attend_back_kernel, 10, extra),
        grid=(PAIRS,),
        in_specs=[
            whole_block((seq, rows)),
            whole_block((rows, D)),
            whole_block((NBASIS, D)),
            whole_block((8, NBASIS)),
            pl.BlockSpec((1, 8, rows), lambda p: (p, 0, 0)),
            pair_block(rows),
            pair_block(seq),
            pair_block(seq, PAIRS),
            pair_block(NBASIS, PAIRS),
            pair_block(rows),
        ]
        + [ANY] * len(extra),
        out_specs=[
            whole_block((rows, D)),
            pair_block(seq),
            pair_block(seq),
            whole_block((NBASIS, D)),
            pair_block(NBASIS),
            whole_block((8, NBASIS)),
        ],
        out_shape=[
            jax.ShapeDtypeStruct((rows, D), bf16),
            jax.ShapeDtypeStruct((seq, D), bf16),
            jax.ShapeDtypeStruct((seq, D), bf16),
            jax.ShapeDtypeStruct((NBASIS, D), bf16),
            jax.ShapeDtypeStruct((NBASIS, D), bf16),
            jax.ShapeDtypeStruct((8, NBASIS), f32),
        ],
        scratch_shapes=[
            pltpu.VMEM((8 * PAIRS, rows), f32),
            pltpu.VMEM((8 * PAIRS, rows), f32),
            pltpu.VMEM((PAIRS, rows, PAIR), f32),
        ],
        compiler_params=pltpu.CompilerParams(vmem_limit_bytes=56 * 1024 * 1024),
        cost_estimate=cost(18.3),
        name="attend_back",
    )(bias, query, memory_kv, maps, lse, query, kv, kv, memory_kv, d_attended, *extra)


def call_options(name, microseconds):
    return dict(
        compiler_params=pltpu.CompilerParams(vmem_limit_bytes=LIMIT),
        cost_estimate=cost(microseconds),
        name=name,
    )


def after(kernel, inputs, extra):
    def body(*refs):
        kernel(*refs[:inputs], *refs[inputs + len(extra) :])

    return body


def gate(values, extra):
    def kernel(*refs):
        del refs

    count = len(values)
    return pl.pallas_call(
        kernel,
        in_specs=[ANY] * (count + len(extra)),
        out_specs=[ANY] * count,
        out_shape=[jax.ShapeDtypeStruct(value.shape, value.dtype) for value in values],
        input_output_aliases={i: i for i in range(count)},
        **call_options("gate", 1.0),
    )(*values, *extra)


def dot_nt(a, b):
    return lax.dot_general(a, b, NT, preferred_element_type=f32)


def dot_tn(a, b):
    return lax.dot_general(a, b, TN, preferred_element_type=f32)


def normalise(value):
    centred = value - jnp.mean(value, axis=1, keepdims=True)
    spread = jnp.mean(centred * centred, axis=1, keepdims=True)
    factor = lax.rsqrt(spread + 1e-05)
    return centred * factor, factor


def norm_backward(value, gain, d_out):
    unit, factor = normalise(value)
    d_unit = d_out * gain
    mean0 = jnp.mean(d_unit, axis=1, keepdims=True)
    mean1 = jnp.mean(d_unit * unit, axis=1, keepdims=True)
    return factor * (d_unit - mean0 - unit * mean1), jnp.sum(d_out * unit, axis=0, keepdims=True)


def gelu_parts(upward):
    outer = 0.7978845608028654
    square = upward * upward
    inner = jnp.tanh(upward * (outer + outer * 0.044715 * square))
    half = 0.5 * (1.0 + inner)
    slope = half + 0.5 * upward * (1.0 - inner * inner) * (outer + 3.0 * outer * 0.044715 * square)
    return upward * half, slope


def store_shard(count, own, shard, rows, send, keep):
    size = rows.shape[0]
    width = count.bit_length() - 1
    relative = jnp.bitwise_xor(own, shard)
    place = 0
    for bit in range(width):
        place += jnp.bitwise_and(lax.shift_right_logical(relative, bit), 1) << (width - 1 - bit)

    @pl.when(place >= count // 2)
    def _():
        send[pl.ds(pl.multiple_of((place - count // 2) * size, 16), size), :] = rows

    @pl.when(place < count // 2)
    def _():
        keep[pl.ds(pl.multiple_of(place * size, 16), size), :] = rows


def store_shards(count, own, value, send, keep):
    size = value.shape[0] // count
    for shard in range(count):
        rows = value[shard * size : (shard + 1) * size, :].astype(bf16)
        store_shard(count, own, shard, rows, send, keep)


def attend_kernel(layer, count, *refs):
    parts = refs[:count]
    bias, coeff, maps, w_hbm = refs[count : count + 4]
    out, lse, query, kv, memory_kv = refs[count + 4 : count + 9]
    w, logits, sem = refs[count + 9 :]
    copy = pltpu.make_async_copy(w_hbm.at[layer], w, sem)
    copy.start()
    copy.wait()
    rows = query.shape[0]
    query[...] = jnp.dot(parts[0][...], w[:, :D], preferred_element_type=f32).astype(bf16)
    memory_kv[...] = jnp.dot(coeff[...], w[:, D:], preferred_element_type=f32).astype(bf16)
    for k in range(count):
        kv[k * rows : (k + 1) * rows, :] = jnp.dot(
            parts[k][...], w[:, D:], preferred_element_type=f32
        ).astype(bf16)
    table = expand_maps(maps[...], memory_kv[:, :D])
    wide = query[...].astype(f32) * HEAD**-0.5
    logits[...] = lax.dot_general(table, wide, NT, precision=highest, preferred_element_type=f32)

    def body(pair, carry):
        at = pl.ds(pl.multiple_of(pair * PAIR, PAIR), PAIR)
        value_at = pl.ds(pl.multiple_of(D + pair * PAIR, PAIR), PAIR)
        lines = logits[pl.ds(pl.multiple_of(pair * 8, 8), 8), :]
        q, k = query[:, at], kv[:, at]
        v_t = kv[:, value_at].T
        mv_t = memory_kv[:, value_at].T
        halves = []
        totals = []
        for s in range(2):
            qh = head_lanes(q, s) * jnp.asarray(HEAD**-0.5, bf16)
            scores = dot_nt(k, qh) + bias[...]
            peak = jnp.max(scores, axis=0, keepdims=True)
            expo = jnp.exp(scores - peak)
            total = jnp.sum(expo, axis=0, keepdims=True)
            local = jnp.dot(v_t, expo.astype(bf16), preferred_element_type=f32) * (1.0 / total)
            weights = memory_weights(lines[2 * s : 2 * s + 2, :])[0]
            recalled = jnp.dot(mv_t, weights.astype(bf16), preferred_element_type=f32)
            halves.append((local + recalled)[s * HEAD : (s + 1) * HEAD, :])
            totals.append(peak + jnp.log(total))
        out[:, at] = jnp.concatenate(halves, 0).T.astype(bf16)
        lse[pair, 0:1, :] = totals[0]
        lse[pair, 1:2, :] = totals[1]
        return carry

    lax.fori_loop(0, PAIRS, body, 0)


def attend(layer, parts, bias, coeff, maps, w_qkv):
    rows = parts[0].shape[0]
    seq = rows * len(parts)
    return pl.pallas_call(
        functools.partial(attend_kernel, layer, len(parts)),
        in_specs=[VMEM] * (len(parts) + 3) + [ANY],
        out_specs=[VMEM] * 5,
        out_shape=[
            jax.ShapeDtypeStruct((rows, D), bf16),
            jax.ShapeDtypeStruct((PAIRS, 8, rows), f32),
            jax.ShapeDtypeStruct((rows, D), bf16),
            jax.ShapeDtypeStruct((seq, 2 * D), bf16),
            jax.ShapeDtypeStruct((NBASIS, 2 * D), bf16),
        ],
        scratch_shapes=[
            pltpu.VMEM((D, 3 * D), bf16),
            pltpu.VMEM((8 * PAIRS, rows), f32),
            pltpu.SemaphoreType.DMA,
        ],
        **call_options("attend", 20.8),
    )(*parts, bias, coeff, maps, w_qkv)


def mlp_kernel(last, count, own, *refs):
    attended, hidden, gain, next_gain, w_out, w_up, w_down = refs[:7]
    middle, normed2, upward, hidden_out, low_out = refs[7:12]
    shards = refs[12:]
    step = pl.program_id(0)

    @pl.when(step == 0)
    def _():
        middle[...] = hidden[...] + jnp.dot(
            attended[...], w_out[0], preferred_element_type=f32
        )
        normed2[...] = (normalise(middle[...])[0] * gain[...]).astype(bf16)
        hidden_out[...] = middle[...]

    up = jnp.dot(normed2[...], w_up[0], preferred_element_type=f32)
    upward[...] = up
    active = gelu_parts(up)[0].astype(bf16)
    hidden_out[...] += jnp.dot(active, w_down[0], preferred_element_type=f32)
    pieces = max(1, count // CHUNKS)
    share = active.shape[1] // pieces
    for i in range(pieces):
        relative = jnp.bitwise_xor(own[0], step * pieces + i)
        for k in range(count):

            @pl.when(relative == k)
            def _(i=i, k=k):
                shards[k][...] = active[:, i * share : (i + 1) * share]

    @pl.when(step == CHUNKS - 1)
    def _():
        value = hidden_out[...]
        low_out[...] = (value if last else normalise(value)[0] * next_gain[...]).astype(bf16)


def mlp(layer, last, count, own, attended, hidden, gain, next_gain, w_out, w_up, w_down):
    rows = hidden.shape[0]
    hidden_units = w_up.shape[2]
    chunk = hidden_units // CHUNKS
    share = hidden_units // count
    assert count >= CHUNKS
    whole = pl.BlockSpec((rows, D), lambda j, own: (0, 0))
    line = pl.BlockSpec((1, D), lambda j, own: (0, 0))
    shard = pl.BlockSpec((rows, share), lambda j, own: (0, 0))
    return pl.pallas_call(
        functools.partial(mlp_kernel, last, count),
        grid_spec=pltpu.PrefetchScalarGridSpec(
            num_scalar_prefetch=1,
            grid=(CHUNKS,),
            in_specs=[
                whole,
                whole,
                line,
                line,
                pl.BlockSpec((1, D, D), lambda j, own: (layer, 0, 0)),
                pl.BlockSpec((1, D, chunk), lambda j, own: (layer, 0, j)),
                pl.BlockSpec((1, chunk, D), lambda j, own: (layer, j, 0)),
            ],
            out_specs=[
                whole,
                whole,
                pl.BlockSpec((rows, chunk), lambda j, own: (0, j)),
                whole,
                whole,
            ]
            + [shard] * count,
        ),
        out_shape=[
            jax.ShapeDtypeStruct((rows, D), f32),
            jax.ShapeDtypeStruct((rows, D), bf16),
            jax.ShapeDtypeStruct((rows, hidden_units), f32),
            jax.ShapeDtypeStruct((rows, D), f32),
            jax.ShapeDtypeStruct((rows, D), bf16),
        ]
        + [jax.ShapeDtypeStruct((rows, share), bf16)] * count,
        **call_options("mlp", 10.4),
    )(own, attended, hidden, gain, next_gain, w_out, w_up, w_down)


def mlp_back_kernel(
    shards, own, grad, grad_low, upward, normed2, middle, gain, attended, w_out, w_up, w_down,
    send, keep, grad_out, low_out, d_attended, d_gain, left, d_normed,
):
    step = pl.program_id(0)

    @pl.when(step == 0)
    def _():
        left[...] = normed2[...].T

    @pl.when(step < CHUNKS)
    def _():
        d_active = dot_nt(grad_low[...], w_down[0])
        d_up = (d_active * gelu_parts(upward[...])[1]).astype(bf16)
        term = dot_nt(d_up, w_up[0])

        @pl.when(step == 0)
        def _():
            d_normed[...] = term

        @pl.when(step > 0)
        def _():
            d_normed[...] += term

        value = jnp.dot(left[...], d_up, preferred_element_type=f32)
        store_shards(shards, own[0], value, send.at[0], keep.at[0])

    @pl.when(step == CHUNKS)
    def _():
        d_middle, d_line = norm_backward(middle[...], gain[...], d_normed[...])
        total = grad[...] + d_middle
        grad_out[...] = total
        low = total.astype(bf16)
        low_out[...] = low
        d_attended[...] = dot_nt(low, w_out[0]).astype(bf16)
        d_gain[...] = d_line
        store_shards(shards, own[0], dot_tn(attended[...], low), send.at[0], keep.at[0])


def mlp_back(
    layer,
    shards,
    own,
    grad,
    grad_low,
    upward,
    normed2,
    middle,
    gain,
    attended,
    w_out,
    w_up,
    w_down,
    extra=(),
):
    rows = grad.shape[0]
    chunk = w_up.shape[2] // CHUNKS
    last = CHUNKS - 1
    whole = pl.BlockSpec((rows, D), lambda j, own: (0, 0))
    line = pl.BlockSpec((1, D), lambda j, own: (0, 0))
    half = pl.BlockSpec((1, D // 2, chunk), lambda j, own: (j, 0, 0))
    shape = jax.ShapeDtypeStruct((CHUNKS + 1, D // 2, chunk), bf16)
    return pl.pallas_call(
        after(functools.partial(mlp_back_kernel, shards), 11, extra),
        grid_spec=pltpu.PrefetchScalarGridSpec(
            num_scalar_prefetch=1,
            grid=(CHUNKS + 1,),
            in_specs=[
                whole,
                whole,
                pl.BlockSpec((rows, chunk), lambda j, own: (0, jnp.minimum(j, last))),
                whole,
                whole,
                line,
                whole,
                pl.BlockSpec((1, D, D), lambda j, own: (layer, 0, 0)),
                pl.BlockSpec((1, D, chunk), lambda j, own: (layer, 0, jnp.minimum(j, last))),
                pl.BlockSpec((1, chunk, D), lambda j, own: (layer, jnp.minimum(j, last), 0)),
            ]
            + [ANY] * len(extra),
            out_specs=[half, half, whole, whole, whole, line],
            scratch_shapes=[pltpu.VMEM((D, rows), bf16), pltpu.VMEM((rows, D), f32)],
        ),
        out_shape=[
            shape,
            shape,
            jax.ShapeDtypeStruct((rows, D), f32),
            jax.ShapeDtypeStruct((rows, D), bf16),
            jax.ShapeDtypeStruct((rows, D), bf16),
            jax.ShapeDtypeStruct((1, D), f32),
        ],
        **call_options("mlp_back", 14.6),
    )(own, grad, grad_low, upward, normed2, middle, gain, attended, w_out, w_up, w_down, *extra)


def down_kernel(count, *refs):
    out = refs[-1]
    total = dot_tn(refs[0][...], refs[count][...])
    for k in range(1, count):
        total += dot_tn(refs[k][...], refs[count + k][...])
    out[...] = total.astype(bf16)


def down_grad(actives, grads, extra=()):
    count = len(actives)
    return pl.pallas_call(
        after(functools.partial(down_kernel, count), 2 * count, extra),
        in_specs=[VMEM] * (2 * count) + [ANY] * len(extra),
        out_specs=VMEM,
        out_shape=jax.ShapeDtypeStruct((actives[0].shape[1], D), bf16),
        **call_options("down_grad", 4.3),
    )(*actives, *grads, *extra)


def input_kernel(layer, d_query, d_keys, d_values, w_hbm, *refs):
    outs, (w, sem) = refs[:-2], refs[-2:]
    copy = pltpu.make_async_copy(w_hbm.at[layer], w, sem)
    copy.start()
    copy.wait()
    rows = d_query.shape[0]
    total = dot_nt(d_keys[...], w[:, D : 2 * D]) + dot_nt(d_values[...], w[:, 2 * D :])
    outs[0][...] = (total[:rows, :] + dot_nt(d_query[...], w[:, :D])).astype(bf16)
    for k in range(1, len(outs)):
        outs[k][...] = total[k * rows : (k + 1) * rows, :].astype(bf16)


def input_terms(layer, count, d_query, d_keys, d_values, w_qkv, extra=()):
    return pl.pallas_call(
        after(functools.partial(input_kernel, layer), 4, extra),
        in_specs=[VMEM] * 3 + [ANY] + [ANY] * len(extra),
        out_specs=[VMEM] * count,
        out_shape=[jax.ShapeDtypeStruct(d_query.shape, bf16)] * count,
        scratch_shapes=[pltpu.VMEM((D, 3 * D), bf16), pltpu.SemaphoreType.DMA],
        **call_options("input_terms", 7.6),
    )(d_query, d_keys, d_values, w_qkv, *extra)


def attention_grad_kernel(count, own, *refs):
    parts = refs[:count]
    coeff, d_query, d_keys, d_values, d_mem_keys, d_mem_values, send, keep, left = refs[count:]
    rows = d_query.shape[0]
    seq = rows * count
    size = D // count
    for k in range(count):
        left[:, k * rows : (k + 1) * rows] = parts[k][...].T
    left[:, seq:] = coeff[...].T

    def product(a, b):
        return jnp.dot(a, b[...], preferred_element_type=f32)

    for shard in range(count):
        line = left[shard * size : (shard + 1) * size, :]
        own_line, all_line, mem_line = line[:, :rows], line[:, :seq], line[:, seq:]
        values = (
            product(own_line, d_query),
            product(all_line, d_keys) + product(mem_line, d_mem_keys),
            product(all_line, d_values) + product(mem_line, d_mem_values),
        )
        for i, value in enumerate(values):
            store_shard(count, own[0], shard, value.astype(bf16), send.at[i], keep.at[i])


def attention_grads(own, parts, coeff, derivatives, extra=()):
    smem = pl.BlockSpec(memory_space=pltpu.SMEM)
    shape = jax.ShapeDtypeStruct((3, D // 2, D), bf16)
    inputs = (*parts, coeff, *derivatives)
    return pl.pallas_call(
        after(functools.partial(attention_grad_kernel, len(parts)), 1 + len(inputs), extra),
        in_specs=[smem] + [VMEM] * len(inputs) + [ANY] * len(extra),
        out_specs=[VMEM, VMEM],
        out_shape=[shape, shape],
        scratch_shapes=[pltpu.VMEM((D, parts[0].shape[0] * len(parts) + NBASIS), bf16)],
        **call_options("attention_grads", 9.6),
    )(own, *inputs, *extra)


def norm_back_kernel(value, gain, d_out, grad, grad_out, low_out, d_gain):
    d_value, d_line = norm_backward(value[...], gain[...], d_out[...].astype(f32))
    total = grad[...] + d_value
    grad_out[...] = total
    low_out[...] = total.astype(bf16)
    d_gain[...] = d_line


def norm_back(value, gain, d_out, grad, extra=()):
    return pl.pallas_call(
        after(norm_back_kernel, 4, extra),
        in_specs=[VMEM] * 4 + [ANY] * len(extra),
        out_specs=[VMEM] * 3,
        out_shape=[
            jax.ShapeDtypeStruct(grad.shape, f32),
            jax.ShapeDtypeStruct(grad.shape, bf16),
            jax.ShapeDtypeStruct((1, D), f32),
        ],
        **call_options("norm_back", 3.1),
    )(value, gain, d_out, grad, *extra)


def start_kernel(live, tokens, gain, cotangent, hidden, normed, grad, grad_low):
    wide = tokens[...].astype(f32)
    hidden[...] = wide
    normed[...] = (normalise(wide)[0] * gain[...]).astype(bf16)
    masked = cotangent[...].astype(f32) * live[0].astype(f32)
    grad[...] = masked
    grad_low[...] = masked.astype(bf16)


def start(live, tokens, gain, cotangent):
    return pl.pallas_call(
        start_kernel,
        in_specs=[pl.BlockSpec(memory_space=pltpu.SMEM)] + [VMEM] * 3,
        out_specs=[VMEM] * 4,
        out_shape=[jax.ShapeDtypeStruct(tokens.shape, kind) for kind in (f32, bf16, f32, bf16)],
        **call_options("start", 2.5),
    )(live, tokens, gain, cotangent)


def swap(value, axis, bit):
    count = lax.axis_size(axis)
    return lax.ppermute(value, axis, [(i, i ^ bit) for i in range(count)])


def bits_of(axis):
    return [1 << i for i in range(lax.axis_size(axis).bit_length() - 1)]


def gather_steps(held, axis, bits):
    held = dict(held)
    for bit in reversed(bits):
        held.update({k | bit: swap(v, axis, bit) for k, v in list(held.items())})
    return held


def relative_gather(value, axis):
    held = gather_steps({0: value}, axis, bits_of(axis))
    return [held[k] for k in range(lax.axis_size(axis))]


def scatter_step(held, axis, bit):
    sent = {k: swap(v, axis, bit) for k, v in held.items() if k & bit}
    return {
        k: (v.astype(f32) + sent[k | bit].astype(f32)).astype(bf16)
        for k, v in held.items()
        if not k & bit
    }


class Sum:
    def __init__(self, *terms):
        self.terms = [(term, 0) for term in terms]
        self.rows = terms[0].shape[1]

    def added(self, terms):
        parts = [
            value
            if value.shape[1] == self.rows
            else lax.dynamic_slice_in_dim(value, at, self.rows, 1)
            for value, at in terms
        ]
        if len(parts) == 1:
            return parts[0]
        return sum(part.astype(f32) for part in parts).astype(bf16)

    def whole(self):
        return self.added(self.terms)

    def blocks(self):
        return self.terms[0][0].shape[0]

    def newest(self):
        return [self.terms[-1][0]]

    def split(self, side):
        self.rows = self.rows // 2
        sent = [(value, at + (1 - side) * self.rows) for value, at in self.terms]
        sent = self.added(sent)
        self.terms = [(value, at + side * self.rows) for value, at in self.terms]
        return sent

    def take(self, got):
        self.terms.append((got, 0))

    def over_blk(self, bit):
        return self.split(0), "blk", bit

    def over_batch(self, bit):
        side = jnp.where(jnp.bitwise_and(lax.axis_index("batch"), bit) > 0, 1, 0)
        return self.split(side), "batch", bit


def side_by_side(items):
    items = [item.whole() for item in items]
    return Sum(jnp.concatenate(items, 0))


def doubled(total, got, bit):
    upper = jnp.bitwise_and(lax.axis_index("batch"), bit) > 0
    return jnp.concatenate([jnp.where(upper, got, total), jnp.where(upper, total, got)], 1)


def gathered(total):
    blocks, rows, columns = total.shape
    whole = lax.all_gather(total.reshape(blocks * rows, columns), "batch", axis=0)
    return whole.reshape(-1, blocks, rows, columns)


def in_place(whole):
    count, blocks, rows, columns = whole.shape
    width = count.bit_length() - 1
    whole = whole.reshape((2,) * width + (blocks, rows, columns))
    order = (width,) + tuple(reversed(range(width))) + (width + 1, width + 2)
    return whole.transpose(order).reshape(blocks, -1, columns)


def on_device(
    tokens,
    memory,
    mem_pos,
    seg_count,
    w_qkv,
    w_out,
    w_up,
    w_down,
    gain_attn,
    gain_mlp,
    w_mu,
    w_sig,
    cotangent,
):
    rows = tokens.shape[0]
    hidden_units = w_up.shape[2]
    count = lax.axis_size("blk")
    length = seg_count[0] * rows
    own = lax.axis_index("blk")
    own_list = own.astype(jnp.int32).reshape(1)
    own_places = own * rows + jnp.arange(rows, dtype=jnp.int32)
    all_places = jnp.concatenate(
        [jnp.bitwise_xor(own, k) * rows + jnp.arange(rows, dtype=jnp.int32) for k in range(count)]
    )
    allowed = (all_places[:, None] <= own_places[None, :]) & (all_places[:, None] < length)
    bias = jnp.where(allowed, 0.0, -1e30).astype(f32)
    lives = (own < seg_count[0]).astype(jnp.int32).reshape(1)
    hidden, normed, grad, grad_low = start(lives, tokens, gain_attn[0:1], cotangent)
    places = jnp.concatenate(relative_gather(mem_pos, "blk"), 1)
    places, sample, normed = lax.optimization_barrier((places, memory[0], normed))
    bits = bits_of("blk")
    far = [gather_steps({0: value}, "blk", bits[1:]) for value in (sample, normed)]
    inverse = ridge_inverse(places)
    inverse, far, grad_low, bias = lax.optimization_barrier((inverse, far, grad_low, bias))
    samples, parts = [gather_steps(held, "blk", bits[:1]) for held in far]
    samples = jnp.concatenate([samples[k] for k in range(count)], 0)
    parts = [parts[k] for k in range(count)]
    coeff_low = ridge_coeffs(places, samples, inverse)
    coeff_low, grad_low = lax.optimization_barrier((coeff_low, grad_low))
    grad_parts = [grad_low] + [swap(grad_low, "blk", k) for k in range(1, count)]
    saved = []
    for layer in range(LAYERS):
        final = layer == LAYERS - 1
        maps = jnp.concatenate(
            [w_mu[layer][None], w_sig[layer][None], jnp.zeros((6, NBASIS), f32)], 0
        )
        attended, lse, query, kv, memory_kv = attend(layer, parts, bias, coeff_low, maps, w_qkv)
        if layer == 0:
            grad_parts, attended = lax.optimization_barrier((grad_parts, attended))
        else:
            before, attended = lax.optimization_barrier((saved[layer - 1][-1], attended))
            saved[layer - 1] = saved[layer - 1][:-1] + (before,)
        after = min(layer + 1, LAYERS - 1)
        middle, normed2, upward, after_block, low, *shards = mlp(
            layer,
            final,
            count,
            own_list,
            attended,
            hidden,
            gain_mlp[layer : layer + 1],
            gain_attn[after : after + 1],
            w_out,
            w_up,
            w_down,
        )
        saved.append((hidden, parts, query, kv, memory_kv, maps, lse))
        saved[layer] += (attended, middle, normed2, upward)
        hidden = after_block
        if not final:
            parts = relative_gather(low, "blk")
            parts, shards = lax.optimization_barrier((parts, shards))
        shards = [shards[0]] + [swap(shards[k], "blk", k) for k in range(1, count)]
        saved[layer] += (shards,)
    mixed = low
    small = [None] * LAYERS
    near, far = bits[0], bits[1:]
    first, *others = bits_of("batch")

    def chain(item, moves):
        for axis, bit in moves:
            move = item.over_blk(bit) if axis == "blk" else item.over_batch(bit)
            item.take(swap(*move))

    def back(layer, grad, grad_low, extra=()):
        layer_input, parts, query, kv, memory_kv, maps, lse = saved[layer][:7]
        attended, middle, normed2, upward, shards = saved[layer][7:]
        inputs = (layer, count, own_list, grad, grad_low, upward, normed2, middle)
        inputs += (gain_mlp[layer : layer + 1], attended, w_out, w_up, w_down)
        return mlp_back(*inputs, extra)

    def attention(layer, d_attended, extra):
        layer_input, parts, query, kv, memory_kv, maps, lse = saved[layer][:7]
        outs = attend_back(bias, query, kv, memory_kv, maps, lse, d_attended, extra)
        return outs[:5], outs[5]

    layer = LAYERS - 1
    parts, shards = saved[layer][1], saved[layer][-1]
    sent, kept, grad, grad_low, d_attended, d_gain_mlp = back(layer, grad, grad_low)
    up1 = Sum(kept)
    (sent,) = gate([sent], shards[1:])
    up1.take(swap(sent, "blk", near))
    down = down_grad(shards, grad_parts)
    down1 = Sum(down.reshape(-1, D // count, D))
    moves = [("blk", bit) for bit in far]
    operand = up1.over_blk(far[0])
    derivatives, d_maps1 = attention(layer, d_attended, [operand[0], down])
    up1.take(swap(*operand))
    chain(up1, moves[1:])
    terms = input_terms(layer, count, *derivatives[:3], w_qkv)
    terms = scatter_step(dict(enumerate(terms)), "blk", near)
    numbers = [k for k in terms if k]
    terms.update(zip(numbers, gate([terms[k] for k in numbers], up1.newest())))
    extra = [terms[k] for k in terms if k] + up1.newest()
    for bit in far:
        terms = scatter_step(terms, "blk", bit)
    mlp1 = side_by_side([up1, down1])
    operand_y1 = mlp1.over_batch(first)
    sent, kept = attention_grads(own_list, parts, coeff_low, derivatives, extra)
    (sent,) = gate([sent], [terms[0]])
    last1 = Sum(kept)
    last1.take(swap(sent, "blk", near))
    grad, grad_low, d_gain_attn = norm_back(
        saved[layer][0], gain_attn[layer : layer + 1], terms[0], grad
    )
    gains = jnp.concatenate([d_gain_attn, d_gain_mlp], 0)
    small[layer] = jnp.concatenate([gains, d_maps1[:2]], 1)

    layer = 0
    parts, shards = saved[layer][1], saved[layer][-1]
    operand = last1.over_blk(far[0])
    grad_first = grad_low
    sent, kept, grad, grad_low, d_attended, d_gain_mlp = back(
        layer, grad, grad_low, [operand[0], operand_y1[0]]
    )
    mlp1.take(swap(*operand_y1))
    last1.take(swap(*operand))
    chain(last1, moves[1:])
    grad_parts = gather_steps({0: grad_first}, "blk", far)
    (sent,) = gate(
        [sent], last1.newest() + mlp1.newest() + [grad_parts[k] for k in grad_parts if k]
    )
    up0 = Sum(kept)
    up0.take(swap(sent, "blk", near))
    operand = up0.over_blk(far[0])
    operand_y = last1.over_batch(first)
    operand_z1 = mlp1.over_batch(others[0])
    values = gate([operand_y[0], operand_z1[0]], up0.newest())
    operand_y = (values[0],) + operand_y[1:]
    operand_z1 = (values[1],) + operand_z1[1:]
    derivatives, d_maps0 = attention(
        layer, d_attended, [operand[0], operand_y[0], operand_z1[0]]
    )
    mlp1.take(swap(*operand_z1))
    up0.take(swap(*operand))
    chain(up0, moves[1:])
    last1.take(swap(*operand_y))
    grad_parts = gather_steps(grad_parts, "blk", [near])
    grad_parts = [grad_parts[k] for k in range(count)]
    operand_z1 = mlp1.over_batch(others[1])
    down = down_grad(shards, grad_parts, [operand_z1[0], d_maps0] + last1.newest())
    mlp1.take(swap(*operand_z1))
    down0 = Sum(down.reshape(-1, D // count, D))
    sent, kept = attention_grads(own_list, parts, coeff_low, derivatives, [down])
    (sent,) = gate([sent], mlp1.newest())
    last0 = Sum(kept)
    last0.take(swap(sent, "blk", near))
    mlp0 = side_by_side([up0, down0])
    chain(mlp1, [("batch", bit) for bit in others[2:]])
    early = mlp1.whole()
    *more, second, third, fourth = reversed(bits_of("batch"))
    for bit in more:
        early = doubled(early, swap(early, "batch", bit), bit)
    operand = last0.over_blk(far[0])
    operand_y = mlp0.over_batch(first)
    operand_z = last1.over_batch(others[0])
    values = gate([operand_y[0], operand_z[0], early], last0.newest())
    operand_y = (values[0],) + operand_y[1:]
    operand_z = (values[1],) + operand_z[1:]
    early = values[2]
    last1.take(swap(*operand_z))
    terms = input_terms(layer, count, *derivatives[:3], w_qkv, [operand[0], operand_y[0], early])
    last0.take(swap(*operand))
    chain(last0, moves[1:])
    mlp0.take(swap(*operand_y))
    got = swap(early, "batch", second)
    chain(last1, [("batch", bit) for bit in others[1:]])
    terms = scatter_step(dict(enumerate(terms)), "blk", near)
    numbers = [k for k in terms if k]
    terms.update(zip(numbers, gate([terms[k] for k in numbers], last0.newest() + mlp0.newest())))
    operand = last0.over_batch(first)
    early = doubled(early, got, second)
    got = swap(early, "batch", third)
    for bit in far:
        terms = scatter_step(terms, "blk", bit)
    last0.take(swap(*operand))
    operand_z = mlp0.over_batch(others[0])
    grad, grad_low, d_gain_attn = norm_back(
        saved[layer][0],
        gain_attn[layer : layer + 1],
        terms[0],
        grad,
        [operand[0], operand_z[0], got],
    )
    early = doubled(early, got, third)
    mlp0.take(swap(*operand_z))
    operand = last0.over_batch(others[0])
    operand = tuple(gate([operand[0]], [d_gain_attn])) + operand[1:]
    last0.take(swap(*operand))
    gains = jnp.concatenate([d_gain_attn, d_gain_mlp], 0)
    small[layer] = jnp.concatenate([gains, d_maps0[:2]], 1)
    packed = jnp.concatenate(small, 0)
    for bit in bits:
        packed = packed + swap(packed, "blk", bit)
    for item in (mlp0, last0):
        chain(item, [("batch", bit) for bit in others[1:]])
    got = swap(early, "batch", fourth)
    low = mlp0.whole()
    split = CHUNKS + 1
    rest = [last1.whole(), low[split:], last0.whole()]
    rows_each = rest[0].shape[1]
    values = packed.astype(bf16).reshape(-1)
    pieces = -(-values.shape[0] // (rows_each * D))
    values = jnp.pad(values, (0, pieces * rows_each * D - values.shape[0]))
    rest.append(values.reshape(pieces, rows_each, D))
    (rest,) = gate([jnp.concatenate(rest, 0)], [got])
    mlp1 = doubled(early, got, fourth)
    up0 = low[:split]
    for bit in reversed(bits_of("batch")):
        up0 = doubled(up0, swap(up0, "batch", bit), bit)
    rest = gathered(rest)
    packed = jnp.sum(rest[:, -pieces:].astype(f32), 0).reshape(-1)[: packed.size]
    rest = in_place(rest)[:-pieces]
    last1, down0, last0 = rest[:3], rest[3:-3], rest[-3:]
    mlp0 = jnp.concatenate([up0, down0], 0)
    packed = packed.reshape(LAYERS, 2, D + NBASIS)

    def share_of(value):
        share = value.shape[1] // count
        return lax.dynamic_slice_in_dim(value, own * share, share, 1)

    shares = [share_of(packed[:, i, at]) for at in (slice(0, D), slice(D, None)) for i in (0, 1)]


    def columns(blocks):
        return jnp.concatenate([blocks[i] for i in range(blocks.shape[0])], 1)

    def both(low, high):
        return jnp.stack([low, high]).astype(f32)

    return (
        mixed,
        grad,
        both(columns(last0), columns(last1)),
        both(mlp0[CHUNKS], mlp1[CHUNKS]),
        both(columns(mlp0[:CHUNKS]), columns(mlp1[:CHUNKS])),
        both(mlp0[CHUNKS + 1 :].reshape(-1, D), mlp1[CHUNKS + 1 :].reshape(-1, D)),
        *shares,
    )


def solution(mesh):
    placed = (
        P(("batch", "blk"), None),
        P("batch", "blk", None),
        P("batch", "blk"),
        P("batch"),
        P(),
        P(),
        P(),
        P(),
        P(),
        P(),
        P(),
        P(),
        P(("batch", "blk"), None),
    )
    return jax.shard_map(
        on_device,
        mesh=mesh,
        in_specs=placed,
        out_specs=(
            P(("batch", "blk"), None),
            P(("batch", "blk"), None),
            P(None, "blk", None),
            P(None, "blk", None),
            P(None, "blk", None),
            P(None, "blk", None),
            P(None, "blk"),
            P(None, "blk"),
            P(None, "blk"),
            P(None, "blk"),
        ),
        check_vma=False,
    )
```

```python
import functools

import jax
import jax.numpy as jnp
from jax import lax
from jax.experimental import pallas as pl
from jax.experimental.pallas import tpu as pltpu
from jax.sharding import PartitionSpec as P

HEADS = 12
HEAD = 64
D = 768
NBASIS = 256
LAYERS = 2
MEMPOS = 4096
PAIRS = HEADS // 2
PAIR = 2 * HEAD

COST_SCALE = 5e8
highest = lax.Precision.HIGHEST
ridge_weight = 0.5
bf16 = jnp.bfloat16
f32 = jnp.float32

NT = (((1,), (1,)), ((), ()))
TN = (((0,), (0,)), ((), ()))
VMEM = pl.BlockSpec(memory_space=pltpu.VMEM)


ANY = pl.BlockSpec(memory_space=pl.ANY)
LIMIT = 58 * 1024 * 1024
CHUNKS = 4


def cost(microseconds):
    return pl.CostEstimate(
        flops=int(microseconds * COST_SCALE), bytes_accessed=0, transcendentals=0
    )


def gauss_jordan(panel, first):
    count, width = panel.shape
    lane = lax.broadcasted_iota(jnp.int32, (1, width), 1)
    line = lax.broadcasted_iota(jnp.int32, (count, 1), 0)

    def spread(value, column):
        return jnp.broadcast_to(value[:, column : column + 1], value.shape)

    for p in range(0, count, 2):
        c = first + p
        row0, row1 = panel[p : p + 1, :], panel[p + 1 : p + 2, :]
        a, b = spread(row0, c), spread(row0, c + 1)
        e, d = spread(row1, c), spread(row1, c + 1)
        over = 1.0 / (a * d - b * e)
        clear0 = jnp.where(lane == c, 1.0, jnp.where(lane == c + 1, 0.0, row0))
        clear1 = jnp.where(lane == c, 0.0, jnp.where(lane == c + 1, 1.0, row1))
        new0 = (d * clear0 - b * clear1) * over
        new1 = (a * clear1 - e * clear0) * over
        factor0, factor1 = spread(panel, c), spread(panel, c + 1)
        rest = jnp.where((lane == c) | (lane == c + 1), 0.0, panel)
        rest = rest - factor0 * new0 - factor1 * new1
        panel = jnp.where(line == p, new0, jnp.where(line == p + 1, new1, rest))
    return panel


def basis_of(places):
    times = (places.astype(f32) + 0.5) / MEMPOS
    centres = (lax.broadcasted_iota(jnp.int32, (NBASIS, 1), 0).astype(f32) + 0.5) / NBASIS
    breadth = 1.0 / NBASIS
    offset = times - centres
    return jnp.exp(-offset * offset / (2.0 * breadth * breadth))


def gram_of(basis):
    line = lax.broadcasted_iota(jnp.int32, (NBASIS, NBASIS), 0)
    lane = lax.broadcasted_iota(jnp.int32, (NBASIS, NBASIS), 1)
    gram = lax.dot_general(basis, basis, NT, precision=highest, preferred_element_type=f32)
    return gram + jnp.where(line == lane, ridge_weight, 0.0)


def inverse_kernel(places_ref, inverse_ref):
    lane = lax.broadcasted_iota(jnp.int32, (NBASIS, NBASIS), 1)
    inverse_ref[...] = gram_of(basis_of(places_ref[...]))
    step = 32
    for first in range(0, NBASIS, step):
        panel = gauss_jordan(inverse_ref[first : first + step, :], first)
        columns = inverse_ref[...][:, first : first + step]
        inside = (lane >= first) & (lane < first + step)
        product = jnp.dot(columns, panel, precision=highest, preferred_element_type=f32)
        inverse_ref[...] = jnp.where(inside, 0.0, inverse_ref[...]) - product
        inverse_ref[first : first + step, :] = panel


def coeff_kernel(places_ref, samples_ref, inverse_ref, coeff_ref):
    def product(a, b):
        return jnp.dot(a, b, precision=highest, preferred_element_type=f32)

    basis = basis_of(places_ref[...])
    right = product(basis, samples_ref[...].astype(f32))
    coeffs = product(inverse_ref[...], right)
    coeffs += product(inverse_ref[...], right - product(gram_of(basis), coeffs))
    coeff_ref[...] = coeffs.astype(bf16)


def ridge_inverse(places):
    return pl.pallas_call(
        inverse_kernel,
        out_shape=jax.ShapeDtypeStruct((NBASIS, NBASIS), f32),
        in_specs=[VMEM],
        out_specs=VMEM,
        compiler_params=pltpu.CompilerParams(vmem_limit_bytes=40 * 1024 * 1024),
        cost_estimate=cost(16.6),
        name="ridge_inverse",
    )(places)


def ridge_coeffs(places, samples, inverse):
    return pl.pallas_call(
        coeff_kernel,
        out_shape=jax.ShapeDtypeStruct((NBASIS, D), bf16),
        in_specs=[VMEM] * 3,
        out_specs=VMEM,
        compiler_params=pltpu.CompilerParams(vmem_limit_bytes=40 * 1024 * 1024),
        cost_estimate=cost(4.4),
        name="ridge_coeffs",
    )(places, samples, inverse)


def expand_maps(maps, mem_keys):
    vectors = jnp.dot(maps, mem_keys.astype(f32), precision=highest, preferred_element_type=f32)
    row = lax.broadcasted_iota(jnp.int32, (8 * PAIRS, D), 0)
    which = row % 8
    lane_head = lax.broadcasted_iota(jnp.int32, (8 * PAIRS, D), 1) // HEAD
    owned = (which < 4) & (lane_head == 2 * (row // 8) + which // 2)
    both = jnp.where(which % 2 == 0, vectors[0:1, :], vectors[1:2, :])
    return jnp.where(owned, both, 0.0)


def memory_weights(logits):
    breadth = 1.0 / NBASIS
    place = 1.0 / (1.0 + jnp.exp(-logits[0:1, :]))
    sigma = logits[1:2, :]
    soft = jnp.maximum(sigma, 0.0) + jnp.log(1.0 + jnp.exp(-jnp.abs(sigma)))
    variance = (0.5 + soft) / 64.0
    centres = (lax.broadcasted_iota(jnp.int32, (NBASIS, 1), 0).astype(f32) + 0.5) / NBASIS
    offset = place - centres
    weights = (breadth * lax.rsqrt(variance)) * jnp.exp(offset * offset * (-0.5 / variance))
    return weights, place, variance, offset


def head_lanes(value, which):
    lane = lax.broadcasted_iota(jnp.int32, value.shape, 1)
    return jnp.where((lane < HEAD) == (which == 0), value, jnp.zeros_like(value))


def pair_block(rows, shift=0):
    return pl.BlockSpec((rows, PAIR), lambda p: (0, p + shift))


def whole_block(shape):
    return pl.BlockSpec(shape, lambda p: (0,) * len(shape))


def attend_back_kernel(
    bias, query_all, mem_keys_all, maps, lse, q, k, v, mv, da,
    dq, dk, dv, dmk, dmv, dmaps, logits, lines, dq_t,
):
    pair = pl.program_id(0)
    scale = HEAD**-0.5

    @pl.when(pair == 0)
    def _():
        table = expand_maps(maps[...], mem_keys_all[...])
        wide = query_all[...].astype(f32) * scale
        logits[...] = lax.dot_general(
            table, wide, NT, precision=highest, preferred_element_type=f32
        )

    rows8 = logits[pl.ds(pl.multiple_of(pair * 8, 8), 8), :]
    k_t = k[...].T
    halves = []
    derived = []
    d_keys = d_values = d_mem_values = None
    for s in range(2):
        qh = head_lanes(q[...], s) * jnp.asarray(scale, bf16)
        dh = head_lanes(da[...], s)
        scores = lax.dot_general(k[...], qh, NT, preferred_element_type=f32) + bias[...]
        probs = jnp.exp(scores - lse[0, s : s + 1, :])
        d_probs = lax.dot_general(v[...], dh, NT, preferred_element_type=f32)
        correction = jnp.sum(probs * d_probs, axis=0, keepdims=True)
        d_scores = (probs * (d_probs - correction)).astype(bf16)
        key_term = jnp.dot(d_scores, qh, preferred_element_type=f32)
        value_term = jnp.dot(probs.astype(bf16), dh, preferred_element_type=f32)
        query_term = jnp.dot(k_t, d_scores, preferred_element_type=f32) * scale
        weights, place, variance, offset = memory_weights(rows8[2 * s : 2 * s + 2, :])
        d_weights = lax.dot_general(mv[...], dh, NT, preferred_element_type=f32)
        mem_term = jnp.dot(weights.astype(bf16), dh, preferred_element_type=f32)
        moved = d_weights * weights
        sum0 = jnp.sum(moved, axis=0, keepdims=True)
        moved = moved * offset
        sum1 = jnp.sum(moved, axis=0, keepdims=True)
        sum2 = jnp.sum(moved * offset, axis=0, keepdims=True)
        d_place = -sum1 / variance
        d_variance = (sum2 / variance - sum0) * (0.5 / variance)
        derived.append(d_place * place * (1.0 - place))
        sigma = rows8[2 * s + 1 : 2 * s + 2, :]
        derived.append(d_variance * (1.0 / 64.0) / (1.0 + jnp.exp(-sigma)))
        halves.append(query_term[s * HEAD : (s + 1) * HEAD, :])
        d_keys = key_term if s == 0 else d_keys + key_term
        d_values = value_term if s == 0 else d_values + value_term
        d_mem_values = mem_term if s == 0 else d_mem_values + mem_term
    dk[...] = d_keys.astype(bf16)
    dv[...] = d_values.astype(bf16)
    dmv[...] = d_mem_values.astype(bf16)
    dq_t[pair] = jnp.concatenate(halves, 0).T
    lines[pl.ds(pl.multiple_of(pair * 8, 8), 8), :] = jnp.concatenate(
        derived + [jnp.zeros((4, derived[0].shape[1]), f32)], 0
    )

    @pl.when(pair == PAIRS - 1)
    def _():
        table = expand_maps(maps[...], mem_keys_all[...])
        low = lines[...].astype(bf16)
        back = lax.dot_general(low, table.astype(bf16), TN, preferred_element_type=f32) * scale
        for p in range(PAIRS):
            at = slice(p * PAIR, (p + 1) * PAIR)
            dq[:, at] = (dq_t[p] + back[:, at]).astype(bf16)
        sums = jnp.dot(low, query_all[...], preferred_element_type=f32) * scale
        row = lax.broadcasted_iota(jnp.int32, sums.shape, 0)
        which = row % 8
        lane_head = lax.broadcasted_iota(jnp.int32, sums.shape, 1) // HEAD
        owned = (which < 4) & (lane_head == 2 * (row // 8) + which // 2)
        sums = jnp.where(owned, sums, 0.0)
        even = jnp.sum(jnp.where(which % 2 == 0, sums, 0.0), axis=0, keepdims=True)
        odd = jnp.sum(jnp.where(which % 2 == 1, sums, 0.0), axis=0, keepdims=True)
        both = jnp.concatenate([even, odd, jnp.zeros((6, D), f32)], 0).astype(bf16)
        dmk[...] = lax.dot_general(
            maps[...].astype(bf16), both, TN, preferred_element_type=f32
        ).astype(bf16)
        dmaps[...] = lax.dot_general(both, mem_keys_all[...], NT, preferred_element_type=f32)


def attend_back(bias, query, kv, memory_kv, maps, lse, d_attended, extra=()):
    rows = query.shape[0]
    seq = kv.shape[0]
    return pl.pallas_call(
        after(attend_back_kernel, 10, extra),
        grid=(PAIRS,),
        in_specs=[
            whole_block((seq, rows)),
            whole_block((rows, D)),
            whole_block((NBASIS, D)),
            whole_block((8, NBASIS)),
            pl.BlockSpec((1, 8, rows), lambda p: (p, 0, 0)),
            pair_block(rows),
            pair_block(seq),
            pair_block(seq, PAIRS),
            pair_block(NBASIS, PAIRS),
            pair_block(rows),
        ]
        + [ANY] * len(extra),
        out_specs=[
            whole_block((rows, D)),
            pair_block(seq),
            pair_block(seq),
            whole_block((NBASIS, D)),
            pair_block(NBASIS),
            whole_block((8, NBASIS)),
        ],
        out_shape=[
            jax.ShapeDtypeStruct((rows, D), bf16),
            jax.ShapeDtypeStruct((seq, D), bf16),
            jax.ShapeDtypeStruct((seq, D), bf16),
            jax.ShapeDtypeStruct((NBASIS, D), bf16),
            jax.ShapeDtypeStruct((NBASIS, D), bf16),
            jax.ShapeDtypeStruct((8, NBASIS), f32),
        ],
        scratch_shapes=[
            pltpu.VMEM((8 * PAIRS, rows), f32),
            pltpu.VMEM((8 * PAIRS, rows), f32),
            pltpu.VMEM((PAIRS, rows, PAIR), f32),
        ],
        compiler_params=pltpu.CompilerParams(vmem_limit_bytes=56 * 1024 * 1024),
        cost_estimate=cost(18.3),
        name="attend_back",
    )(bias, query, memory_kv, maps, lse, query, kv, kv, memory_kv, d_attended, *extra)


def call_options(name, microseconds):
    return dict(
        compiler_params=pltpu.CompilerParams(vmem_limit_bytes=LIMIT),
        cost_estimate=cost(microseconds),
        name=name,
    )


def after(kernel, inputs, extra):
    def body(*refs):
        kernel(*refs[:inputs], *refs[inputs + len(extra) :])

    return body


def gate(values, extra):
    def kernel(*refs):
        del refs

    count = len(values)
    return pl.pallas_call(
        kernel,
        in_specs=[ANY] * (count + len(extra)),
        out_specs=[ANY] * count,
        out_shape=[jax.ShapeDtypeStruct(value.shape, value.dtype) for value in values],
        input_output_aliases={i: i for i in range(count)},
        **call_options("gate", 1.0),
    )(*values, *extra)


def dot_nt(a, b):
    return lax.dot_general(a, b, NT, preferred_element_type=f32)


def dot_tn(a, b):
    return lax.dot_general(a, b, TN, preferred_element_type=f32)


def normalise(value):
    centred = value - jnp.mean(value, axis=1, keepdims=True)
    spread = jnp.mean(centred * centred, axis=1, keepdims=True)
    factor = lax.rsqrt(spread + 1e-05)
    return centred * factor, factor


def norm_backward(value, gain, d_out):
    unit, factor = normalise(value)
    d_unit = d_out * gain
    mean0 = jnp.mean(d_unit, axis=1, keepdims=True)
    mean1 = jnp.mean(d_unit * unit, axis=1, keepdims=True)
    return factor * (d_unit - mean0 - unit * mean1), jnp.sum(d_out * unit, axis=0, keepdims=True)


def gelu_parts(upward):
    outer = 0.7978845608028654
    square = upward * upward
    inner = jnp.tanh(upward * (outer + outer * 0.044715 * square))
    half = 0.5 * (1.0 + inner)
    slope = half + 0.5 * upward * (1.0 - inner * inner) * (outer + 3.0 * outer * 0.044715 * square)
    return upward * half, slope


def store_shard(count, own, shard, rows, send, keep):
    size = rows.shape[0]
    width = count.bit_length() - 1
    relative = jnp.bitwise_xor(own, shard)
    place = 0
    for bit in range(width):
        place += jnp.bitwise_and(lax.shift_right_logical(relative, bit), 1) << (width - 1 - bit)

    @pl.when(place >= count // 2)
    def _():
        send[pl.ds(pl.multiple_of((place - count // 2) * size, 16), size), :] = rows

    @pl.when(place < count // 2)
    def _():
        keep[pl.ds(pl.multiple_of(place * size, 16), size), :] = rows


def store_shards(count, own, value, send, keep):
    size = value.shape[0] // count
    for shard in range(count):
        rows = value[shard * size : (shard + 1) * size, :].astype(bf16)
        store_shard(count, own, shard, rows, send, keep)


def attend_kernel(layer, count, *refs):
    parts = refs[:count]
    bias, coeff, maps, w_hbm = refs[count : count + 4]
    out, lse, query, kv, memory_kv = refs[count + 4 : count + 9]
    w, logits, sem = refs[count + 9 :]
    copy = pltpu.make_async_copy(w_hbm.at[layer], w, sem)
    copy.start()
    copy.wait()
    rows = query.shape[0]
    query[...] = jnp.dot(parts[0][...], w[:, :D], preferred_element_type=f32).astype(bf16)
    memory_kv[...] = jnp.dot(coeff[...], w[:, D:], preferred_element_type=f32).astype(bf16)
    for k in range(count):
        kv[k * rows : (k + 1) * rows, :] = jnp.dot(
            parts[k][...], w[:, D:], preferred_element_type=f32
        ).astype(bf16)
    table = expand_maps(maps[...], memory_kv[:, :D])
    wide = query[...].astype(f32) * HEAD**-0.5
    logits[...] = lax.dot_general(table, wide, NT, precision=highest, preferred_element_type=f32)

    def body(pair, carry):
        at = pl.ds(pl.multiple_of(pair * PAIR, PAIR), PAIR)
        value_at = pl.ds(pl.multiple_of(D + pair * PAIR, PAIR), PAIR)
        lines = logits[pl.ds(pl.multiple_of(pair * 8, 8), 8), :]
        q, k = query[:, at], kv[:, at]
        v_t = kv[:, value_at].T
        mv_t = memory_kv[:, value_at].T
        halves = []
        totals = []
        for s in range(2):
            qh = head_lanes(q, s) * jnp.asarray(HEAD**-0.5, bf16)
            blocks = [slice(i * rows, (i + 1) * rows) for i in range(count)]
            scores = [dot_nt(k[blocks[0]], qh) + bias[blocks[0], :]]
            for block in blocks[1:]:
                scores.append(dot_nt(k[block], qh) + bias[block.start : block.start + 1, :])
            peak = functools.reduce(
                jnp.maximum, [jnp.max(item, axis=0, keepdims=True) for item in scores]
            )
            expo = [jnp.exp(item - peak) for item in scores]
            total = sum(jnp.sum(item, axis=0, keepdims=True) for item in expo)
            local = sum(
                jnp.dot(v_t[:, block], item.astype(bf16), preferred_element_type=f32)
                for block, item in zip(blocks, expo)
            ) * (1.0 / total)
            weights = memory_weights(lines[2 * s : 2 * s + 2, :])[0]
            recalled = jnp.dot(mv_t, weights.astype(bf16), preferred_element_type=f32)
            halves.append((local + recalled)[s * HEAD : (s + 1) * HEAD, :])
            totals.append(peak + jnp.log(total))
        out[:, at] = jnp.concatenate(halves, 0).T.astype(bf16)
        lse[pair, 0:1, :] = totals[0]
        lse[pair, 1:2, :] = totals[1]
        return carry

    lax.fori_loop(0, PAIRS, body, 0, unroll=2)


def attend(layer, parts, bias, coeff, maps, w_qkv):
    rows = parts[0].shape[0]
    seq = rows * len(parts)
    return pl.pallas_call(
        functools.partial(attend_kernel, layer, len(parts)),
        in_specs=[VMEM] * (len(parts) + 3) + [ANY],
        out_specs=[VMEM] * 5,
        out_shape=[
            jax.ShapeDtypeStruct((rows, D), bf16),
            jax.ShapeDtypeStruct((PAIRS, 8, rows), f32),
            jax.ShapeDtypeStruct((rows, D), bf16),
            jax.ShapeDtypeStruct((seq, 2 * D), bf16),
            jax.ShapeDtypeStruct((NBASIS, 2 * D), bf16),
        ],
        scratch_shapes=[
            pltpu.VMEM((D, 3 * D), bf16),
            pltpu.VMEM((8 * PAIRS, rows), f32),
            pltpu.SemaphoreType.DMA,
        ],
        **call_options("attend", 20.8),
    )(*parts, bias, coeff, maps, w_qkv)


def mlp_kernel(last, count, own, *refs):
    attended, hidden, gain, next_gain, w_out, w_up, w_down = refs[:7]
    middle, normed2, upward, hidden_out, low_out = refs[7:12]
    shards = refs[12:]
    step = pl.program_id(0)

    @pl.when(step == 0)
    def _():
        middle[...] = hidden[...] + jnp.dot(
            attended[...], w_out[0], preferred_element_type=f32
        )
        normed2[...] = (normalise(middle[...])[0] * gain[...]).astype(bf16)
        hidden_out[...] = middle[...]

    up = jnp.dot(normed2[...], w_up[0], preferred_element_type=f32)
    upward[...] = up
    active = gelu_parts(up)[0].astype(bf16)
    hidden_out[...] += jnp.dot(active, w_down[0], preferred_element_type=f32)
    pieces = max(1, count // CHUNKS)
    share = active.shape[1] // pieces
    for i in range(pieces):
        relative = jnp.bitwise_xor(own[0], step * pieces + i)
        for k in range(count):

            @pl.when(relative == k)
            def _(i=i, k=k):
                shards[k][...] = active[:, i * share : (i + 1) * share]

    @pl.when(step == CHUNKS - 1)
    def _():
        value = hidden_out[...]
        low_out[...] = (value if last else normalise(value)[0] * next_gain[...]).astype(bf16)


def mlp(layer, last, count, own, attended, hidden, gain, next_gain, w_out, w_up, w_down):
    rows = hidden.shape[0]
    hidden_units = w_up.shape[2]
    chunk = hidden_units // CHUNKS
    share = hidden_units // count
    assert count >= CHUNKS
    whole = pl.BlockSpec((rows, D), lambda j, own: (0, 0))
    line = pl.BlockSpec((1, D), lambda j, own: (0, 0))
    shard = pl.BlockSpec((rows, share), lambda j, own: (0, 0))
    return pl.pallas_call(
        functools.partial(mlp_kernel, last, count),
        grid_spec=pltpu.PrefetchScalarGridSpec(
            num_scalar_prefetch=1,
            grid=(CHUNKS,),
            in_specs=[
                whole,
                whole,
                line,
                line,
                pl.BlockSpec((1, D, D), lambda j, own: (layer, 0, 0)),
                pl.BlockSpec((1, D, chunk), lambda j, own: (layer, 0, j)),
                pl.BlockSpec((1, chunk, D), lambda j, own: (layer, j, 0)),
            ],
            out_specs=[
                whole,
                whole,
                pl.BlockSpec((rows, chunk), lambda j, own: (0, j)),
                whole,
                whole,
            ]
            + [shard] * count,
        ),
        out_shape=[
            jax.ShapeDtypeStruct((rows, D), f32),
            jax.ShapeDtypeStruct((rows, D), bf16),
            jax.ShapeDtypeStruct((rows, hidden_units), f32),
            jax.ShapeDtypeStruct((rows, D), f32),
            jax.ShapeDtypeStruct((rows, D), bf16),
        ]
        + [jax.ShapeDtypeStruct((rows, share), bf16)] * count,
        **call_options("mlp", 10.4),
    )(own, attended, hidden, gain, next_gain, w_out, w_up, w_down)


def mlp_back_kernel(
    shards, own, grad, grad_low, upward, normed2, middle, gain, attended, w_out, w_up, w_down,
    send, keep, grad_out, low_out, d_attended, d_gain, left, d_normed,
):
    step = pl.program_id(0)

    @pl.when(step == 0)
    def _():
        left[...] = normed2[...].T

    @pl.when(step < CHUNKS)
    def _():
        d_active = dot_nt(grad_low[...], w_down[0])
        d_up = (d_active * gelu_parts(upward[...])[1]).astype(bf16)
        term = dot_nt(d_up, w_up[0])

        @pl.when(step == 0)
        def _():
            d_normed[...] = term

        @pl.when(step > 0)
        def _():
            d_normed[...] += term

        value = jnp.dot(left[...], d_up, preferred_element_type=f32)
        store_shards(shards, own[0], value, send.at[0], keep.at[0])

    @pl.when(step == CHUNKS)
    def _():
        d_middle, d_line = norm_backward(middle[...], gain[...], d_normed[...])
        total = grad[...] + d_middle
        grad_out[...] = total
        low = total.astype(bf16)
        low_out[...] = low
        d_attended[...] = dot_nt(low, w_out[0]).astype(bf16)
        d_gain[...] = d_line
        store_shards(shards, own[0], dot_tn(attended[...], low), send.at[0], keep.at[0])


def mlp_back(
    layer,
    shards,
    own,
    grad,
    grad_low,
    upward,
    normed2,
    middle,
    gain,
    attended,
    w_out,
    w_up,
    w_down,
    extra=(),
):
    rows = grad.shape[0]
    chunk = w_up.shape[2] // CHUNKS
    last = CHUNKS - 1
    whole = pl.BlockSpec((rows, D), lambda j, own: (0, 0))
    line = pl.BlockSpec((1, D), lambda j, own: (0, 0))
    half = pl.BlockSpec((1, D // 2, chunk), lambda j, own: (j, 0, 0))
    shape = jax.ShapeDtypeStruct((CHUNKS + 1, D // 2, chunk), bf16)
    return pl.pallas_call(
        after(functools.partial(mlp_back_kernel, shards), 11, extra),
        grid_spec=pltpu.PrefetchScalarGridSpec(
            num_scalar_prefetch=1,
            grid=(CHUNKS + 1,),
            in_specs=[
                whole,
                whole,
                pl.BlockSpec((rows, chunk), lambda j, own: (0, jnp.minimum(j, last))),
                whole,
                whole,
                line,
                whole,
                pl.BlockSpec((1, D, D), lambda j, own: (layer, 0, 0)),
                pl.BlockSpec((1, D, chunk), lambda j, own: (layer, 0, jnp.minimum(j, last))),
                pl.BlockSpec((1, chunk, D), lambda j, own: (layer, jnp.minimum(j, last), 0)),
            ]
            + [ANY] * len(extra),
            out_specs=[half, half, whole, whole, whole, line],
            scratch_shapes=[pltpu.VMEM((D, rows), bf16), pltpu.VMEM((rows, D), f32)],
        ),
        out_shape=[
            shape,
            shape,
            jax.ShapeDtypeStruct((rows, D), f32),
            jax.ShapeDtypeStruct((rows, D), bf16),
            jax.ShapeDtypeStruct((rows, D), bf16),
            jax.ShapeDtypeStruct((1, D), f32),
        ],
        **call_options("mlp_back", 14.6),
    )(own, grad, grad_low, upward, normed2, middle, gain, attended, w_out, w_up, w_down, *extra)


def down_kernel(count, *refs):
    out = refs[-1]
    total = dot_tn(refs[0][...], refs[count][...])
    for k in range(1, count):
        total += dot_tn(refs[k][...], refs[count + k][...])
    out[...] = total.astype(bf16)


def down_grad(actives, grads, extra=()):
    count = len(actives)
    return pl.pallas_call(
        after(functools.partial(down_kernel, count), 2 * count, extra),
        in_specs=[VMEM] * (2 * count) + [ANY] * len(extra),
        out_specs=VMEM,
        out_shape=jax.ShapeDtypeStruct((actives[0].shape[1], D), bf16),
        **call_options("down_grad", 4.3),
    )(*actives, *grads, *extra)


def input_kernel(layer, d_query, d_keys, d_values, w_hbm, *refs):
    outs, (w, sem) = refs[:-2], refs[-2:]
    copy = pltpu.make_async_copy(w_hbm.at[layer], w, sem)
    copy.start()
    copy.wait()
    rows = d_query.shape[0]
    total = dot_nt(d_keys[...], w[:, D : 2 * D]) + dot_nt(d_values[...], w[:, 2 * D :])
    outs[0][...] = (total[:rows, :] + dot_nt(d_query[...], w[:, :D])).astype(bf16)
    for k in range(1, len(outs)):
        outs[k][...] = total[k * rows : (k + 1) * rows, :].astype(bf16)


def input_terms(layer, count, d_query, d_keys, d_values, w_qkv, extra=()):
    return pl.pallas_call(
        after(functools.partial(input_kernel, layer), 4, extra),
        in_specs=[VMEM] * 3 + [ANY] + [ANY] * len(extra),
        out_specs=[VMEM] * count,
        out_shape=[jax.ShapeDtypeStruct(d_query.shape, bf16)] * count,
        scratch_shapes=[pltpu.VMEM((D, 3 * D), bf16), pltpu.SemaphoreType.DMA],
        **call_options("input_terms", 7.6),
    )(d_query, d_keys, d_values, w_qkv, *extra)


def attention_grad_kernel(count, own, *refs):
    parts = refs[:count]
    coeff, d_query, d_keys, d_values, d_mem_keys, d_mem_values, send, keep, left = refs[count:]
    rows = d_query.shape[0]
    seq = rows * count
    size = D // count
    for k in range(count):
        left[:, k * rows : (k + 1) * rows] = parts[k][...].T
    left[:, seq:] = coeff[...].T

    def product(a, b):
        return jnp.dot(a, b[...], preferred_element_type=f32)

    for shard in range(count):
        line = left[shard * size : (shard + 1) * size, :]
        own_line, all_line, mem_line = line[:, :rows], line[:, :seq], line[:, seq:]
        values = (
            product(own_line, d_query),
            product(all_line, d_keys) + product(mem_line, d_mem_keys),
            product(all_line, d_values) + product(mem_line, d_mem_values),
        )
        for i, value in enumerate(values):
            store_shard(count, own[0], shard, value.astype(bf16), send.at[i], keep.at[i])


def attention_grads(own, parts, coeff, derivatives, extra=()):
    smem = pl.BlockSpec(memory_space=pltpu.SMEM)
    shape = jax.ShapeDtypeStruct((3, D // 2, D), bf16)
    inputs = (*parts, coeff, *derivatives)
    return pl.pallas_call(
        after(functools.partial(attention_grad_kernel, len(parts)), 1 + len(inputs), extra),
        in_specs=[smem] + [VMEM] * len(inputs) + [ANY] * len(extra),
        out_specs=[VMEM, VMEM],
        out_shape=[shape, shape],
        scratch_shapes=[pltpu.VMEM((D, parts[0].shape[0] * len(parts) + NBASIS), bf16)],
        **call_options("attention_grads", 9.6),
    )(own, *inputs, *extra)


def norm_back_kernel(value, gain, d_out, grad, grad_out, low_out, d_gain):
    d_value, d_line = norm_backward(value[...], gain[...], d_out[...].astype(f32))
    total = grad[...] + d_value
    grad_out[...] = total
    low_out[...] = total.astype(bf16)
    d_gain[...] = d_line


def norm_back(value, gain, d_out, grad, extra=()):
    return pl.pallas_call(
        after(norm_back_kernel, 4, extra),
        in_specs=[VMEM] * 4 + [ANY] * len(extra),
        out_specs=[VMEM] * 3,
        out_shape=[
            jax.ShapeDtypeStruct(grad.shape, f32),
            jax.ShapeDtypeStruct(grad.shape, bf16),
            jax.ShapeDtypeStruct((1, D), f32),
        ],
        **call_options("norm_back", 3.1),
    )(value, gain, d_out, grad, *extra)


def start_kernel(live, tokens, gain, cotangent, hidden, normed, grad, grad_low):
    wide = tokens[...].astype(f32)
    hidden[...] = wide
    normed[...] = (normalise(wide)[0] * gain[...]).astype(bf16)
    masked = cotangent[...].astype(f32) * live[0].astype(f32)
    grad[...] = masked
    grad_low[...] = masked.astype(bf16)


def start(live, tokens, gain, cotangent):
    return pl.pallas_call(
        start_kernel,
        in_specs=[pl.BlockSpec(memory_space=pltpu.SMEM)] + [VMEM] * 3,
        out_specs=[VMEM] * 4,
        out_shape=[jax.ShapeDtypeStruct(tokens.shape, kind) for kind in (f32, bf16, f32, bf16)],
        **call_options("start", 2.5),
    )(live, tokens, gain, cotangent)


def swap(value, axis, bit):
    count = lax.axis_size(axis)
    return lax.ppermute(value, axis, [(i, i ^ bit) for i in range(count)])


def bits_of(axis):
    return [1 << i for i in range(lax.axis_size(axis).bit_length() - 1)]


def gather_steps(held, axis, bits):
    held = dict(held)
    for bit in reversed(bits):
        held.update({k | bit: swap(v, axis, bit) for k, v in list(held.items())})
    return held


def relative_gather(value, axis):
    held = gather_steps({0: value}, axis, bits_of(axis))
    return [held[k] for k in range(lax.axis_size(axis))]


def scatter_step(held, axis, bit):
    sent = {k: swap(v, axis, bit) for k, v in held.items() if k & bit}
    return {
        k: (v.astype(f32) + sent[k | bit].astype(f32)).astype(bf16)
        for k, v in held.items()
        if not k & bit
    }


class Sum:
    def __init__(self, *terms):
        self.terms = [(term, 0) for term in terms]
        self.rows = terms[0].shape[1]

    def added(self, terms):
        parts = [
            value
            if value.shape[1] == self.rows
            else lax.dynamic_slice_in_dim(value, at, self.rows, 1)
            for value, at in terms
        ]
        if len(parts) == 1:
            return parts[0]
        return sum(part.astype(f32) for part in parts).astype(bf16)

    def whole(self):
        return self.added(self.terms)

    def blocks(self):
        return self.terms[0][0].shape[0]

    def newest(self):
        return [self.terms[-1][0]]

    def split(self, side):
        self.rows = self.rows // 2
        sent = [(value, at + (1 - side) * self.rows) for value, at in self.terms]
        sent = self.added(sent)
        self.terms = [(value, at + side * self.rows) for value, at in self.terms]
        return sent

    def take(self, got):
        self.terms.append((got, 0))

    def over_blk(self, bit):
        return self.split(0), "blk", bit

    def over_batch(self, bit):
        side = jnp.where(jnp.bitwise_and(lax.axis_index("batch"), bit) > 0, 1, 0)
        return self.split(side), "batch", bit


def side_by_side(items):
    items = [item.whole() for item in items]
    return Sum(jnp.concatenate(items, 0))


def doubled(total, got, bit):
    upper = jnp.bitwise_and(lax.axis_index("batch"), bit) > 0
    return jnp.concatenate([jnp.where(upper, got, total), jnp.where(upper, total, got)], 1)


def gathered(total):
    blocks, rows, columns = total.shape
    whole = lax.all_gather(total.reshape(blocks * rows, columns), "batch", axis=0)
    return whole.reshape(-1, blocks, rows, columns)


def in_place(whole):
    count, blocks, rows, columns = whole.shape
    width = count.bit_length() - 1
    whole = whole.reshape((2,) * width + (blocks, rows, columns))
    order = (width,) + tuple(reversed(range(width))) + (width + 1, width + 2)
    return whole.transpose(order).reshape(blocks, -1, columns)


def on_device(
    tokens,
    memory,
    mem_pos,
    seg_count,
    w_qkv,
    w_out,
    w_up,
    w_down,
    gain_attn,
    gain_mlp,
    w_mu,
    w_sig,
    cotangent,
):
    rows = tokens.shape[0]
    hidden_units = w_up.shape[2]
    count = lax.axis_size("blk")
    length = seg_count[0] * rows
    own = lax.axis_index("blk")
    own_list = own.astype(jnp.int32).reshape(1)
    own_places = own * rows + jnp.arange(rows, dtype=jnp.int32)
    all_places = jnp.concatenate(
        [jnp.bitwise_xor(own, k) * rows + jnp.arange(rows, dtype=jnp.int32) for k in range(count)]
    )
    allowed = (all_places[:, None] <= own_places[None, :]) & (all_places[:, None] < length)
    bias = jnp.where(allowed, 0.0, -1e30).astype(f32)
    lives = (own < seg_count[0]).astype(jnp.int32).reshape(1)
    hidden, normed, grad, grad_low = start(lives, tokens, gain_attn[0:1], cotangent)
    places = jnp.concatenate(relative_gather(mem_pos, "blk"), 1)
    places, sample, normed = lax.optimization_barrier((places, memory[0], normed))
    bits = bits_of("blk")
    far = [gather_steps({0: value}, "blk", bits[1:]) for value in (sample, normed)]
    inverse = ridge_inverse(places)
    inverse, far, grad_low, bias = lax.optimization_barrier((inverse, far, grad_low, bias))
    samples, parts = [gather_steps(held, "blk", bits[:1]) for held in far]
    samples = jnp.concatenate([samples[k] for k in range(count)], 0)
    parts = [parts[k] for k in range(count)]
    coeff_low = ridge_coeffs(places, samples, inverse)
    coeff_low, grad_low = lax.optimization_barrier((coeff_low, grad_low))
    grad_parts = [grad_low] + [swap(grad_low, "blk", k) for k in range(1, count)]
    saved = []
    for layer in range(LAYERS):
        final = layer == LAYERS - 1
        maps = jnp.concatenate(
            [w_mu[layer][None], w_sig[layer][None], jnp.zeros((6, NBASIS), f32)], 0
        )
        attended, lse, query, kv, memory_kv = attend(layer, parts, bias, coeff_low, maps, w_qkv)
        if layer == 0:
            grad_parts, attended = lax.optimization_barrier((grad_parts, attended))
        else:
            before, attended = lax.optimization_barrier((saved[layer - 1][-1], attended))
            saved[layer - 1] = saved[layer - 1][:-1] + (before,)
        after = min(layer + 1, LAYERS - 1)
        middle, normed2, upward, after_block, low, *shards = mlp(
            layer,
            final,
            count,
            own_list,
            attended,
            hidden,
            gain_mlp[layer : layer + 1],
            gain_attn[after : after + 1],
            w_out,
            w_up,
            w_down,
        )
        saved.append((hidden, parts, query, kv, memory_kv, maps, lse))
        saved[layer] += (attended, middle, normed2, upward)
        hidden = after_block
        if not final:
            parts = relative_gather(low, "blk")
            parts, shards = lax.optimization_barrier((parts, shards))
        shards = [shards[0]] + [swap(shards[k], "blk", k) for k in range(1, count)]
        saved[layer] += (shards,)
    mixed = low
    small = [None] * LAYERS
    near, far = bits[0], bits[1:]
    first, *others = bits_of("batch")

    def chain(item, moves):
        for axis, bit in moves:
            move = item.over_blk(bit) if axis == "blk" else item.over_batch(bit)
            item.take(swap(*move))

    def back(layer, grad, grad_low, extra=()):
        layer_input, parts, query, kv, memory_kv, maps, lse = saved[layer][:7]
        attended, middle, normed2, upward, shards = saved[layer][7:]
        inputs = (layer, count, own_list, grad, grad_low, upward, normed2, middle)
        inputs += (gain_mlp[layer : layer + 1], attended, w_out, w_up, w_down)
        return mlp_back(*inputs, extra)

    def attention(layer, d_attended, extra):
        layer_input, parts, query, kv, memory_kv, maps, lse = saved[layer][:7]
        outs = attend_back(bias, query, kv, memory_kv, maps, lse, d_attended, extra)
        return outs[:5], outs[5]

    layer = LAYERS - 1
    parts, shards = saved[layer][1], saved[layer][-1]
    sent, kept, grad, grad_low, d_attended, d_gain_mlp = back(layer, grad, grad_low)
    up1 = Sum(kept)
    (sent,) = gate([sent], shards[1:])
    up1.take(swap(sent, "blk", near))
    down = down_grad(shards, grad_parts)
    down1 = Sum(down.reshape(-1, D // count, D))
    moves = [("blk", bit) for bit in far]
    operand = up1.over_blk(far[0])
    derivatives, d_maps1 = attention(layer, d_attended, [operand[0], down])
    up1.take(swap(*operand))
    chain(up1, moves[1:])
    terms = input_terms(layer, count, *derivatives[:3], w_qkv)
    terms = scatter_step(dict(enumerate(terms)), "blk", near)
    numbers = [k for k in terms if k]
    terms.update(zip(numbers, gate([terms[k] for k in numbers], up1.newest())))
    extra = [terms[k] for k in terms if k] + up1.newest()
    for bit in far:
        terms = scatter_step(terms, "blk", bit)
    mlp1 = side_by_side([up1, down1])
    operand_y1 = mlp1.over_batch(first)
    sent, kept = attention_grads(own_list, parts, coeff_low, derivatives, extra)
    (sent,) = gate([sent], [terms[0]])
    last1 = Sum(kept)
    last1.take(swap(sent, "blk", near))
    grad, grad_low, d_gain_attn = norm_back(
        saved[layer][0], gain_attn[layer : layer + 1], terms[0], grad
    )
    gains = jnp.concatenate([d_gain_attn, d_gain_mlp], 0)
    small[layer] = jnp.concatenate([gains, d_maps1[:2]], 1)

    layer = 0
    parts, shards = saved[layer][1], saved[layer][-1]
    operand = last1.over_blk(far[0])
    grad_first = grad_low
    sent, kept, grad, grad_low, d_attended, d_gain_mlp = back(
        layer, grad, grad_low, [operand[0], operand_y1[0]]
    )
    mlp1.take(swap(*operand_y1))
    last1.take(swap(*operand))
    chain(last1, moves[1:])
    grad_parts = gather_steps({0: grad_first}, "blk", far)
    (sent,) = gate(
        [sent], last1.newest() + mlp1.newest() + [grad_parts[k] for k in grad_parts if k]
    )
    up0 = Sum(kept)
    up0.take(swap(sent, "blk", near))
    operand = up0.over_blk(far[0])
    operand_y = last1.over_batch(first)
    operand_z1 = mlp1.over_batch(others[0])
    values = gate([operand_y[0], operand_z1[0]], up0.newest())
    operand_y = (values[0],) + operand_y[1:]
    operand_z1 = (values[1],) + operand_z1[1:]
    derivatives, d_maps0 = attention(
        layer, d_attended, [operand[0], operand_y[0], operand_z1[0]]
    )
    mlp1.take(swap(*operand_z1))
    up0.take(swap(*operand))
    chain(up0, moves[1:])
    last1.take(swap(*operand_y))
    grad_parts = gather_steps(grad_parts, "blk", [near])
    grad_parts = [grad_parts[k] for k in range(count)]
    operand_z1 = mlp1.over_batch(others[1])
    down = down_grad(shards, grad_parts, [operand_z1[0], d_maps0] + last1.newest())
    mlp1.take(swap(*operand_z1))
    down0 = Sum(down.reshape(-1, D // count, D))
    sent, kept = attention_grads(own_list, parts, coeff_low, derivatives, [down])
    (sent,) = gate([sent], mlp1.newest())
    last0 = Sum(kept)
    last0.take(swap(sent, "blk", near))
    mlp0 = side_by_side([up0, down0])
    chain(mlp1, [("batch", bit) for bit in others[2:]])
    early = mlp1.whole()
    *more, second, third, fourth = reversed(bits_of("batch"))
    for bit in more:
        early = doubled(early, swap(early, "batch", bit), bit)
    operand = last0.over_blk(far[0])
    operand_y = mlp0.over_batch(first)
    operand_z = last1.over_batch(others[0])
    values = gate([operand_y[0], operand_z[0], early], last0.newest())
    operand_y = (values[0],) + operand_y[1:]
    operand_z = (values[1],) + operand_z[1:]
    early = values[2]
    last1.take(swap(*operand_z))
    terms = input_terms(layer, count, *derivatives[:3], w_qkv, [operand[0], operand_y[0], early])
    last0.take(swap(*operand))
    chain(last0, moves[1:])
    mlp0.take(swap(*operand_y))
    got = swap(early, "batch", second)
    chain(last1, [("batch", bit) for bit in others[1:]])
    terms = scatter_step(dict(enumerate(terms)), "blk", near)
    numbers = [k for k in terms if k]
    terms.update(zip(numbers, gate([terms[k] for k in numbers], last0.newest() + mlp0.newest())))
    operand = last0.over_batch(first)
    early = doubled(early, got, second)
    got = swap(early, "batch", third)
    for bit in far:
        terms = scatter_step(terms, "blk", bit)
    last0.take(swap(*operand))
    operand_z = mlp0.over_batch(others[0])
    grad, grad_low, d_gain_attn = norm_back(
        saved[layer][0],
        gain_attn[layer : layer + 1],
        terms[0],
        grad,
        [operand[0], operand_z[0], got],
    )
    early = doubled(early, got, third)
    mlp0.take(swap(*operand_z))
    operand = last0.over_batch(others[0])
    operand = tuple(gate([operand[0]], [d_gain_attn])) + operand[1:]
    last0.take(swap(*operand))
    gains = jnp.concatenate([d_gain_attn, d_gain_mlp], 0)
    small[layer] = jnp.concatenate([gains, d_maps0[:2]], 1)
    packed = jnp.concatenate(small, 0)
    for bit in bits:
        packed = packed + swap(packed, "blk", bit)
    for item in (mlp0, last0):
        chain(item, [("batch", bit) for bit in others[1:]])
    got = swap(early, "batch", fourth)
    low = mlp0.whole()
    split = CHUNKS + 1
    rest = [last1.whole(), low[:split], last0.whole()]
    rows_each = rest[0].shape[1]
    values = packed.astype(bf16).reshape(-1)
    pieces = -(-values.shape[0] // (rows_each * D))
    values = jnp.pad(values, (0, pieces * rows_each * D - values.shape[0]))
    rest.append(values.reshape(pieces, rows_each, D))
    (rest,) = gate([jnp.concatenate(rest, 0)], [got])
    mlp1 = doubled(early, got, fourth)
    down0 = low[split:]
    for bit in reversed(bits_of("batch")):
        down0 = doubled(down0, swap(down0, "batch", bit), bit)
    rest = gathered(rest)
    packed = jnp.sum(rest[:, -pieces:].astype(f32), 0).reshape(-1)[: packed.size]
    rest = in_place(rest)[:-pieces]
    last1, up0, last0 = rest[:3], rest[3:-3], rest[-3:]
    mlp0 = jnp.concatenate([up0, down0], 0)
    packed = packed.reshape(LAYERS, 2, D + NBASIS)

    def share_of(value):
        share = value.shape[1] // count
        return lax.dynamic_slice_in_dim(value, own * share, share, 1)

    shares = [share_of(packed[:, i, at]) for at in (slice(0, D), slice(D, None)) for i in (0, 1)]


    def columns(blocks):
        return jnp.concatenate([blocks[i] for i in range(blocks.shape[0])], 1)

    def both(low, high):
        return jnp.stack([low, high]).astype(f32)

    return (
        mixed,
        grad,
        both(columns(last0), columns(last1)),
        both(mlp0[CHUNKS], mlp1[CHUNKS]),
        both(columns(mlp0[:CHUNKS]), columns(mlp1[:CHUNKS])),
        both(mlp0[CHUNKS + 1 :].reshape(-1, D), mlp1[CHUNKS + 1 :].reshape(-1, D)),
        *shares,
    )


def solution(mesh):
    placed = (
        P(("batch", "blk"), None),
        P("batch", "blk", None),
        P("batch", "blk"),
        P("batch"),
        P(),
        P(),
        P(),
        P(),
        P(),
        P(),
        P(),
        P(),
        P(("batch", "blk"), None),
    )
    return jax.shard_map(
        on_device,
        mesh=mesh,
        in_specs=placed,
        out_specs=(
            P(("batch", "blk"), None),
            P(("batch", "blk"), None),
            P(None, "blk", None),
            P(None, "blk", None),
            P(None, "blk", None),
            P(None, "blk", None),
            P(None, "blk"),
            P(None, "blk"),
            P(None, "blk"),
            P(None, "blk"),
        ),
        check_vma=False,
    )
```

```python
import functools

import jax
import jax.numpy as jnp
from jax import lax
from jax.experimental import pallas as pl
from jax.experimental.pallas import tpu as pltpu
from jax.sharding import PartitionSpec as P

HEADS = 12
HEAD = 64
D = 768
NBASIS = 256
LAYERS = 2
MEMPOS = 4096
PAIRS = HEADS // 2
PAIR = 2 * HEAD

COST_SCALE = 5e8
highest = lax.Precision.HIGHEST
ridge_weight = 0.5
bf16 = jnp.bfloat16
f32 = jnp.float32

NT = (((1,), (1,)), ((), ()))
TN = (((0,), (0,)), ((), ()))
VMEM = pl.BlockSpec(memory_space=pltpu.VMEM)


ANY = pl.BlockSpec(memory_space=pl.ANY)
LIMIT = 58 * 1024 * 1024
CHUNKS = 4


def cost(microseconds):
    return pl.CostEstimate(
        flops=int(microseconds * COST_SCALE), bytes_accessed=0, transcendentals=0
    )


def gauss_jordan(panel, first):
    count, width = panel.shape
    lane = lax.broadcasted_iota(jnp.int32, (1, width), 1)
    line = lax.broadcasted_iota(jnp.int32, (count, 1), 0)

    def spread(value, column):
        return jnp.broadcast_to(value[:, column : column + 1], value.shape)

    for p in range(0, count, 2):
        c = first + p
        row0, row1 = panel[p : p + 1, :], panel[p + 1 : p + 2, :]
        a, b = spread(row0, c), spread(row0, c + 1)
        e, d = spread(row1, c), spread(row1, c + 1)
        over = 1.0 / (a * d - b * e)
        clear0 = jnp.where(lane == c, 1.0, jnp.where(lane == c + 1, 0.0, row0))
        clear1 = jnp.where(lane == c, 0.0, jnp.where(lane == c + 1, 1.0, row1))
        new0 = (d * clear0 - b * clear1) * over
        new1 = (a * clear1 - e * clear0) * over
        factor0, factor1 = spread(panel, c), spread(panel, c + 1)
        rest = jnp.where((lane == c) | (lane == c + 1), 0.0, panel)
        rest = rest - factor0 * new0 - factor1 * new1
        panel = jnp.where(line == p, new0, jnp.where(line == p + 1, new1, rest))
    return panel


def basis_of(places):
    times = (places.astype(f32) + 0.5) / MEMPOS
    centres = (lax.broadcasted_iota(jnp.int32, (NBASIS, 1), 0).astype(f32) + 0.5) / NBASIS
    breadth = 1.0 / NBASIS
    offset = times - centres
    return jnp.exp(-offset * offset / (2.0 * breadth * breadth))


def gram_of(basis):
    line = lax.broadcasted_iota(jnp.int32, (NBASIS, NBASIS), 0)
    lane = lax.broadcasted_iota(jnp.int32, (NBASIS, NBASIS), 1)
    gram = lax.dot_general(basis, basis, NT, precision=highest, preferred_element_type=f32)
    return gram + jnp.where(line == lane, ridge_weight, 0.0)


def inverse_kernel(places_ref, inverse_ref):
    lane = lax.broadcasted_iota(jnp.int32, (NBASIS, NBASIS), 1)
    inverse_ref[...] = gram_of(basis_of(places_ref[...]))
    step = 32
    for first in range(0, NBASIS, step):
        panel = gauss_jordan(inverse_ref[first : first + step, :], first)
        columns = inverse_ref[...][:, first : first + step]
        inside = (lane >= first) & (lane < first + step)
        product = jnp.dot(columns, panel, precision=highest, preferred_element_type=f32)
        inverse_ref[...] = jnp.where(inside, 0.0, inverse_ref[...]) - product
        inverse_ref[first : first + step, :] = panel


def coeff_kernel(places_ref, samples_ref, inverse_ref, coeff_ref):
    def product(a, b):
        return jnp.dot(a, b, precision=highest, preferred_element_type=f32)

    basis = basis_of(places_ref[...])
    right = product(basis, samples_ref[...].astype(f32))
    coeffs = product(inverse_ref[...], right)
    coeffs += product(inverse_ref[...], right - product(gram_of(basis), coeffs))
    coeff_ref[...] = coeffs.astype(bf16)


def ridge_inverse(places):
    return pl.pallas_call(
        inverse_kernel,
        out_shape=jax.ShapeDtypeStruct((NBASIS, NBASIS), f32),
        in_specs=[VMEM],
        out_specs=VMEM,
        compiler_params=pltpu.CompilerParams(vmem_limit_bytes=40 * 1024 * 1024),
        cost_estimate=cost(16.6),
        name="ridge_inverse",
    )(places)


def ridge_coeffs(places, samples, inverse):
    return pl.pallas_call(
        coeff_kernel,
        out_shape=jax.ShapeDtypeStruct((NBASIS, D), bf16),
        in_specs=[VMEM] * 3,
        out_specs=VMEM,
        compiler_params=pltpu.CompilerParams(vmem_limit_bytes=40 * 1024 * 1024),
        cost_estimate=cost(4.4),
        name="ridge_coeffs",
    )(places, samples, inverse)


def expand_maps(maps, mem_keys):
    vectors = jnp.dot(maps, mem_keys.astype(f32), precision=highest, preferred_element_type=f32)
    row = lax.broadcasted_iota(jnp.int32, (8 * PAIRS, D), 0)
    which = row % 8
    lane_head = lax.broadcasted_iota(jnp.int32, (8 * PAIRS, D), 1) // HEAD
    owned = (which < 4) & (lane_head == 2 * (row // 8) + which // 2)
    both = jnp.where(which % 2 == 0, vectors[0:1, :], vectors[1:2, :])
    return jnp.where(owned, both, 0.0)


def memory_weights(logits):
    breadth = 1.0 / NBASIS
    place = 1.0 / (1.0 + jnp.exp(-logits[0:1, :]))
    sigma = logits[1:2, :]
    soft = jnp.maximum(sigma, 0.0) + jnp.log(1.0 + jnp.exp(-jnp.abs(sigma)))
    variance = (0.5 + soft) / 64.0
    centres = (lax.broadcasted_iota(jnp.int32, (NBASIS, 1), 0).astype(f32) + 0.5) / NBASIS
    offset = place - centres
    weights = (breadth * lax.rsqrt(variance)) * jnp.exp(offset * offset * (-0.5 / variance))
    return weights, place, variance, offset


def head_lanes(value, which):
    lane = lax.broadcasted_iota(jnp.int32, value.shape, 1)
    return jnp.where((lane < HEAD) == (which == 0), value, jnp.zeros_like(value))


def pair_block(rows, shift=0):
    return pl.BlockSpec((rows, PAIR), lambda p: (0, p + shift))


def whole_block(shape):
    return pl.BlockSpec(shape, lambda p: (0,) * len(shape))


def attend_back_kernel(
    bias, query_all, mem_keys_all, maps, lse, q, k, v, mv, da,
    dq, dk, dv, dmk, dmv, dmaps, logits, lines, dq_t,
):
    pair = pl.program_id(0)
    scale = HEAD**-0.5

    @pl.when(pair == 0)
    def _():
        table = expand_maps(maps[...], mem_keys_all[...])
        wide = query_all[...].astype(f32) * scale
        logits[...] = lax.dot_general(
            table, wide, NT, precision=highest, preferred_element_type=f32
        )

    rows8 = logits[pl.ds(pl.multiple_of(pair * 8, 8), 8), :]
    k_t = k[...].T
    halves = []
    derived = []
    d_keys = d_values = d_mem_values = None
    for s in range(2):
        qh = head_lanes(q[...], s) * jnp.asarray(scale, bf16)
        dh = head_lanes(da[...], s)
        scores = lax.dot_general(k[...], qh, NT, preferred_element_type=f32) + bias[...]
        probs = jnp.exp(scores - lse[0, s : s + 1, :])
        d_probs = lax.dot_general(v[...], dh, NT, preferred_element_type=f32)
        correction = jnp.sum(probs * d_probs, axis=0, keepdims=True)
        d_scores = (probs * (d_probs - correction)).astype(bf16)
        key_term = jnp.dot(d_scores, qh, preferred_element_type=f32)
        value_term = jnp.dot(probs.astype(bf16), dh, preferred_element_type=f32)
        query_term = jnp.dot(k_t, d_scores, preferred_element_type=f32) * scale
        weights, place, variance, offset = memory_weights(rows8[2 * s : 2 * s + 2, :])
        d_weights = lax.dot_general(mv[...], dh, NT, preferred_element_type=f32)
        mem_term = jnp.dot(weights.astype(bf16), dh, preferred_element_type=f32)
        moved = d_weights * weights
        sum0 = jnp.sum(moved, axis=0, keepdims=True)
        moved = moved * offset
        sum1 = jnp.sum(moved, axis=0, keepdims=True)
        sum2 = jnp.sum(moved * offset, axis=0, keepdims=True)
        d_place = -sum1 / variance
        d_variance = (sum2 / variance - sum0) * (0.5 / variance)
        derived.append(d_place * place * (1.0 - place))
        sigma = rows8[2 * s + 1 : 2 * s + 2, :]
        derived.append(d_variance * (1.0 / 64.0) / (1.0 + jnp.exp(-sigma)))
        halves.append(query_term[s * HEAD : (s + 1) * HEAD, :])
        d_keys = key_term if s == 0 else d_keys + key_term
        d_values = value_term if s == 0 else d_values + value_term
        d_mem_values = mem_term if s == 0 else d_mem_values + mem_term
    dk[...] = d_keys.astype(bf16)
    dv[...] = d_values.astype(bf16)
    dmv[...] = d_mem_values.astype(bf16)
    dq_t[pair] = jnp.concatenate(halves, 0).T
    lines[pl.ds(pl.multiple_of(pair * 8, 8), 8), :] = jnp.concatenate(
        derived + [jnp.zeros((4, derived[0].shape[1]), f32)], 0
    )

    @pl.when(pair == PAIRS - 1)
    def _():
        table = expand_maps(maps[...], mem_keys_all[...])
        low = lines[...].astype(bf16)
        back = lax.dot_general(low, table.astype(bf16), TN, preferred_element_type=f32) * scale
        for p in range(PAIRS):
            at = slice(p * PAIR, (p + 1) * PAIR)
            dq[:, at] = (dq_t[p] + back[:, at]).astype(bf16)
        sums = jnp.dot(low, query_all[...], preferred_element_type=f32) * scale
        row = lax.broadcasted_iota(jnp.int32, sums.shape, 0)
        which = row % 8
        lane_head = lax.broadcasted_iota(jnp.int32, sums.shape, 1) // HEAD
        owned = (which < 4) & (lane_head == 2 * (row // 8) + which // 2)
        sums = jnp.where(owned, sums, 0.0)
        even = jnp.sum(jnp.where(which % 2 == 0, sums, 0.0), axis=0, keepdims=True)
        odd = jnp.sum(jnp.where(which % 2 == 1, sums, 0.0), axis=0, keepdims=True)
        both = jnp.concatenate([even, odd, jnp.zeros((6, D), f32)], 0).astype(bf16)
        dmk[...] = lax.dot_general(
            maps[...].astype(bf16), both, TN, preferred_element_type=f32
        ).astype(bf16)
        dmaps[...] = lax.dot_general(both, mem_keys_all[...], NT, preferred_element_type=f32)


def attend_back(bias, query, kv, memory_kv, maps, lse, d_attended, extra=()):
    rows = query.shape[0]
    seq = kv.shape[0]
    return pl.pallas_call(
        after(attend_back_kernel, 10, extra),
        grid=(PAIRS,),
        in_specs=[
            whole_block((seq, rows)),
            whole_block((rows, D)),
            whole_block((NBASIS, D)),
            whole_block((8, NBASIS)),
            pl.BlockSpec((1, 8, rows), lambda p: (p, 0, 0)),
            pair_block(rows),
            pair_block(seq),
            pair_block(seq, PAIRS),
            pair_block(NBASIS, PAIRS),
            pair_block(rows),
        ]
        + [ANY] * len(extra),
        out_specs=[
            whole_block((rows, D)),
            pair_block(seq),
            pair_block(seq),
            whole_block((NBASIS, D)),
            pair_block(NBASIS),
            whole_block((8, NBASIS)),
        ],
        out_shape=[
            jax.ShapeDtypeStruct((rows, D), bf16),
            jax.ShapeDtypeStruct((seq, D), bf16),
            jax.ShapeDtypeStruct((seq, D), bf16),
            jax.ShapeDtypeStruct((NBASIS, D), bf16),
            jax.ShapeDtypeStruct((NBASIS, D), bf16),
            jax.ShapeDtypeStruct((8, NBASIS), f32),
        ],
        scratch_shapes=[
            pltpu.VMEM((8 * PAIRS, rows), f32),
            pltpu.VMEM((8 * PAIRS, rows), f32),
            pltpu.VMEM((PAIRS, rows, PAIR), f32),
        ],
        compiler_params=pltpu.CompilerParams(vmem_limit_bytes=56 * 1024 * 1024),
        cost_estimate=cost(18.3),
        name="attend_back",
    )(bias, query, memory_kv, maps, lse, query, kv, kv, memory_kv, d_attended, *extra)


def call_options(name, microseconds):
    return dict(
        compiler_params=pltpu.CompilerParams(vmem_limit_bytes=LIMIT),
        cost_estimate=cost(microseconds),
        name=name,
    )


def after(kernel, inputs, extra):
    def body(*refs):
        kernel(*refs[:inputs], *refs[inputs + len(extra) :])

    return body


def gate(values, extra):
    def kernel(*refs):
        del refs

    count = len(values)
    return pl.pallas_call(
        kernel,
        in_specs=[ANY] * (count + len(extra)),
        out_specs=[ANY] * count,
        out_shape=[jax.ShapeDtypeStruct(value.shape, value.dtype) for value in values],
        input_output_aliases={i: i for i in range(count)},
        **call_options("gate", 1.0),
    )(*values, *extra)


def dot_nt(a, b):
    return lax.dot_general(a, b, NT, preferred_element_type=f32)


def dot_tn(a, b):
    return lax.dot_general(a, b, TN, preferred_element_type=f32)


def normalise(value):
    centred = value - jnp.mean(value, axis=1, keepdims=True)
    spread = jnp.mean(centred * centred, axis=1, keepdims=True)
    factor = lax.rsqrt(spread + 1e-05)
    return centred * factor, factor


def norm_backward(value, gain, d_out):
    unit, factor = normalise(value)
    d_unit = d_out * gain
    mean0 = jnp.mean(d_unit, axis=1, keepdims=True)
    mean1 = jnp.mean(d_unit * unit, axis=1, keepdims=True)
    return factor * (d_unit - mean0 - unit * mean1), jnp.sum(d_out * unit, axis=0, keepdims=True)


def gelu_parts(upward):
    outer = 0.7978845608028654
    square = upward * upward
    inner = jnp.tanh(upward * (outer + outer * 0.044715 * square))
    half = 0.5 * (1.0 + inner)
    slope = half + 0.5 * upward * (1.0 - inner * inner) * (outer + 3.0 * outer * 0.044715 * square)
    return upward * half, slope


def store_shard(count, own, shard, rows, send, keep):
    size = rows.shape[0]
    width = count.bit_length() - 1
    relative = jnp.bitwise_xor(own, shard)
    place = 0
    for bit in range(width):
        place += jnp.bitwise_and(lax.shift_right_logical(relative, bit), 1) << (width - 1 - bit)

    @pl.when(place >= count // 2)
    def _():
        send[pl.ds(pl.multiple_of((place - count // 2) * size, 16), size), :] = rows

    @pl.when(place < count // 2)
    def _():
        keep[pl.ds(pl.multiple_of(place * size, 16), size), :] = rows


def store_shards(count, own, value, send, keep):
    size = value.shape[0] // count
    for shard in range(count):
        rows = value[shard * size : (shard + 1) * size, :].astype(bf16)
        store_shard(count, own, shard, rows, send, keep)


def attend_kernel(layer, count, *refs):
    parts = refs[:count]
    bias, coeff, maps, w_hbm = refs[count : count + 4]
    out, lse, query, kv, memory_kv = refs[count + 4 : count + 9]
    w, logits, sem = refs[count + 9 :]
    copy = pltpu.make_async_copy(w_hbm.at[layer], w, sem)
    copy.start()
    copy.wait()
    rows = query.shape[0]
    query[...] = jnp.dot(parts[0][...], w[:, :D], preferred_element_type=f32).astype(bf16)
    memory_kv[...] = jnp.dot(coeff[...], w[:, D:], preferred_element_type=f32).astype(bf16)
    for k in range(count):
        kv[k * rows : (k + 1) * rows, :] = jnp.dot(
            parts[k][...], w[:, D:], preferred_element_type=f32
        ).astype(bf16)
    table = expand_maps(maps[...], memory_kv[:, :D])
    wide = query[...].astype(f32) * HEAD**-0.5
    logits[...] = lax.dot_general(table, wide, NT, precision=highest, preferred_element_type=f32)

    def body(pair, carry):
        at = pl.ds(pl.multiple_of(pair * PAIR, PAIR), PAIR)
        value_at = pl.ds(pl.multiple_of(D + pair * PAIR, PAIR), PAIR)
        lines = logits[pl.ds(pl.multiple_of(pair * 8, 8), 8), :]
        q, k = query[:, at], kv[:, at]
        v_t = kv[:, value_at].T
        mv_t = memory_kv[:, value_at].T
        halves = []
        totals = []
        for s in range(2):
            qh = head_lanes(q, s) * jnp.asarray(HEAD**-0.5, bf16)
            blocks = [slice(i * rows, (i + 1) * rows) for i in range(count)]
            scores = [dot_nt(k[blocks[0]], qh) + bias[blocks[0], :]]
            for block in blocks[1:]:
                scores.append(dot_nt(k[block], qh) + bias[block.start : block.start + 1, :])
            peak = functools.reduce(
                jnp.maximum, [jnp.max(item, axis=0, keepdims=True) for item in scores]
            )
            expo = [jnp.exp(item - peak) for item in scores]
            total = sum(jnp.sum(item, axis=0, keepdims=True) for item in expo)
            local = sum(
                jnp.dot(v_t[:, block], item.astype(bf16), preferred_element_type=f32)
                for block, item in zip(blocks, expo)
            ) * (1.0 / total)
            weights = memory_weights(lines[2 * s : 2 * s + 2, :])[0]
            recalled = jnp.dot(mv_t, weights.astype(bf16), preferred_element_type=f32)
            halves.append((local + recalled)[s * HEAD : (s + 1) * HEAD, :])
            totals.append(peak + jnp.log(total))
        out[:, at] = jnp.concatenate(halves, 0).T.astype(bf16)
        lse[pair, 0:1, :] = totals[0]
        lse[pair, 1:2, :] = totals[1]
        return carry

    lax.fori_loop(0, PAIRS, body, 0, unroll=2)


def attend(layer, parts, bias, coeff, maps, w_qkv):
    rows = parts[0].shape[0]
    seq = rows * len(parts)
    return pl.pallas_call(
        functools.partial(attend_kernel, layer, len(parts)),
        in_specs=[VMEM] * (len(parts) + 3) + [ANY],
        out_specs=[VMEM] * 5,
        out_shape=[
            jax.ShapeDtypeStruct((rows, D), bf16),
            jax.ShapeDtypeStruct((PAIRS, 8, rows), f32),
            jax.ShapeDtypeStruct((rows, D), bf16),
            jax.ShapeDtypeStruct((seq, 2 * D), bf16),
            jax.ShapeDtypeStruct((NBASIS, 2 * D), bf16),
        ],
        scratch_shapes=[
            pltpu.VMEM((D, 3 * D), bf16),
            pltpu.VMEM((8 * PAIRS, rows), f32),
            pltpu.SemaphoreType.DMA,
        ],
        **call_options("attend", 20.8),
    )(*parts, bias, coeff, maps, w_qkv)


def mlp_kernel(last, count, own, *refs):
    attended, hidden, gain, next_gain, w_out, w_up, w_down = refs[:7]
    middle, normed2, upward, hidden_out, low_out = refs[7:12]
    shards = refs[12:]
    step = pl.program_id(0)

    @pl.when(step == 0)
    def _():
        middle[...] = hidden[...] + jnp.dot(
            attended[...], w_out[0], preferred_element_type=f32
        )
        normed2[...] = (normalise(middle[...])[0] * gain[...]).astype(bf16)
        hidden_out[...] = middle[...]

    up = jnp.dot(normed2[...], w_up[0], preferred_element_type=f32)
    upward[...] = up
    active = gelu_parts(up)[0].astype(bf16)
    hidden_out[...] += jnp.dot(active, w_down[0], preferred_element_type=f32)
    pieces = max(1, count // CHUNKS)
    share = active.shape[1] // pieces
    for i in range(pieces):
        relative = jnp.bitwise_xor(own[0], step * pieces + i)
        for k in range(count):

            @pl.when(relative == k)
            def _(i=i, k=k):
                shards[k][...] = active[:, i * share : (i + 1) * share]

    @pl.when(step == CHUNKS - 1)
    def _():
        value = hidden_out[...]
        low_out[...] = (value if last else normalise(value)[0] * next_gain[...]).astype(bf16)


def mlp(layer, last, count, own, attended, hidden, gain, next_gain, w_out, w_up, w_down):
    rows = hidden.shape[0]
    hidden_units = w_up.shape[2]
    chunk = hidden_units // CHUNKS
    share = hidden_units // count
    assert count >= CHUNKS
    whole = pl.BlockSpec((rows, D), lambda j, own: (0, 0))
    line = pl.BlockSpec((1, D), lambda j, own: (0, 0))
    shard = pl.BlockSpec((rows, share), lambda j, own: (0, 0))
    return pl.pallas_call(
        functools.partial(mlp_kernel, last, count),
        grid_spec=pltpu.PrefetchScalarGridSpec(
            num_scalar_prefetch=1,
            grid=(CHUNKS,),
            in_specs=[
                whole,
                whole,
                line,
                line,
                pl.BlockSpec((1, D, D), lambda j, own: (layer, 0, 0)),
                pl.BlockSpec((1, D, chunk), lambda j, own: (layer, 0, j)),
                pl.BlockSpec((1, chunk, D), lambda j, own: (layer, j, 0)),
            ],
            out_specs=[
                whole,
                whole,
                pl.BlockSpec((rows, chunk), lambda j, own: (0, j)),
                whole,
                whole,
            ]
            + [shard] * count,
        ),
        out_shape=[
            jax.ShapeDtypeStruct((rows, D), f32),
            jax.ShapeDtypeStruct((rows, D), bf16),
            jax.ShapeDtypeStruct((rows, hidden_units), f32),
            jax.ShapeDtypeStruct((rows, D), f32),
            jax.ShapeDtypeStruct((rows, D), bf16),
        ]
        + [jax.ShapeDtypeStruct((rows, share), bf16)] * count,
        **call_options("mlp", 10.4),
    )(own, attended, hidden, gain, next_gain, w_out, w_up, w_down)


def mlp_back_kernel(
    shards, own, grad, grad_low, upward, normed2, middle, gain, attended, w_out, w_up, w_down,
    send, keep, grad_out, low_out, d_attended, d_gain, left, d_normed,
):
    step = pl.program_id(0)

    @pl.when(step == 0)
    def _():
        left[...] = normed2[...].T

    @pl.when(step < CHUNKS)
    def _():
        d_active = dot_nt(grad_low[...], w_down[0])
        d_up = (d_active * gelu_parts(upward[...])[1]).astype(bf16)
        term = dot_nt(d_up, w_up[0])

        @pl.when(step == 0)
        def _():
            d_normed[...] = term

        @pl.when(step > 0)
        def _():
            d_normed[...] += term

        value = jnp.dot(left[...], d_up, preferred_element_type=f32)
        store_shards(shards, own[0], value, send.at[0], keep.at[0])

    @pl.when(step == CHUNKS)
    def _():
        d_middle, d_line = norm_backward(middle[...], gain[...], d_normed[...])
        total = grad[...] + d_middle
        grad_out[...] = total
        low = total.astype(bf16)
        low_out[...] = low
        d_attended[...] = dot_nt(low, w_out[0]).astype(bf16)
        d_gain[...] = d_line
        store_shards(shards, own[0], dot_tn(attended[...], low), send.at[0], keep.at[0])


def mlp_back(
    layer,
    shards,
    own,
    grad,
    grad_low,
    upward,
    normed2,
    middle,
    gain,
    attended,
    w_out,
    w_up,
    w_down,
    extra=(),
):
    rows = grad.shape[0]
    chunk = w_up.shape[2] // CHUNKS
    last = CHUNKS - 1
    whole = pl.BlockSpec((rows, D), lambda j, own: (0, 0))
    line = pl.BlockSpec((1, D), lambda j, own: (0, 0))
    half = pl.BlockSpec((1, D // 2, chunk), lambda j, own: (j, 0, 0))
    shape = jax.ShapeDtypeStruct((CHUNKS + 1, D // 2, chunk), bf16)
    return pl.pallas_call(
        after(functools.partial(mlp_back_kernel, shards), 11, extra),
        grid_spec=pltpu.PrefetchScalarGridSpec(
            num_scalar_prefetch=1,
            grid=(CHUNKS + 1,),
            in_specs=[
                whole,
                whole,
                pl.BlockSpec((rows, chunk), lambda j, own: (0, jnp.minimum(j, last))),
                whole,
                whole,
                line,
                whole,
                pl.BlockSpec((1, D, D), lambda j, own: (layer, 0, 0)),
                pl.BlockSpec((1, D, chunk), lambda j, own: (layer, 0, jnp.minimum(j, last))),
                pl.BlockSpec((1, chunk, D), lambda j, own: (layer, jnp.minimum(j, last), 0)),
            ]
            + [ANY] * len(extra),
            out_specs=[half, half, whole, whole, whole, line],
            scratch_shapes=[pltpu.VMEM((D, rows), bf16), pltpu.VMEM((rows, D), f32)],
        ),
        out_shape=[
            shape,
            shape,
            jax.ShapeDtypeStruct((rows, D), f32),
            jax.ShapeDtypeStruct((rows, D), bf16),
            jax.ShapeDtypeStruct((rows, D), bf16),
            jax.ShapeDtypeStruct((1, D), f32),
        ],
        **call_options("mlp_back", 14.6),
    )(own, grad, grad_low, upward, normed2, middle, gain, attended, w_out, w_up, w_down, *extra)


def down_kernel(count, *refs):
    out = refs[-1]
    total = dot_tn(refs[0][...], refs[count][...])
    for k in range(1, count):
        total += dot_tn(refs[k][...], refs[count + k][...])
    out[...] = total.astype(bf16)


def down_grad(actives, grads, extra=()):
    count = len(actives)
    return pl.pallas_call(
        after(functools.partial(down_kernel, count), 2 * count, extra),
        in_specs=[VMEM] * (2 * count) + [ANY] * len(extra),
        out_specs=VMEM,
        out_shape=jax.ShapeDtypeStruct((actives[0].shape[1], D), bf16),
        **call_options("down_grad", 4.3),
    )(*actives, *grads, *extra)


def input_kernel(layer, d_query, d_keys, d_values, w_hbm, *refs):
    outs, (w, sem) = refs[:-2], refs[-2:]
    copy = pltpu.make_async_copy(w_hbm.at[layer], w, sem)
    copy.start()
    copy.wait()
    rows = d_query.shape[0]
    total = dot_nt(d_keys[...], w[:, D : 2 * D]) + dot_nt(d_values[...], w[:, 2 * D :])
    outs[0][...] = (total[:rows, :] + dot_nt(d_query[...], w[:, :D])).astype(bf16)
    for k in range(1, len(outs)):
        outs[k][...] = total[k * rows : (k + 1) * rows, :].astype(bf16)


def input_terms(layer, count, d_query, d_keys, d_values, w_qkv, extra=()):
    return pl.pallas_call(
        after(functools.partial(input_kernel, layer), 4, extra),
        in_specs=[VMEM] * 3 + [ANY] + [ANY] * len(extra),
        out_specs=[VMEM] * count,
        out_shape=[jax.ShapeDtypeStruct(d_query.shape, bf16)] * count,
        scratch_shapes=[pltpu.VMEM((D, 3 * D), bf16), pltpu.SemaphoreType.DMA],
        **call_options("input_terms", 7.6),
    )(d_query, d_keys, d_values, w_qkv, *extra)


def attention_grad_kernel(count, own, *refs):
    parts = refs[:count]
    coeff, d_query, d_keys, d_values, d_mem_keys, d_mem_values, send, keep, left = refs[count:]
    rows = d_query.shape[0]
    seq = rows * count
    size = D // count
    for k in range(count):
        left[:, k * rows : (k + 1) * rows] = parts[k][...].T
    left[:, seq:] = coeff[...].T

    def product(a, b):
        return jnp.dot(a, b[...], preferred_element_type=f32)

    for shard in range(count):
        line = left[shard * size : (shard + 1) * size, :]
        own_line, all_line, mem_line = line[:, :rows], line[:, :seq], line[:, seq:]
        values = (
            product(own_line, d_query),
            product(all_line, d_keys) + product(mem_line, d_mem_keys),
            product(all_line, d_values) + product(mem_line, d_mem_values),
        )
        for i, value in enumerate(values):
            store_shard(count, own[0], shard, value.astype(bf16), send.at[i], keep.at[i])


def attention_grads(own, parts, coeff, derivatives, extra=()):
    smem = pl.BlockSpec(memory_space=pltpu.SMEM)
    shape = jax.ShapeDtypeStruct((3, D // 2, D), bf16)
    inputs = (*parts, coeff, *derivatives)
    return pl.pallas_call(
        after(functools.partial(attention_grad_kernel, len(parts)), 1 + len(inputs), extra),
        in_specs=[smem] + [VMEM] * len(inputs) + [ANY] * len(extra),
        out_specs=[VMEM, VMEM],
        out_shape=[shape, shape],
        scratch_shapes=[pltpu.VMEM((D, parts[0].shape[0] * len(parts) + NBASIS), bf16)],
        **call_options("attention_grads", 9.6),
    )(own, *inputs, *extra)


def norm_back_kernel(value, gain, d_out, grad, grad_out, low_out, d_gain):
    d_value, d_line = norm_backward(value[...], gain[...], d_out[...].astype(f32))
    total = grad[...] + d_value
    grad_out[...] = total
    low_out[...] = total.astype(bf16)
    d_gain[...] = d_line


def norm_back(value, gain, d_out, grad, extra=()):
    return pl.pallas_call(
        after(norm_back_kernel, 4, extra),
        in_specs=[VMEM] * 4 + [ANY] * len(extra),
        out_specs=[VMEM] * 3,
        out_shape=[
            jax.ShapeDtypeStruct(grad.shape, f32),
            jax.ShapeDtypeStruct(grad.shape, bf16),
            jax.ShapeDtypeStruct((1, D), f32),
        ],
        **call_options("norm_back", 3.1),
    )(value, gain, d_out, grad, *extra)


def start_kernel(live, tokens, gain, cotangent, hidden, normed, grad, grad_low):
    wide = tokens[...].astype(f32)
    hidden[...] = wide
    normed[...] = (normalise(wide)[0] * gain[...]).astype(bf16)
    masked = cotangent[...].astype(f32) * live[0].astype(f32)
    grad[...] = masked
    grad_low[...] = masked.astype(bf16)


def start(live, tokens, gain, cotangent):
    return pl.pallas_call(
        start_kernel,
        in_specs=[pl.BlockSpec(memory_space=pltpu.SMEM)] + [VMEM] * 3,
        out_specs=[VMEM] * 4,
        out_shape=[jax.ShapeDtypeStruct(tokens.shape, kind) for kind in (f32, bf16, f32, bf16)],
        **call_options("start", 2.5),
    )(live, tokens, gain, cotangent)


def swap(value, axis, bit):
    count = lax.axis_size(axis)
    return lax.ppermute(value, axis, [(i, i ^ bit) for i in range(count)])


def bits_of(axis):
    return [1 << i for i in range(lax.axis_size(axis).bit_length() - 1)]


def gather_steps(held, axis, bits):
    held = dict(held)
    for bit in reversed(bits):
        held.update({k | bit: swap(v, axis, bit) for k, v in list(held.items())})
    return held


def relative_gather(value, axis):
    held = gather_steps({0: value}, axis, bits_of(axis))
    return [held[k] for k in range(lax.axis_size(axis))]


def scatter_step(held, axis, bit):
    sent = {k: swap(v, axis, bit) for k, v in held.items() if k & bit}
    return {
        k: (v.astype(f32) + sent[k | bit].astype(f32)).astype(bf16)
        for k, v in held.items()
        if not k & bit
    }


class Sum:
    def __init__(self, *terms):
        self.terms = [(term, 0) for term in terms]
        self.rows = terms[0].shape[1]

    def added(self, terms):
        parts = [
            value
            if value.shape[1] == self.rows
            else lax.dynamic_slice_in_dim(value, at, self.rows, 1)
            for value, at in terms
        ]
        if len(parts) == 1:
            return parts[0]
        return sum(part.astype(f32) for part in parts).astype(bf16)

    def whole(self):
        return self.added(self.terms)

    def blocks(self):
        return self.terms[0][0].shape[0]

    def newest(self):
        return [self.terms[-1][0]]

    def split(self, side):
        self.rows = self.rows // 2
        sent = [(value, at + (1 - side) * self.rows) for value, at in self.terms]
        sent = self.added(sent)
        self.terms = [(value, at + side * self.rows) for value, at in self.terms]
        return sent

    def take(self, got):
        self.terms.append((got, 0))

    def over_blk(self, bit):
        return self.split(0), "blk", bit

    def over_batch(self, bit):
        side = jnp.where(jnp.bitwise_and(lax.axis_index("batch"), bit) > 0, 1, 0)
        return self.split(side), "batch", bit


def side_by_side(items):
    items = [item.whole() for item in items]
    return Sum(jnp.concatenate(items, 0))


def doubled(total, got, bit):
    upper = jnp.bitwise_and(lax.axis_index("batch"), bit) > 0
    return jnp.concatenate([jnp.where(upper, got, total), jnp.where(upper, total, got)], 1)


def gathered(total):
    blocks, rows, columns = total.shape
    whole = lax.all_gather(total.reshape(blocks * rows, columns), "batch", axis=0)
    return whole.reshape(-1, blocks, rows, columns)


def in_place(whole):
    count, blocks, rows, columns = whole.shape
    width = count.bit_length() - 1
    whole = whole.reshape((2,) * width + (blocks, rows, columns))
    order = (width,) + tuple(reversed(range(width))) + (width + 1, width + 2)
    return whole.transpose(order).reshape(blocks, -1, columns)


def on_device(
    tokens,
    memory,
    mem_pos,
    seg_count,
    w_qkv,
    w_out,
    w_up,
    w_down,
    gain_attn,
    gain_mlp,
    w_mu,
    w_sig,
    cotangent,
):
    rows = tokens.shape[0]
    hidden_units = w_up.shape[2]
    count = lax.axis_size("blk")
    length = seg_count[0] * rows
    own = lax.axis_index("blk")
    own_list = own.astype(jnp.int32).reshape(1)
    own_places = own * rows + jnp.arange(rows, dtype=jnp.int32)
    all_places = jnp.concatenate(
        [jnp.bitwise_xor(own, k) * rows + jnp.arange(rows, dtype=jnp.int32) for k in range(count)]
    )
    allowed = (all_places[:, None] <= own_places[None, :]) & (all_places[:, None] < length)
    bias = jnp.where(allowed, 0.0, -1e30).astype(f32)
    lives = (own < seg_count[0]).astype(jnp.int32).reshape(1)
    hidden, normed, grad, grad_low = start(lives, tokens, gain_attn[0:1], cotangent)
    places = jnp.concatenate(relative_gather(mem_pos, "blk"), 1)
    places, sample, normed = lax.optimization_barrier((places, memory[0], normed))
    bits = bits_of("blk")
    far = [gather_steps({0: value}, "blk", bits[1:]) for value in (sample, normed)]
    inverse = ridge_inverse(places)
    inverse, far, grad_low, bias = lax.optimization_barrier((inverse, far, grad_low, bias))
    samples, parts = [gather_steps(held, "blk", bits[:1]) for held in far]
    samples = jnp.concatenate([samples[k] for k in range(count)], 0)
    parts = [parts[k] for k in range(count)]
    coeff_low = ridge_coeffs(places, samples, inverse)
    coeff_low, grad_low = lax.optimization_barrier((coeff_low, grad_low))
    grad_parts = [grad_low] + [swap(grad_low, "blk", k) for k in range(1, count)]
    saved = []
    for layer in range(LAYERS):
        final = layer == LAYERS - 1
        maps = jnp.concatenate(
            [w_mu[layer][None], w_sig[layer][None], jnp.zeros((6, NBASIS), f32)], 0
        )
        attended, lse, query, kv, memory_kv = attend(layer, parts, bias, coeff_low, maps, w_qkv)
        if layer == 0:
            grad_parts, attended = lax.optimization_barrier((grad_parts, attended))
        else:
            before, attended = lax.optimization_barrier((saved[layer - 1][-1], attended))
            saved[layer - 1] = saved[layer - 1][:-1] + (before,)
        after = min(layer + 1, LAYERS - 1)
        middle, normed2, upward, after_block, low, *shards = mlp(
            layer,
            final,
            count,
            own_list,
            attended,
            hidden,
            gain_mlp[layer : layer + 1],
            gain_attn[after : after + 1],
            w_out,
            w_up,
            w_down,
        )
        saved.append((hidden, parts, query, kv, memory_kv, maps, lse))
        saved[layer] += (attended, middle, normed2, upward)
        hidden = after_block
        if not final:
            parts = relative_gather(low, "blk")
            parts, shards = lax.optimization_barrier((parts, shards))
        shards = [shards[0]] + [swap(shards[k], "blk", k) for k in range(1, count)]
        saved[layer] += (shards,)
    mixed = low
    small = [None] * LAYERS
    near, far = bits[0], bits[1:]
    first, *others = bits_of("batch")

    def chain(item, moves):
        for axis, bit in moves:
            move = item.over_blk(bit) if axis == "blk" else item.over_batch(bit)
            item.take(swap(*move))

    def back(layer, grad, grad_low, extra=()):
        layer_input, parts, query, kv, memory_kv, maps, lse = saved[layer][:7]
        attended, middle, normed2, upward, shards = saved[layer][7:]
        inputs = (layer, count, own_list, grad, grad_low, upward, normed2, middle)
        inputs += (gain_mlp[layer : layer + 1], attended, w_out, w_up, w_down)
        return mlp_back(*inputs, extra)

    def attention(layer, d_attended, extra):
        layer_input, parts, query, kv, memory_kv, maps, lse = saved[layer][:7]
        outs = attend_back(bias, query, kv, memory_kv, maps, lse, d_attended, extra)
        return outs[:5], outs[5]

    layer = LAYERS - 1
    parts, shards = saved[layer][1], saved[layer][-1]
    sent, kept, grad, grad_low, d_attended, d_gain_mlp = back(layer, grad, grad_low)
    up1 = Sum(kept)
    (sent,) = gate([sent], shards[1:])
    up1.take(swap(sent, "blk", near))
    down = down_grad(shards, grad_parts)
    down1 = Sum(down.reshape(-1, D // count, D))
    moves = [("blk", bit) for bit in far]
    operand = up1.over_blk(far[0])
    derivatives, d_maps1 = attention(layer, d_attended, [operand[0], down])
    up1.take(swap(*operand))
    chain(up1, moves[1:])
    terms = input_terms(layer, count, *derivatives[:3], w_qkv)
    terms = scatter_step(dict(enumerate(terms)), "blk", near)
    numbers = [k for k in terms if k]
    terms.update(zip(numbers, gate([terms[k] for k in numbers], up1.newest())))
    extra = [terms[k] for k in terms if k] + up1.newest()
    for bit in far:
        terms = scatter_step(terms, "blk", bit)
    mlp1 = side_by_side([up1, down1])
    operand_y1 = mlp1.over_batch(first)
    sent, kept = attention_grads(own_list, parts, coeff_low, derivatives, extra)
    (sent,) = gate([sent], [terms[0]])
    last1 = Sum(kept)
    last1.take(swap(sent, "blk", near))
    grad, grad_low, d_gain_attn = norm_back(
        saved[layer][0], gain_attn[layer : layer + 1], terms[0], grad
    )
    gains = jnp.concatenate([d_gain_attn, d_gain_mlp], 0)
    small[layer] = jnp.concatenate([gains, d_maps1[:2]], 1)

    layer = 0
    parts, shards = saved[layer][1], saved[layer][-1]
    operand = last1.over_blk(far[0])
    grad_first = grad_low
    sent, kept, grad, grad_low, d_attended, d_gain_mlp = back(
        layer, grad, grad_low, [operand[0], operand_y1[0]]
    )
    mlp1.take(swap(*operand_y1))
    last1.take(swap(*operand))
    chain(last1, moves[1:])
    grad_parts = gather_steps({0: grad_first}, "blk", far)
    (sent,) = gate(
        [sent], last1.newest() + mlp1.newest() + [grad_parts[k] for k in grad_parts if k]
    )
    up0 = Sum(kept)
    up0.take(swap(sent, "blk", near))
    operand = up0.over_blk(far[0])
    operand_y = last1.over_batch(first)
    operand_z1 = mlp1.over_batch(others[0])
    values = gate([operand_y[0], operand_z1[0]], up0.newest())
    operand_y = (values[0],) + operand_y[1:]
    operand_z1 = (values[1],) + operand_z1[1:]
    derivatives, d_maps0 = attention(
        layer, d_attended, [operand[0], operand_y[0], operand_z1[0]]
    )
    mlp1.take(swap(*operand_z1))
    up0.take(swap(*operand))
    chain(up0, moves[1:])
    last1.take(swap(*operand_y))
    grad_parts = gather_steps(grad_parts, "blk", [near])
    grad_parts = [grad_parts[k] for k in range(count)]
    operand_z1 = mlp1.over_batch(others[1])
    down = down_grad(shards, grad_parts, [operand_z1[0], d_maps0] + last1.newest())
    mlp1.take(swap(*operand_z1))
    down0 = Sum(down.reshape(-1, D // count, D))
    sent, kept = attention_grads(own_list, parts, coeff_low, derivatives, [down])
    (sent,) = gate([sent], mlp1.newest())
    last0 = Sum(kept)
    last0.take(swap(sent, "blk", near))
    mlp0 = side_by_side([up0, down0])
    chain(mlp1, [("batch", bit) for bit in others[2:]])
    early = mlp1.whole()
    *more, second, third, fourth = reversed(bits_of("batch"))
    for bit in more:
        early = doubled(early, swap(early, "batch", bit), bit)
    operand = last0.over_blk(far[0])
    operand_y = mlp0.over_batch(first)
    operand_z = last1.over_batch(others[0])
    values = gate([operand_y[0], operand_z[0], early], last0.newest())
    operand_y = (values[0],) + operand_y[1:]
    operand_z = (values[1],) + operand_z[1:]
    early = values[2]
    last1.take(swap(*operand_z))
    terms = input_terms(layer, count, *derivatives[:3], w_qkv, [operand[0], operand_y[0], early])
    last0.take(swap(*operand))
    chain(last0, moves[1:])
    mlp0.take(swap(*operand_y))
    got = swap(early, "batch", second)
    chain(last1, [("batch", bit) for bit in others[1:]])
    terms = scatter_step(dict(enumerate(terms)), "blk", near)
    numbers = [k for k in terms if k]
    terms.update(zip(numbers, gate([terms[k] for k in numbers], last0.newest() + mlp0.newest())))
    operand = last0.over_batch(first)
    early = doubled(early, got, second)
    got = swap(early, "batch", third)
    for bit in far:
        terms = scatter_step(terms, "blk", bit)
    last0.take(swap(*operand))
    operand_z = mlp0.over_batch(others[0])
    grad, grad_low, d_gain_attn = norm_back(
        saved[layer][0],
        gain_attn[layer : layer + 1],
        terms[0],
        grad,
        [operand[0], operand_z[0], got],
    )
    early = doubled(early, got, third)
    mlp0.take(swap(*operand_z))
    operand = last0.over_batch(others[0])
    last0.take(swap(*operand))
    gains = jnp.concatenate([d_gain_attn, d_gain_mlp], 0)
    small[layer] = jnp.concatenate([gains, d_maps0[:2]], 1)
    packed = jnp.concatenate(small, 0)
    for bit in bits:
        packed = packed + swap(packed, "blk", bit)
    for item in (mlp0, last0):
        chain(item, [("batch", bit) for bit in others[1:]])
    got = swap(early, "batch", fourth)
    low = mlp0.whole()
    split = CHUNKS + 1
    rest = [last1.whole(), low[:split], last0.whole()]
    rows_each = rest[0].shape[1]
    values = packed.astype(bf16).reshape(-1)
    pieces = -(-values.shape[0] // (rows_each * D))
    values = jnp.pad(values, (0, pieces * rows_each * D - values.shape[0]))
    rest.append(values.reshape(pieces, rows_each, D))
    (rest,) = gate([jnp.concatenate(rest, 0)], [got])
    mlp1 = doubled(early, got, fourth)
    down0 = low[split:]
    for bit in reversed(bits_of("batch")):
        down0 = doubled(down0, swap(down0, "batch", bit), bit)
    rest = gathered(rest)
    packed = jnp.sum(rest[:, -pieces:].astype(f32), 0).reshape(-1)[: packed.size]
    rest = in_place(rest)[:-pieces]
    last1, up0, last0 = rest[:3], rest[3:-3], rest[-3:]
    mlp0 = jnp.concatenate([up0, down0], 0)
    packed = packed.reshape(LAYERS, 2, D + NBASIS)

    def share_of(value):
        share = value.shape[1] // count
        return lax.dynamic_slice_in_dim(value, own * share, share, 1)

    shares = [share_of(packed[:, i, at]) for at in (slice(0, D), slice(D, None)) for i in (0, 1)]


    def columns(blocks):
        return jnp.concatenate([blocks[i] for i in range(blocks.shape[0])], 1)

    def both(low, high):
        return jnp.stack([low, high]).astype(f32)

    return (
        mixed,
        grad,
        both(columns(last0), columns(last1)),
        both(mlp0[CHUNKS], mlp1[CHUNKS]),
        both(columns(mlp0[:CHUNKS]), columns(mlp1[:CHUNKS])),
        both(mlp0[CHUNKS + 1 :].reshape(-1, D), mlp1[CHUNKS + 1 :].reshape(-1, D)),
        *shares,
    )


def solution(mesh):
    placed = (
        P(("batch", "blk"), None),
        P("batch", "blk", None),
        P("batch", "blk"),
        P("batch"),
        P(),
        P(),
        P(),
        P(),
        P(),
        P(),
        P(),
        P(),
        P(("batch", "blk"), None),
    )
    return jax.shard_map(
        on_device,
        mesh=mesh,
        in_specs=placed,
        out_specs=(
            P(("batch", "blk"), None),
            P(("batch", "blk"), None),
            P(None, "blk", None),
            P(None, "blk", None),
            P(None, "blk", None),
            P(None, "blk", None),
            P(None, "blk"),
            P(None, "blk"),
            P(None, "blk"),
            P(None, "blk"),
        ),
        check_vma=False,
    )
```
